128 devices in a mesh: wide: 16 (over z, y), narrow: 8 (over x, core).
Axes of the slice: x: 4, y: 4, z: 4, core: 2. Of those that a mesh axis runs over, the one named last changes fastest.
Arguments:
- tokens: bfloat16 [22528, 1024], P(('wide', 'narrow')), may hold values from -6 to 6
- layer_cotangent: bfloat16 [22528, 1024], P(('wide', 'narrow')), may hold values from -6 to 6
- attn_gain: float32 [1024], replicated, may hold values from 0.25 to 1.75
- qkv_weight: float32 [3, 1024, 1024], P(None, None, 'narrow'), may hold values from -0.1875 to 0.1875
- out_weight: float32 [1024, 1024], P('narrow'), may hold values from -2.5 to 2.5
- rel_bias: float32 [16, 32], P('narrow'), may hold values from -4 to 4
- moe_gain: float32 [1024], replicated, may hold values from 0.25 to 1.75
- router_weight: float32 [1024, 32], replicated, may hold values from -0.125 to 0.125
- expert_in: float32 [32, 2, 1024, 2816], P('wide', None, None, 'narrow'), may hold values from -0.1875 to 0.1875
- expert_out: float32 [32, 2816, 1024], P('wide', 'narrow'), may hold values from -0.15625 to 0.15625
- routes: int32 [22528, 2], P(('wide', 'narrow')), may hold values from 0 to 31, all different within a row; in each aligned block of 176 rows (0 to 175, 176 to 351, ...) at most 26 rows name the same one
- buckets: int32 [2815], replicated, may hold values from 0 to 31, as said below
Outputs:
- layer_out: bfloat16 [22528, 1024], P(('wide', 'narrow'))
- input_grad: float32 [22528, 1024], P(('wide', 'narrow'))
- attn_gain_grad: float32 [1024], replicated
- qkv_weight_grad: float32 [3, 1024, 1024], P(None, None, 'narrow')
- out_weight_grad: float32 [1024, 1024], P('narrow')
- rel_bias_grad: float32 [16, 32], P('narrow')
- moe_gain_grad: float32 [1024], replicated
- router_grad: float32 [1024, 32], replicated
- expert_in_grad: float32 [32, 2, 1024, 2816], P('wide', None, None, 'narrow')
- expert_out_grad: float32 [32, 2816, 1024], P('wide', 'narrow')
The draws below stay inside these ranges and needn't reach their ends.
Inputs may be any that keep to these rules, and one draw needn't show every extreme that they name: `routes`: each row names 2 different experts; within each aligned block of 176 rows no expert is named more than 2 * 13 times. Entry 1407 + j - i is the bucket of key position j for query position i of the same sequence; entry 1407 is 0; keys at or after the query use buckets below 16, keys before it the others.
All inputs are finite; a program needn't handle non-finite values.
Results may differ from the reference program's by a relative error of at most 0.02.
Values may be sent and summed in bfloat16 or wider, within the bound.
No kernel may reach another device: no remote copies, remote signals or barrier semaphores. Data moves between devices by JAX's collectives and lax.ppermute only.
A program may use at most 320 MiB of HBM per device.

```python
import math
import jax
import jax.numpy as jnp
import numpy as np
from jax import lax

D = 1024
HEADS = 16
HEAD_DIM = 64
FF = 2816
EXPERTS = 32
BUCKETS = 32
TOP = 2
LEN = 1408
QBLOCK = 704
TOK_DEV = 176
TOKENS = 22528
CAP = 13
N_WIDE = 16
N_NARROW = 8


def draw_buckets(key, part):
    key = jax.random.fold_in(key, 7)
    half = BUCKETS // 2
    ahead_key, behind_key = jax.random.split(key)
    distance = jnp.arange(LEN, dtype=jnp.int32)
    ahead_marks = jax.random.permutation(ahead_key, LEN - 1)[:half - 1].astype(jnp.int32) + 1
    behind_marks = jax.random.permutation(behind_key, LEN - 1)[:half - 1].astype(jnp.int32) + 1
    ahead = jnp.sum((ahead_marks[None, :] <= distance[:, None]).astype(jnp.int32), axis=1)
    behind = half + jnp.sum((behind_marks[None, :] <= distance[:, None]).astype(jnp.int32), axis=1)
    return jnp.concatenate([behind[1:][::-1], ahead]).astype(jnp.int32)


def level_of(rng, shape, cuts, smallest, largest):
    level = 1.0
    for position, parts in cuts:
        heights = jax.random.uniform(jax.random.fold_in(jax.random.fold_in(rng, 6), position), (parts,), jnp.float32, smallest / len(cuts), largest / len(cuts))
        level = level * jnp.repeat(jnp.exp(heights), shape[position] // parts).reshape((-1,) + (1,) * (len(shape) - 1 - position))
    return level


def routed_block(stream_key, own, number, rows, count, top, bound, lean):
    order = jax.random.permutation(stream_key, count)
    heavy_load, common = portions_of(count, rows * top, bound, lean, True), portions_of(count, rows * top, bound, lean, False)
    places = jnp.arange(count)

    def named(tallies, turn):
        used = int((tallies > 0).sum())
        fixed = max(1, used // 4)
        passed = fixed + (places - fixed + turn * (used - fixed)) % max(1, count - fixed)
        return jnp.zeros((count,), jnp.int32).at[order[jnp.where(places < fixed, places, passed)]].set(jnp.asarray(tallies, jnp.int32))

    tallies = jnp.where(number % 4 == 0, named(heavy_load, number // 4), named(common, number - number // 4 - 1))
    mixed = jax.random.permutation(jax.random.fold_in(own, 3), count)
    giver, receiver = mixed[0:count // 2 * 2:2], mixed[1:count // 2 * 2:2]
    room = jnp.minimum(tallies[giver] - 1, bound - tallies[receiver]) // 2
    room = jnp.where((giver == order[0]) | (receiver == order[0]) | (tallies[receiver] == 0), 0, jnp.maximum(room, 0))
    passed = jax.random.randint(jax.random.fold_in(own, 4), (count // 2,), 0, 1 << 20) % (room + 1)
    tallies = tallies.at[giver].add(-passed).at[receiver].add(passed)
    items = jnp.searchsorted(jnp.cumsum(tallies), jnp.arange(rows * top), side="right").astype(jnp.int32)
    grid = items.reshape(top, rows).T
    grid = grid[jax.random.permutation(jax.random.fold_in(own, 1), rows)]
    turn = jax.random.randint(jax.random.fold_in(own, 2), (rows, 1), 0, top)
    return jnp.take_along_axis(grid, (jnp.arange(top)[None, :] + turn) % top, axis=1)


def portions_of(number_of, total, reach, slope, full):
    portions = [(1 << 20) // math.isqrt(grade ** slope) + 1 for grade in range(1, number_of + 1)]
    largest = reach if full else min(reach, max(-(-total // number_of), total * portions[0] // sum(portions)))
    least = 1 if total - largest >= number_of - 1 else 0
    holding, surplus = [largest] + [least] * (number_of - 1), total - largest - least * (number_of - 1)
    while surplus > 0:
        movable = [i for i in range(1, number_of) if holding[i] < largest] or [i for i in range(1, number_of) if holding[i] < reach]
        pool, left = sum([portions[i] for i in movable]), surplus
        for i in movable:
            addition = min(reach - holding[i], max(1, left * portions[i] // pool), surplus)
            holding[i] = holding[i] + addition
            surplus = surplus - addition
    return np.array(holding)


def normal_values(rng, shape, scale, bound, cuts=(), held_as=jnp.bfloat16):
    entries = scale * jax.random.normal(rng, shape, jnp.float32)
    if cuts:
        entries = entries * level_of(rng, shape, cuts, -0.22, 0.18)
    return jnp.clip(entries, -bound, bound).astype(held_as)


def setup_inputs(seed: int = 0) -> dict:
    keys = jax.random.split(jax.random.key(seed), 13)
    tokens = normal_values(keys[0], (TOKENS, D), 1.0, 6.0, ((0, 128),))
    layer_cotangent = normal_values(keys[1], (TOKENS, D), 1.0, 6.0, ((0, 128),))
    attn_gain = jnp.clip(1.0 + 0.15 * jax.random.normal(keys[2], (D,), jnp.float32), 0.25, 1.75)
    qkv_weight = normal_values(keys[3], (3, D, HEADS * HEAD_DIM), D ** -0.5, 0.1875, ((2, 8),), jnp.float32)
    out_weight = normal_values(keys[4], (HEADS * HEAD_DIM, D), (max(1, HEADS * HEAD_DIM * 8 // LEN)) ** -0.5, 2.5, ((0, 8),), jnp.float32)
    rel_bias = normal_values(keys[5], (HEADS, BUCKETS), 1.0, 4.0, ((0, 8),), jnp.float32)
    moe_gain = jnp.clip(1.0 + 0.15 * jax.random.normal(keys[6], (D,), jnp.float32), 0.25, 1.75)
    router_weight = normal_values(keys[7], (D, EXPERTS), (2 * D) ** -0.5, 0.125, (), jnp.float32)
    expert_in = normal_values(keys[8], (EXPERTS, 2, D, FF), D ** -0.5, 0.1875, ((0, 16), (3, 8)), jnp.float32)
    expert_out = normal_values(keys[9], (EXPERTS, FF, D), (FF // 2) ** -0.5, 0.15625, ((0, 16), (1, 8)), jnp.float32)
    routes_keys = jax.random.split(jax.random.fold_in(keys[10], 1), TOKENS // TOK_DEV)
    routes_turns = jax.random.permutation(jax.random.fold_in(keys[10], 3), TOKENS // TOK_DEV)
    routes = jax.vmap(lambda own, number: routed_block(jax.random.fold_in(keys[10], 2), own, number, TOK_DEV, EXPERTS, TOP, 2 * CAP, 2))(routes_keys, routes_turns).reshape((TOKENS, TOP))
    buckets = draw_buckets(jax.random.fold_in(keys[12], 71), 0)
    return dict(tokens=tokens, layer_cotangent=layer_cotangent, attn_gain=attn_gain, qkv_weight=qkv_weight, out_weight=out_weight, rel_bias=rel_bias, moe_gain=moe_gain, router_weight=router_weight, expert_in=expert_in, expert_out=expert_out, routes=routes, buckets=buckets)


EPSILON = 1e-06
HIGHEST = lax.Precision.HIGHEST
SCORE_SCALE = 0.125

@jax.custom_vjp
def low(v):
    return lax.optimization_barrier(v.astype(jnp.bfloat16)).astype(jnp.float32)

@jax.custom_vjp
def low_back(v):
    return v

def low_keep(v):
    return (low(v), None)

def low_pass(kept, grad):
    return (grad,)

def back_keep(v):
    return (v, None)

def back_low(kept, grad):
    return (low(grad),)
low.defvjp(low_keep, low_pass)
low_back.defvjp(back_keep, back_low)

def normalize(values, gain):
    return values * lax.rsqrt(lax.optimization_barrier(jnp.mean(values * values, axis=-1, keepdims=True)) + EPSILON) * gain

def geglu(gate_input, up_input):
    return jax.nn.gelu(gate_input, approximate=True) * up_input

def device_slots(routes):
    groups = N_WIDE * N_NARROW
    order = routes.reshape(groups, TOK_DEV, TOP).transpose(0, 2, 1).reshape(groups, TOP * TOK_DEV)
    named = (order[:, :, None] == jnp.arange(EXPERTS, dtype=jnp.int32)).astype(jnp.int32)
    earlier = jnp.cumsum(named, axis=1) - named
    place = lax.optimization_barrier(jnp.sum(earlier * named, axis=2))
    slot = jnp.where(place < CAP, order * CAP + place, -1)
    return slot.reshape(groups, TOP, TOK_DEV).astype(jnp.int32)

def run_expert(inputs):
    expert_rows, pair, back_weight = inputs
    pair = low(pair)
    back_weight = low(back_weight)
    gate_input = low_back(jnp.dot(expert_rows, pair[0], precision=HIGHEST))
    up_input = low_back(jnp.dot(expert_rows, pair[1], precision=HIGHEST))
    middles = low(geglu(gate_input, up_input))
    return low(low_back(jnp.dot(middles, back_weight, precision=HIGHEST)))

def reference(tokens, layer_cotangent, attn_gain, qkv_weight, out_weight, rel_bias, moe_gain, router_weight, expert_in, expert_out, routes, buckets):
    groups = N_WIDE * N_NARROW
    slot = device_slots(routes)
    cells = jnp.arange(EXPERTS * CAP, dtype=jnp.int32)
    picks = (slot[:, :, None, :] == cells[None, None, :, None]).astype(jnp.float32)
    choose = (routes[:, :, None] == jnp.arange(EXPERTS, dtype=jnp.int32)).astype(jnp.float32)
    places = jnp.arange(LEN, dtype=jnp.int32)
    bucket_grid = buckets[(places[None, :] - places[:, None] + LEN - 1).astype(jnp.int32)]

    def forward(inputs, gain_one, qkv_w, out_w, bias_w, gain_two, router_w, pair_w, back_w):
        normed_one = low(normalize(inputs, gain_one))
        qkv_low = low(qkv_w)
        bias_grid = low(bias_w)[:, bucket_grid]

        def attend(sequence_rows):
            projected = low(low_back(jnp.einsum('td,cdf->ctf', sequence_rows, qkv_low, precision=HIGHEST)))
            projected = projected.reshape(3, LEN, HEADS, HEAD_DIM)

            def block(index):
                start = (index * QBLOCK).astype(jnp.int32)
                query = lax.dynamic_slice_in_dim(projected[0], start, QBLOCK, 0)
                bias_rows = lax.dynamic_slice_in_dim(bias_grid, start, QBLOCK, 1)
                scores = low_back(jnp.einsum('ihd,jhd->hij', query, projected[1], precision=HIGHEST) * SCORE_SCALE) + bias_rows
                weights = low(jax.nn.softmax(scores, axis=-1))
                return low(low_back(jnp.einsum('hij,jhd->ihd', weights, projected[2], precision=HIGHEST)))
            outputs = lax.map(jax.checkpoint(block), jnp.arange(LEN // QBLOCK, dtype=jnp.int32))
            return outputs.reshape(LEN, HEADS * HEAD_DIM)
        attended = lax.map(jax.checkpoint(attend), normed_one.reshape(TOKENS // LEN, LEN, D))
        attended = low_back(jnp.dot(attended.reshape(TOKENS, HEADS * HEAD_DIM), low(out_w), precision=HIGHEST))
        middle = inputs + attended
        normed_two = normalize(middle, gain_two)
        logits = jnp.dot(normed_two, router_w, precision=HIGHEST)
        gates = jax.nn.softmax(lax.optimization_barrier(jnp.sum(choose * logits[:, None, :], axis=-1)), axis=-1)
        grouped = low(normed_two).reshape(groups, TOK_DEV, D)
        buffer = low_back(jnp.einsum('gkst,gtd->gsd', picks, grouped, precision=HIGHEST))
        expert_rows = buffer.reshape(groups, EXPERTS, CAP, D).transpose(1, 0, 2, 3).reshape(EXPERTS, groups * CAP, D)
        returned = lax.map(jax.checkpoint(run_expert), (expert_rows, pair_w, back_w))
        returned = returned.reshape(EXPERTS, groups, CAP, D).transpose(1, 0, 2, 3).reshape(groups, EXPERTS * CAP, D)
        chosen = jnp.einsum('gkst,gsd->gktd', picks, returned, precision=HIGHEST)
        gate_rows = gates.reshape(groups, TOK_DEV, TOP).transpose(0, 2, 1)
        mixed = lax.optimization_barrier(jnp.sum(gate_rows[:, :, :, None] * chosen, axis=1)).reshape(TOKENS, D)
        return middle + mixed
    layer, pull = jax.vjp(forward, tokens.astype(jnp.float32), attn_gain, qkv_weight, out_weight, rel_bias, moe_gain, router_weight, expert_in, expert_out)
    grads = pull(layer_cotangent.astype(jnp.float32))
    return (layer.astype(jnp.bfloat16), grads[0], grads[1], grads[2], grads[3], grads[4], grads[5], grads[6], grads[7], grads[8])
```

```python
import math

import jax
import jax.numpy as jnp
from jax import lax
from jax.experimental import pallas as pl
from jax.experimental.pallas import tpu as pltpu
from jax.sharding import PartitionSpec as P

HEAD_DIM = 64
EXPERTS = 32
BUCKETS = 32
TOP = 2
LEN = 1408
WIDTH = 1024
TOK = 176
CAP = 13
SLOTS = 16
EPSILON = 1e-06
BLOCK = 128
SPAN = 2816
LOG2E = math.log2(math.e)
HIGHEST = lax.Precision.HIGHEST
F32 = jnp.float32
BF16 = jnp.bfloat16
NT = (((1,), (1,)), ((), ()))
TN = (((0,), (0,)), ((), ()))
VMEM = pl.BlockSpec(memory_space=pltpu.VMEM)
SMEM = pl.BlockSpec(memory_space=pltpu.SMEM)
HIDDEN = 352
PADDED = 384
ROWS = 416
HALF = 208


def shape(dims, dtype):
    return jax.ShapeDtypeStruct(dims, dtype)


def call(kernel, name, out_shape, ins, scratch=(), flops=1e9, transcendentals=0, smem=0):
    outs = tuple(out_shape)
    moved = sum(math.prod(a.shape) * a.dtype.itemsize for a in (*ins, *outs))
    return pl.pallas_call(
        kernel,
        out_shape=outs,
        in_specs=[SMEM] * smem + [VMEM] * (len(ins) - smem),
        out_specs=tuple([VMEM] * len(outs)),
        scratch_shapes=list(scratch),
        compiler_params=pltpu.CompilerParams(vmem_limit_bytes=52 << 20),
        cost_estimate=pl.CostEstimate(
            flops=int(flops), bytes_accessed=moved, transcendentals=int(transcendentals)
        ),
        name=name,
    )(*ins)


def dot(a, b, dims=None, precision=None):
    if dims is None:
        dims = (((1,), (0,)), ((), ()))
    return lax.dot_general(a, b, dims, precision=precision, preferred_element_type=F32)


def block_of(i):
    return pl.ds(pl.multiple_of(i * BLOCK, BLOCK), BLOCK)


def offset_row(buckets, bias_ref, head):
    total = jnp.zeros(buckets.shape, F32)
    for bucket in range(BUCKETS):
        total = jnp.where(buckets == bucket, bias_ref[head, bucket], total)
    return total


def skew(row):
    return pltpu.roll(
        jnp.broadcast_to(row, (BLOCK, SPAN)), SPAN - (BLOCK - 1), 1, stride=1, stride_axis=0
    )


def attend_forward_kernel(
    place_ref, bias_ref, *refs
):
    shards = refs[:8]
    gain_ref, w_ref, buckets_ref = refs[8:11]
    h_ref, q_ref, k_ref, v_ref, o_ref, lse_ref, band, key_parts, value_parts = refs[11:]
    count = LEN // BLOCK
    for head in range(2):
        band[head] = skew(offset_row(buckets_ref[...], bias_ref, head) * LOG2E)
    weights = [w_ref[c].astype(BF16) for c in range(3)]
    low_tok = lax.broadcasted_iota(jnp.int32, (TOK, 128), 1) < HEAD_DIM
    for index, shard in enumerate(shards):
        rows = pl.ds(pl.multiple_of(place_ref[index] * TOK, TOK), TOK)
        x = shard[...].astype(F32)
        scale = lax.rsqrt(jnp.mean(x * x, axis=-1, keepdims=True) + EPSILON)
        normed = (x * scale * gain_ref[...]).astype(BF16)
        h_ref[rows, :] = normed
        q, k, v = (dot(normed, w).astype(BF16) for w in weights)
        q_ref[rows, :] = q
        k_ref[rows, :] = k
        v_ref[rows, :] = v
        zero = jnp.zeros_like(k)
        one = jnp.ones_like(v)
        key_parts[0, rows, :] = jnp.where(low_tok, k, zero)
        key_parts[1, rows, :] = jnp.where(low_tok, zero, k)
        value_parts[0, rows, :] = jnp.where(low_tok, v, one)
        value_parts[1, rows, :] = jnp.where(low_tok, one, v)
    low = lax.broadcasted_iota(jnp.int32, (BLOCK, 128), 1) < HEAD_DIM

    def attend(i, carry):
        rows = block_of(i)
        window = pl.ds(pl.multiple_of((count - 1 - i) * BLOCK, BLOCK), LEN)
        query = q_ref[rows, :]
        parts = []
        peaks = []
        for head in range(2):
            scores = dot(query, key_parts[head], NT) * (LOG2E / 8) + band[head, :, window]
            peak = jnp.max(scores, axis=-1, keepdims=True)
            weights = jnp.exp2(scores - peak).astype(BF16)
            parts.append(dot(weights, value_parts[head]))
            peaks.append(peak)
        top = jnp.where(low, parts[0], parts[1])
        totals = pltpu.roll(jnp.where(low, parts[1], parts[0]), HEAD_DIM, 1)
        o_ref[rows, :] = (top / totals).astype(BF16)
        logs = (jnp.where(low, peaks[0], peaks[1]) + jnp.log2(totals)).T
        lse_ref[0:1, rows] = logs[0:1]
        lse_ref[1:2, rows] = logs[HEAD_DIM : HEAD_DIM + 1]
        return carry

    lax.fori_loop(0, count, attend, 0)


def attend_forward(places, bias, shards, gain, weights, buckets):
    head = (LEN, 128)
    return call(
        attend_forward_kernel,
        "attend_forward",
        [shape((LEN, WIDTH), BF16)] + [shape(head, BF16)] * 4 + [shape((2, LEN), F32)],
        [places, bias, *shards, gain, weights, buckets],
        [pltpu.VMEM((2, BLOCK, SPAN), F32), pltpu.VMEM((2,) + head, BF16), pltpu.VMEM((2,) + head, BF16)],
        flops=4e9,
        transcendentals=4e6,
        smem=2,
    )


def attend_backward_kernel(
    bias_ref, q_ref, k_ref, v_ref, o_ref, do_ref, lse_ref, buckets_ref,
    out_ref, bias_grad_ref, band, band_grad, query_grad, sums,
):
    count = LEN // BLOCK
    for head in range(2):
        band[head] = skew(offset_row(buckets_ref[...], bias_ref, head) * LOG2E)
    band_grad[...] = jnp.zeros_like(band_grad)
    query_grad[...] = jnp.zeros_like(query_grad)
    low = lax.broadcasted_iota(jnp.int32, (BLOCK, 128), 1) < HEAD_DIM
    pick = (
        lax.broadcasted_iota(jnp.int32, (8, 128), 1) // HEAD_DIM
        == lax.broadcasted_iota(jnp.int32, (8, 128), 0)
    ).astype(F32)
    sums[...] = dot(pick, do_ref[...].astype(F32) * o_ref[...].astype(F32), NT, HIGHEST)

    def step(j, carry):
        rows = block_of(j)
        window = pl.ds(pl.multiple_of((count - 1 - j) * BLOCK, BLOCK), LEN)
        keys = k_ref[rows, :]
        values = v_ref[rows, :]
        zero = jnp.zeros_like(keys)
        key_grads = []
        value_grads = []
        for head in range(2):
            mine = low if head == 0 else jnp.logical_not(low)
            key = jnp.where(mine, keys, zero)
            value = jnp.where(mine, values, zero)
            scores = dot(key, q_ref[...], NT) * (LOG2E / 8) + band[head, :, window]
            probs = jnp.exp2(scores - lse_ref[head : head + 1, :])
            prob_grads = dot(value, do_ref[...], NT)
            score_grads = probs * (prob_grads - sums[head : head + 1, :])
            band_grad[head, :, window] += score_grads
            score_low = score_grads.astype(BF16)
            value_grads.append(dot(probs.astype(BF16), do_ref[...]))
            key_grads.append(dot(score_low, q_ref[...]))
            query_grad[...] += dot(key, score_low, TN)
        out_ref[rows, 128:256] = (jnp.where(low, *key_grads) * 0.125).astype(BF16)
        out_ref[rows, 256:384] = jnp.where(low, *value_grads).astype(BF16)
        return carry

    lax.fori_loop(0, count, step, 0)

    def turn(j, carry):
        rows = block_of(j)
        out_ref[rows, 0:128] = (query_grad[:, rows].T * 0.125).astype(BF16)
        return carry

    lax.fori_loop(0, count, turn, 0)
    hot = buckets_ref[...] == lax.broadcasted_iota(jnp.int32, (BUCKETS, SPAN), 0)
    for head in range(2):
        total = jnp.zeros((8, SPAN), F32)
        for group in range(BLOCK // 8):
            total = total + pltpu.roll(
                band_grad[head, group * 8 : (group + 1) * 8, :], (BLOCK - 1 - 8 * group) % SPAN, 1
            )
        row = jnp.zeros((1, SPAN), F32)
        for part in range(8):
            row = row + pltpu.roll(total, (SPAN - part) % SPAN, 1)[part : part + 1]
        by_bucket = jnp.sum(jnp.where(hot, row, 0.0), axis=1, keepdims=True)
        bias_grad_ref[head : head + 1, :] = jnp.broadcast_to(by_bucket, (BUCKETS, 128)).T[0:1]


def attend_backward(bias, q, k, v, o, head_grads, logs, buckets):
    return call(
        attend_backward_kernel,
        "attend_backward",
        [shape((LEN, 384), BF16), shape((2, BUCKETS), F32)],
        [bias, q, k, v, o, head_grads, logs, buckets],
        [
            pltpu.VMEM((2, BLOCK, SPAN), F32),
            pltpu.VMEM((2, BLOCK, SPAN), F32),
            pltpu.VMEM((128, LEN), F32),
            pltpu.VMEM((8, LEN), F32),
        ],
        flops=8e9,
        transcendentals=4e6,
        smem=1,
    )


def place_rows(routes, rank, oh, before, first):
    earlier = dot(before, oh[rank].astype(BF16))
    if rank:
        earlier = earlier + first
    return jnp.sum(jnp.where(oh[rank], earlier, 0.0), axis=1, keepdims=True)


def dispatch_kernel(
    heads_ref, wout_ref, tok_ref, gain_ref, router_ref, routes_ref, turned_ref, cot_ref,
    middle_ref, gates_ref, rows_ref, grads_ref,
):
    heads = jnp.concatenate([heads_ref[n] for n in range(8)], axis=1)
    middle = tok_ref[...].astype(F32) + dot(heads, wout_ref[...])
    middle_ref[...] = middle
    scale = lax.rsqrt(jnp.mean(middle * middle, axis=-1, keepdims=True) + EPSILON)
    normed = middle * scale * gain_ref[...]
    logits = dot(normed, router_ref[...], precision=HIGHEST)
    expert = lax.broadcasted_iota(jnp.int32, (TOK, EXPERTS), 1)
    picked = [
        jnp.sum(jnp.where(routes_ref[:, c : c + 1] == expert, logits, 0.0), axis=1, keepdims=True)
        for c in range(TOP)
    ]
    peak = jnp.maximum(picked[0], picked[1])
    powers = [jnp.exp(p - peak) for p in picked]
    total = powers[0] + powers[1]
    gates = [p / total for p in powers]
    gates_ref[:, 0:1] = gates[0]
    gates_ref[:, 1:2] = gates[1]
    expert_down = lax.broadcasted_iota(jnp.int32, (EXPERTS, TOK), 0)
    before = (
        lax.broadcasted_iota(jnp.int32, (TOK, TOK), 0) < lax.broadcasted_iota(jnp.int32, (TOK, TOK), 1)
    ).astype(BF16)
    cells = lax.broadcasted_iota(jnp.int32, (EXPERTS * SLOTS, TOK), 0)
    named = [turned_ref[c : c + 1, :] == expert_down for c in range(TOP)]
    earlier = [dot(n.astype(BF16), before) for n in named]
    earlier[1] = earlier[1] + jnp.sum(named[0].astype(F32), axis=1, keepdims=True)
    picks = []
    for c in range(TOP):
        place = jnp.sum(jnp.where(named[c], earlier[c], 0.0), axis=0, keepdims=True).astype(jnp.int32)
        slot = jnp.where(place < CAP, turned_ref[c : c + 1, :] * SLOTS + place, -1)
        picks.append((cells == slot).astype(F32))
    rows_ref[...] = dot((picks[0] + picks[1]).astype(BF16), normed.astype(BF16)).astype(BF16)
    cot = cot_ref[...].astype(F32)
    grads_ref[...] = (
        dot(picks[0].astype(BF16), (gates[0] * cot).astype(BF16))
        + dot(picks[1].astype(BF16), (gates[1] * cot).astype(BF16))
    ).astype(BF16)


def slot_picks(routes_ref):
    expert = lax.broadcasted_iota(jnp.int32, (TOK, EXPERTS), 1)
    before = (
        lax.broadcasted_iota(jnp.int32, (TOK, TOK), 1) < lax.broadcasted_iota(jnp.int32, (TOK, TOK), 0)
    ).astype(BF16)
    named = [routes_ref[:, c : c + 1] == expert for c in range(TOP)]
    earlier = [dot(before, n.astype(BF16)) for n in named]
    earlier[1] = earlier[1] + jnp.sum(named[0].astype(F32), axis=0, keepdims=True)
    cells = lax.broadcasted_iota(jnp.int32, (TOK, EXPERTS * SLOTS), 1)
    picks = []
    for c in range(TOP):
        place = jnp.sum(jnp.where(named[c], earlier[c], 0.0), axis=1, keepdims=True).astype(jnp.int32)
        slot = jnp.where(place < CAP, routes_ref[:, c : c + 1] * SLOTS + place, -1)
        picks.append((cells == slot).astype(F32))
    return named, picks


def combine_kernel(
    returned_ref, middle_ref, gates_ref, cot_ref, routes_ref, gain_ref,
    layer_ref, logit_ref, router_grad_ref,
):
    named, picks = slot_picks(routes_ref)
    chosen = [dot(p.astype(BF16), returned_ref[...]) for p in picks]
    gates = [gates_ref[:, 0:1], gates_ref[:, 1:2]]
    middle = middle_ref[...]
    layer_ref[...] = (middle + (gates[0] * chosen[0] + gates[1] * chosen[1])).astype(BF16)
    cot = cot_ref[...].astype(F32)
    gate_grads = [jnp.sum(cot * c, axis=-1, keepdims=True) for c in chosen]
    mean = gates[0] * gate_grads[0] + gates[1] * gate_grads[1]
    logit_grads = sum(
        jnp.where(n, g * (d - mean), 0.0) for n, g, d in zip(named, gates, gate_grads)
    )
    logit_ref[...] = logit_grads
    scale = lax.rsqrt(jnp.mean(middle * middle, axis=-1, keepdims=True) + EPSILON)
    normed = middle * scale * gain_ref[...]
    router_grad_ref[...] = dot(logit_grads, normed, TN, HIGHEST)


def middle_grad_kernel(
    rows_ref, logit_ref, middle_ref, cot_ref, routes_ref, gain_ref, router_ref, wout_ref,
    middle_grad_ref, low_ref, heads_ref, gain_grad_ref,
):
    _, picks = slot_picks(routes_ref)
    normed_grad = dot((picks[0] + picks[1]).astype(BF16), rows_ref[...]) + dot(
        logit_ref[...], router_ref[...], NT, HIGHEST
    )
    middle = middle_ref[...]
    scale = lax.rsqrt(jnp.mean(middle * middle, axis=-1, keepdims=True) + EPSILON)
    unit = middle * scale
    gain_grad_ref[...] = jnp.sum(normed_grad * unit, axis=0, keepdims=True)
    weighted = normed_grad * gain_ref[...]
    middle_grad = cot_ref[...].astype(F32) + scale * (
        weighted - unit * jnp.mean(weighted * unit, axis=-1, keepdims=True)
    )
    middle_grad_ref[...] = middle_grad
    low = middle_grad.astype(BF16)
    low_ref[...] = low
    for n in range(8):
        heads_ref[n] = dot(low, wout_ref[n * 128 : (n + 1) * 128, :], NT).astype(BF16)


CUBIC = 0.044715
ROOT = math.sqrt(2.0 / math.pi)


def expert_forward_kernel(rows_ref, pair_ref, down_ref, mid_ref, gate_ref, up_ref, out_ref):
    def step(i, carry):
        rows = pl.ds(pl.multiple_of(i * HALF, HALF), HALF)
        inner = dot(rows_ref[rows, :], pair_ref[...])
        gate = inner[:, : 2 * PADDED]
        up = inner[:, 2 * PADDED :]
        square = gate * gate
        turned = jnp.tanh(ROOT * gate * (1.0 + CUBIC * square))
        half = 0.5 * (1.0 + turned)
        curved = gate * half
        slope = half + 0.5 * gate * (1.0 - turned * turned) * (ROOT * (1.0 + 3.0 * CUBIC * square))
        mid = (curved * up).astype(BF16)
        mid_ref[rows, :] = mid
        gate_ref[rows, :] = (up * slope).astype(BF16)
        up_ref[rows, :] = curved.astype(BF16)
        out_ref[rows, :] = dot(mid, down_ref[...]).astype(BF16)
        return carry

    lax.fori_loop(0, 4 * ROWS // HALF, step, 0)


def expert_backward_kernel(grads_ref, pair_ref, down_ref, gate_ref, up_ref, inner_ref, out_ref):
    def step(i, carry):
        rows = pl.ds(pl.multiple_of(i * HALF, HALF), HALF)
        mid_grad = dot(grads_ref[rows, :], down_ref[...], NT)
        inner_ref[rows, : 2 * PADDED] = (mid_grad * gate_ref[rows, :].astype(F32)).astype(BF16)
        inner_ref[rows, 2 * PADDED :] = (mid_grad * up_ref[rows, :].astype(F32)).astype(BF16)
        out_ref[rows, :] = dot(inner_ref[rows, :], pair_ref[...], NT).astype(BF16)
        return carry

    lax.fori_loop(0, 4 * ROWS // HALF, step, 0)


def on_device(
    tokens,
    layer_cotangent,
    attn_gain,
    qkv_weight,
    out_weight,
    rel_bias,
    moe_gain,
    router_weight,
    expert_in,
    expert_out,
    routes,
    buckets,
):
    narrow = lax.axis_index("narrow")
    core = lax.rem(narrow, 2)
    x = lax.div(narrow, 2)

    def shift(value, step):
        return lax.ppermute(value, "narrow", [(i, (i + 2 * step) % 8) for i in range(8)])

    def swap(value):
        return lax.ppermute(value, "narrow", [(i, i ^ 1) for i in range(8)])

    def flip(value, axis, mask):
        size = lax.axis_size(axis)
        return lax.ppermute(value, axis, [(i, i ^ mask) for i in range(size)])

    def sum_four(value, axis, unit):
        near = value + flip(value, axis, unit)
        far = flip(value, axis, 2 * unit) + flip(value, axis, 3 * unit)
        return near + far

    def sum_wide(value):
        return sum_four(sum_four(value, "wide", 1), "wide", 4)

    def sum_narrow(value):
        value = sum_four(value, "narrow", 2)
        return value + flip(value, "narrow", 1)

    def reduce_wide(value):
        parts = value.reshape((16, value.shape[0] // 16) + value.shape[1:])
        arrived = lax.all_to_all(parts, "wide", 0, 0, tiled=True)
        summed = jnp.sum(arrived.astype(F32), axis=0).astype(BF16)
        return lax.all_gather(summed, "wide", axis=0, tiled=True).astype(F32)

    exchange_groups = [
        [w * 8 + chip * 2 + c for w in range(16) for c in range(2)] for chip in range(4)
    ]

    def exchange(value):
        return lax.all_to_all(
            value, ("wide", "narrow"), 0, 0, tiled=True, axis_index_groups=exchange_groups
        )

    near = [tokens, shift(tokens, 1), shift(tokens, -1), shift(tokens, 2)]
    shards = near + [swap(s) for s in near]
    chips = [x, lax.rem(x + 3, 4), lax.rem(x + 1, 4), lax.rem(x + 2, 4)]
    places = jnp.stack([2 * c + core for c in chips] + [2 * c + (1 - core) for c in chips])
    places = places.astype(jnp.int32)

    wout = lax.all_gather(out_weight.astype(BF16), "narrow", axis=0, tiled=True)
    bias = rel_bias.astype(BF16).astype(F32)
    offsets = jnp.pad(buckets, (0, 1), constant_values=-1)[None]
    backward_offsets = jnp.pad(buckets[::-1], (0, 1), constant_values=-1)[None]

    def own_and_other(weights):
        own = lax.dynamic_index_in_dim(weights, core, 0, keepdims=False).astype(BF16)
        other = lax.dynamic_index_in_dim(weights, 1 - core, 0, keepdims=False).astype(BF16)
        return own, other

    def widen(value, axis):
        pads = [(0, 0)] * value.ndim
        pads[axis] = (0, PADDED - HIDDEN)
        return jnp.pad(value, pads)

    pair_own, pair_other = own_and_other(expert_in)
    down_own, down_other = own_and_other(expert_out)
    pair_own, pair_other = widen(pair_own, 2), widen(pair_other, 2)
    down_own, down_other = widen(down_own, 1 - 1), widen(down_other, 1 - 1)
    pair_new, down_new = swap(pair_other), swap(down_other)
    pair = jnp.concatenate([pair_own[0], pair_new[0], pair_own[1], pair_new[1]], axis=1)
    down = jnp.concatenate([down_own, down_new], axis=0)

    gain_one = attn_gain[None]
    gain_two = moe_gain[None]
    normed, q, k, v, attended, logs = attend_forward(
        places, bias, shards, gain_one, qkv_weight, offsets
    )
    heads = lax.all_to_all(attended.reshape(8, TOK, 128), "narrow", 0, 0, tiled=True)
    middle, gates, send_rows, send_grads = call(
        dispatch_kernel,
        "dispatch",
        [
            shape((TOK, WIDTH), F32),
            shape((TOK, TOP), F32),
            shape((EXPERTS * SLOTS, WIDTH), BF16),
            shape((EXPERTS * SLOTS, WIDTH), BF16),
        ],
        [heads, wout, tokens, gain_two, router_weight, routes, routes.T, layer_cotangent],
        flops=2e9,
    )

    def to_experts(send):
        arrived = exchange(send.reshape(EXPERTS, SLOTS, WIDTH))
        own = arrived[:, :CAP].reshape(ROWS, WIDTH)
        left = shift(own, 1)
        right = shift(own, -1)
        over_top = shift(left[:HALF], 1)
        over_end = shift(right[HALF:], -1)
        return jnp.concatenate([own, left, right, over_top, over_end], axis=0)

    def from_experts(terms):
        own = terms[:ROWS]
        left_top, left_end = terms[ROWS : ROWS + HALF], terms[ROWS + HALF : 2 * ROWS]
        right_top, right_end = terms[2 * ROWS : 2 * ROWS + HALF], terms[2 * ROWS + HALF : 3 * ROWS]
        over_top, over_end = terms[3 * ROWS : 3 * ROWS + HALF], terms[3 * ROWS + HALF :]

        def add(a, b):
            return (a.astype(F32) + b.astype(F32)).astype(BF16)

        from_top = shift(over_top, -1)
        from_end = shift(over_end, 1)
        got_left_end = shift(left_end, -1)
        got_right_top = shift(right_top, 1)
        got_left_top = shift(add(left_top, from_top), -1)
        got_right_end = shift(add(right_end, from_end), 1)
        top = own[:HALF].astype(F32) + got_left_top.astype(F32) + got_right_top.astype(F32)
        end = own[HALF:].astype(F32) + got_left_end.astype(F32) + got_right_end.astype(F32)
        summed = jnp.concatenate([top, end], axis=0).astype(BF16).reshape(EXPERTS, CAP, WIDTH)
        padded = jnp.pad(summed, ((0, 0), (0, SLOTS - CAP), (0, 0)))
        return exchange(padded).reshape(EXPERTS * SLOTS, WIDTH)

    expert_rows = to_experts(send_rows)
    term_grads = to_experts(send_grads)
    count = 4 * ROWS
    mid, gate_slope, up_slope, terms = call(
        expert_forward_kernel,
        "expert_forward",
        [shape((count, 2 * PADDED), BF16)] * 3 + [shape((count, WIDTH), BF16)],
        [expert_rows, pair, down],
        flops=7.8e9,
        transcendentals=1.3e6,
    )
    returned = from_experts(terms)
    inner_grads, row_terms = call(
        expert_backward_kernel,
        "expert_backward",
        [shape((count, 4 * PADDED), BF16), shape((count, WIDTH), BF16)],
        [term_grads, pair, down, gate_slope, up_slope],
        flops=7.8e9,
    )
    row_grads = from_experts(row_terms)
    pair_grad = dot(expert_rows, inner_grads, TN)
    down_grad = dot(mid, term_grads, TN)

    layer_out, logit_grads, router_grad = call(
        combine_kernel,
        "combine",
        [shape((TOK, WIDTH), BF16), shape((TOK, EXPERTS), F32), shape((EXPERTS, WIDTH), F32)],
        [returned, middle, gates, layer_cotangent, routes, gain_two],
    )
    middle_grad, middle_low, send_heads, moe_gain_grad = call(
        middle_grad_kernel,
        "middle_grad",
        [
            shape((TOK, WIDTH), F32),
            shape((TOK, WIDTH), BF16),
            shape((8, TOK, 128), BF16),
            shape((1, WIDTH), F32),
        ],
        [row_grads, logit_grads, middle, layer_cotangent, routes, gain_two, router_weight, wout],
    )
    head_grads = lax.all_to_all(send_heads, "narrow", 0, 0, tiled=True).reshape(LEN, 128)
    attended_grad = lax.all_gather(middle_low, "narrow", axis=0, tiled=True)
    out_weight_grad = reduce_wide(dot(attended, attended_grad, TN).astype(BF16))
    projected_grads, bias_grad = attend_backward(
        bias, q, k, v, attended, head_grads, logs, backward_offsets
    )

    proj = jnp.transpose(qkv_weight.astype(BF16), (1, 0, 2)).reshape(WIDTH, 384)
    by_core = projected_grads.reshape(4, 2, TOK, 384)
    sent = lax.dynamic_index_in_dim(by_core, 1 - core, 1, keepdims=False).reshape(4 * TOK, 384)
    kept = lax.dynamic_index_in_dim(by_core, core, 1, keepdims=False).reshape(4 * TOK, 384)
    other_terms = swap(dot(sent, proj, NT).astype(BF16))
    by_chip = (dot(kept, proj, NT) + other_terms.astype(F32)).astype(BF16).reshape(4, TOK, WIDTH)

    def chip_part(step):
        return lax.dynamic_index_in_dim(by_chip, lax.rem(x + step, 4), 0, keepdims=False)

    normed_grad = chip_part(0).astype(F32)
    for step in (1, 2, 3):
        normed_grad = normed_grad + shift(chip_part(step), step).astype(F32)
    proj_grad = dot(normed, projected_grads, TN).astype(BF16)
    qkv_weight_grad = jnp.transpose(reduce_wide(proj_grad).reshape(WIDTH, 3, 128), (1, 0, 2))

    inputs = tokens.astype(F32)
    scale = lax.rsqrt(jnp.mean(inputs * inputs, axis=-1, keepdims=True) + EPSILON)
    unit = inputs * scale
    weighted = normed_grad * gain_one
    input_grad = middle_grad + scale * (
        weighted - unit * jnp.mean(weighted * unit, axis=-1, keepdims=True)
    )
    gain_grad = jnp.sum(normed_grad * unit, axis=0)

    small = jnp.concatenate([gain_grad, bias_grad.reshape(2 * BUCKETS), jnp.zeros((64,), F32)])
    small = sum_wide(small.reshape(9, 128))
    rel_bias_grad = small.reshape(1152)[WIDTH : WIDTH + 2 * BUCKETS].reshape(2, BUCKETS)
    attn_gain_grad = sum_narrow(small).reshape(1152)[:WIDTH]
    shared = sum_narrow(sum_wide(jnp.concatenate([router_grad, moe_gain_grad], axis=0)))

    pair_parts = pair_grad.reshape(WIDTH, 2, 2, PADDED)
    pair_parts = jnp.transpose(pair_parts, (2, 1, 0, 3))[..., :HIDDEN]
    down_parts = down_grad.reshape(2, PADDED, WIDTH)[:, :HIDDEN]

    def assemble(own, got):
        first = core == 0
        return jnp.stack([jnp.where(first, own, got), jnp.where(first, got, own)])

    pair_grads = assemble(pair_parts[0], swap(pair_parts[1].astype(BF16)).astype(F32))
    down_grads = assemble(down_parts[0], swap(down_parts[1].astype(BF16)).astype(F32))
    return (
        layer_out,
        input_grad,
        attn_gain_grad,
        qkv_weight_grad,
        out_weight_grad,
        rel_bias_grad,
        shared[EXPERTS],
        shared[:EXPERTS].T,
        pair_grads,
        down_grads,
    )


def solution(mesh):
    placed = (
        P(("wide", "narrow"), None),
        P(("wide", "narrow"), None),
        P(),
        P(None, None, "narrow"),
        P("narrow", None),
        P("narrow", None),
        P(),
        P(),
        P("wide", None, None, "narrow"),
        P("wide", "narrow", None),
        P(("wide", "narrow"), None),
        P(),
    )
    return jax.shard_map(
        on_device,
        mesh=mesh,
        in_specs=placed,
        out_specs=(
            P(("wide", "narrow"), None),
            P(("wide", "narrow"), None),
            P(),
            P(None, None, "narrow"),
            P("narrow", None),
            P("narrow", None),
            P(),
            P(),
            P("wide", None, None, "narrow"),
            P("wide", "narrow", None),
        ),
        check_vma=False,
    )
```

```python
import functools
import math

import jax
import jax.numpy as jnp
from jax import lax
from jax.experimental import pallas as pl
from jax.experimental.pallas import tpu as pltpu
from jax.sharding import PartitionSpec as P

HEAD_DIM = 64
EXPERTS = 32
BUCKETS = 32
TOP = 2
LEN = 1408
WIDTH = 1024
TOK = 176
CAP = 13
SLOTS = 16
EPSILON = 1e-06
BLOCK = 128
SPAN = 2816
LOG2E = math.log2(math.e)
HIGHEST = lax.Precision.HIGHEST
F32 = jnp.float32
BF16 = jnp.bfloat16
NT = (((1,), (1,)), ((), ()))
TN = (((0,), (0,)), ((), ()))
VMEM = pl.BlockSpec(memory_space=pltpu.VMEM)
SMEM = pl.BlockSpec(memory_space=pltpu.SMEM)
HIDDEN = 352
PADDED = 384
FULL = 2 * PADDED
ROWS = 416
HALF = 208
TILED = 432


def shape(dims, dtype):
    return jax.ShapeDtypeStruct(dims, dtype)


def call(kernel, name, out_shape, ins, scratch=(), smem=0, micros=0.1, mib=24):
    outs = tuple(out_shape)
    return pl.pallas_call(
        kernel,
        out_shape=outs,
        in_specs=[SMEM] * smem + [VMEM] * (len(ins) - smem),
        out_specs=tuple([VMEM] * len(outs)),
        scratch_shapes=list(scratch),
        compiler_params=pltpu.CompilerParams(vmem_limit_bytes=mib << 20),
        cost_estimate=pl.CostEstimate(
            flops=int(micros * 1.15e9), bytes_accessed=0, transcendentals=0
        ),
        name=name,
    )(*ins)


def dot(a, b, dims=None, precision=None):
    if dims is None:
        dims = (((1,), (0,)), ((), ()))
    return lax.dot_general(a, b, dims, precision=precision, preferred_element_type=F32)


def block_of(i):
    return pl.ds(pl.multiple_of(i * BLOCK, BLOCK), BLOCK)


def offset_row(buckets, bias_ref, head):
    total = jnp.zeros(buckets.shape, F32)
    for bucket in range(BUCKETS):
        total = jnp.where(buckets == bucket, bias_ref[head, bucket], total)
    return total


def skew(row):
    return pltpu.roll(
        jnp.broadcast_to(row, (BLOCK, SPAN)), SPAN - (BLOCK - 1), 1, stride=1, stride_axis=0
    )


def project_kernel(place_ref, *refs):
    shards = refs[:8]
    gain_ref, w_ref, h_ref, q_ref, k_ref, v_ref, proj_ref = refs[8:]
    weights = jnp.concatenate([w_ref[c].astype(BF16) for c in range(3)], axis=1)
    for index, shard in enumerate(shards):
        rows = pl.ds(pl.multiple_of(place_ref[index] * TOK, TOK), TOK)
        x = shard[...].astype(F32)
        scale = lax.rsqrt(jnp.mean(x * x, axis=-1, keepdims=True) + EPSILON)
        normed = (x * scale * gain_ref[...]).astype(BF16)
        h_ref[rows, :] = normed
        projected = dot(normed, weights).astype(BF16)
        for c, ref in enumerate((q_ref, k_ref, v_ref)):
            ref[rows, :] = projected[:, c * 128 : (c + 1) * 128]
    for c in range(3):
        proj_ref[c * 128 : (c + 1) * 128, :] = w_ref[c].T.astype(BF16)


def project(places, shards, gain, weights):
    head = shape((LEN, 128), BF16)
    return call(
        project_kernel,
        "project",
        [shape((LEN, WIDTH), BF16), head, head, head, shape((384, WIDTH), BF16)],
        [places, *shards, gain, weights],
        smem=1,
        micros=50,
    )


def attend_forward_kernel(
    bias_ref, q_ref, k_ref, v_ref, buckets_ref, o_ref, lse_ref, band, key_parts, value_parts
):
    count = LEN // BLOCK
    for head in range(2):
        band[head] = skew(offset_row(buckets_ref[...], bias_ref, head) * LOG2E)
    low_all = lax.broadcasted_iota(jnp.int32, (LEN, 128), 1) < HEAD_DIM
    keys, values = k_ref[...], v_ref[...]
    zero, one = jnp.zeros_like(keys), jnp.ones_like(values)
    key_parts[0] = jnp.where(low_all, keys, zero)
    key_parts[1] = jnp.where(low_all, zero, keys)
    value_parts[0] = jnp.where(low_all, values, one)
    value_parts[1] = jnp.where(low_all, one, values)
    low = lax.broadcasted_iota(jnp.int32, (BLOCK, 128), 1) < HEAD_DIM

    def attend(i, carry):
        rows = block_of(i)
        window = pl.ds(pl.multiple_of((count - 1 - i) * BLOCK, BLOCK), LEN)
        query = q_ref[rows, :]
        parts = []
        peaks = []
        for head in range(2):
            scores = dot(query, key_parts[head], NT) * (LOG2E / 8) + band[head, :, window]
            peak = jnp.max(scores, axis=-1, keepdims=True)
            weights = jnp.exp2(scores - peak).astype(BF16)
            parts.append(dot(weights, value_parts[head]))
            peaks.append(peak)
        top = jnp.where(low, parts[0], parts[1])
        totals = pltpu.roll(jnp.where(low, parts[1], parts[0]), HEAD_DIM, 1)
        o_ref[rows, :] = (top / totals).astype(BF16)
        logs = (jnp.where(low, peaks[0], peaks[1]) + jnp.log2(totals)).T
        lse_ref[0:1, rows] = logs[0:1]
        lse_ref[1:2, rows] = logs[HEAD_DIM : HEAD_DIM + 1]
        return carry

    lax.fori_loop(0, count, attend, 0)


def attend_forward(bias, q, k, v, buckets):
    head = (LEN, 128)
    return call(
        attend_forward_kernel,
        "attend_forward",
        [shape(head, BF16), shape((2, LEN), F32)],
        [bias, q, k, v, buckets],
        [pltpu.VMEM((2, BLOCK, SPAN), F32), pltpu.VMEM((2,) + head, BF16), pltpu.VMEM((2,) + head, BF16)],
        smem=1,
        micros=50,
    )


def attend_backward_kernel(
    bias_ref, q_ref, k_ref, v_ref, o_ref, do_ref, lse_ref, buckets_ref,
    out_ref, bias_grad_ref, band, band_grad, query_grad, sums,
):
    count = LEN // BLOCK
    for head in range(2):
        band[head] = skew(offset_row(buckets_ref[...], bias_ref, head) * LOG2E)
    band_grad[...] = jnp.zeros_like(band_grad)
    query_grad[...] = jnp.zeros_like(query_grad)
    low = lax.broadcasted_iota(jnp.int32, (BLOCK, 128), 1) < HEAD_DIM
    pick = (
        lax.broadcasted_iota(jnp.int32, (8, 128), 1) // HEAD_DIM
        == lax.broadcasted_iota(jnp.int32, (8, 128), 0)
    ).astype(F32)
    sums[...] = dot(pick, do_ref[...].astype(F32) * o_ref[...].astype(F32), NT, HIGHEST)

    def step(j, carry):
        rows = block_of(j)
        window = pl.ds(pl.multiple_of((count - 1 - j) * BLOCK, BLOCK), LEN)
        keys = k_ref[rows, :]
        values = v_ref[rows, :]
        zero = jnp.zeros_like(keys)
        key_grads = []
        value_grads = []
        for head in range(2):
            mine = low if head == 0 else jnp.logical_not(low)
            key = jnp.where(mine, keys, zero)
            value = jnp.where(mine, values, zero)
            scores = dot(key, q_ref[...], NT) * (LOG2E / 8) + band[head, :, window]
            probs = jnp.exp2(scores - lse_ref[head : head + 1, :])
            prob_grads = dot(value, do_ref[...], NT)
            score_grads = probs * (prob_grads - sums[head : head + 1, :])
            band_grad[head, :, window] += score_grads
            score_low = score_grads.astype(BF16)
            value_grads.append(dot(probs.astype(BF16), do_ref[...]))
            key_grads.append(dot(score_low, q_ref[...]))
            query_grad[...] += dot(key, score_low, TN)
        out_ref[rows, 128:256] = (jnp.where(low, *key_grads) * 0.125).astype(BF16)
        out_ref[rows, 256:384] = jnp.where(low, *value_grads).astype(BF16)
        return carry

    lax.fori_loop(0, count, step, 0)

    def turn(j, carry):
        rows = block_of(j)
        out_ref[rows, 0:128] = (query_grad[:, rows].T * 0.125).astype(BF16)
        return carry

    lax.fori_loop(0, count, turn, 0)
    hot = buckets_ref[...] == lax.broadcasted_iota(jnp.int32, (BUCKETS, SPAN), 0)
    for head in range(2):
        total = jnp.zeros((8, SPAN), F32)
        for group in range(BLOCK // 8):
            total = total + pltpu.roll(
                band_grad[head, group * 8 : (group + 1) * 8, :], (BLOCK - 1 - 8 * group) % SPAN, 1
            )
        row = jnp.zeros((1, SPAN), F32)
        for part in range(8):
            row = row + pltpu.roll(total, (SPAN - part) % SPAN, 1)[part : part + 1]
        by_bucket = jnp.sum(jnp.where(hot, row, 0.0), axis=1, keepdims=True)
        bias_grad_ref[head : head + 1, :] = jnp.broadcast_to(by_bucket, (BUCKETS, 128)).T[0:1]


def attend_backward(bias, q, k, v, o, head_grads, logs, buckets):
    return call(
        attend_backward_kernel,
        "attend_backward",
        [shape((LEN, 384), BF16), shape((2, BUCKETS), F32)],
        [bias, q, k, v, o, head_grads, logs, buckets],
        [
            pltpu.VMEM((2, BLOCK, SPAN), F32),
            pltpu.VMEM((2, BLOCK, SPAN), F32),
            pltpu.VMEM((128, LEN), F32),
            pltpu.VMEM((8, LEN), F32),
        ],
        smem=1,
        micros=50,
    )


def iota(dims, axis):
    return lax.broadcasted_iota(jnp.int32, dims, axis)


def spread_kernel(turned_ref, routes_ref, cot_ref, picks_ref, place_ref, grads_ref):
    down = iota((EXPERTS, TOK), 0)
    before = (iota((TOK, TOK), 0) < iota((TOK, TOK), 1)).astype(BF16)
    named = [turned_ref[c : c + 1, :] == down for c in range(TOP)]
    earlier = [dot(n.astype(BF16), before) for n in named]
    earlier[1] = earlier[1] + jnp.sum(named[0].astype(F32), axis=1, keepdims=True)
    cells = iota((EXPERTS * SLOTS, TOK), 0)
    picks = jnp.zeros((EXPERTS * SLOTS, TOK), F32)
    for c in range(TOP):
        place = jnp.sum(jnp.where(named[c], earlier[c], 0.0), axis=0, keepdims=True).astype(jnp.int32)
        slot = jnp.where(place < CAP, turned_ref[c : c + 1, :] * SLOTS + place, -1)
        picks = picks + (cells == slot).astype(F32)
    picks = picks.astype(BF16)
    picks_ref[...] = picks
    grads_ref[...] = dot(picks, cot_ref[...]).astype(BF16)
    across = iota((TOK, EXPERTS), 1)
    after = (iota((TOK, TOK), 1) < iota((TOK, TOK), 0)).astype(BF16)
    named = [routes_ref[:, c : c + 1] == across for c in range(TOP)]
    earlier = [dot(after, n.astype(BF16)) for n in named]
    earlier[1] = earlier[1] + jnp.sum(named[0].astype(F32), axis=0, keepdims=True)
    for c in range(TOP):
        place = jnp.sum(jnp.where(named[c], earlier[c], 0.0), axis=1, keepdims=True)
        place_ref[:, c : c + 1] = place.astype(jnp.int32)


def split_low(value):
    high = value.astype(BF16)
    return high, (value - high.astype(F32)).astype(BF16)


def embed(values):
    rows = iota((EXPERTS * SLOTS, EXPERTS), 0)
    first = iota((EXPERTS * SLOTS, EXPERTS), 1) * SLOTS + CAP
    high, low = split_low(values)
    return dot((rows == first).astype(BF16), high) + dot((rows == first + 1).astype(BF16), low)


def dispatch_kernel(
    heads_ref, wout_ref, tok_ref, gain_ref, router_ref, routes_ref, place_ref, picks_ref,
    middle_ref, gates_ref, rows_ref,
):
    heads = jnp.concatenate([heads_ref[n] for n in range(8)], axis=1)
    middle = tok_ref[...].astype(F32) + dot(heads, wout_ref[...])
    middle_ref[...] = middle
    scale = lax.rsqrt(jnp.mean(middle * middle, axis=-1, keepdims=True) + EPSILON)
    normed = middle * scale * gain_ref[...]
    rows_ref[...] = dot(picks_ref[...], normed.astype(BF16)).astype(BF16)
    logits = dot(normed, router_ref[...], NT, HIGHEST)
    across = iota((TOK, EXPERTS), 1)
    named = [routes_ref[:, c : c + 1] == across for c in range(TOP)]
    picked = [jnp.sum(jnp.where(n, logits, 0.0), axis=1, keepdims=True) for n in named]
    peak = jnp.maximum(picked[0], picked[1])
    powers = [jnp.exp(p - peak) for p in picked]
    total = powers[0] + powers[1]
    table = jnp.zeros((EXPERTS, 128), F32)
    for c in range(TOP):
        gate = powers[c] / total
        gates_ref[:, c : c + 1] = gate
        spot = (iota((TOK, 128), 1) == place_ref[:, c : c + 1]) & (place_ref[:, c : c + 1] < CAP)
        expert = named[c].astype(F32).astype(BF16)
        high, low = split_low(gate)
        for term in (high, low):
            table = table + dot(expert, jnp.where(spot, term.astype(F32), 0.0).astype(BF16), TN)
    rows_ref[:, :128] = (rows_ref[:, :128].astype(F32) + embed(table)).astype(BF16)


def slot_picks(routes_ref, place_ref):
    cells = iota((TOK, EXPERTS * SLOTS), 1)
    picks = []
    for c in range(TOP):
        place = place_ref[:, c : c + 1]
        slot = jnp.where(place < CAP, routes_ref[:, c : c + 1] * SLOTS + place, -1)
        picks.append(cells == slot)
    return picks


def middle_grad_kernel(
    rows_ref, gates_ref, middle_ref, cot_ref, routes_ref, place_ref, gain_ref, router_ref, wout_ref,
    middle_grad_ref, low_ref, heads_ref, gain_grad_ref, logit_ref,
):
    spots = iota((EXPERTS, EXPERTS * SLOTS), 1)
    first = iota((EXPERTS, EXPERTS * SLOTS), 0) * SLOTS + CAP
    packed = rows_ref[:, :128]
    table = [dot((spots == first + step).astype(BF16), packed).astype(BF16) for step in range(2)]
    across = iota((TOK, EXPERTS), 1)
    named = [routes_ref[:, c : c + 1] == across for c in range(TOP)]
    gates = [gates_ref[:, c : c + 1] for c in range(TOP)]
    gate_grads = []
    for c in range(TOP):
        expert = named[c].astype(F32).astype(BF16)
        lines = dot(expert, table[0]) + dot(expert, table[1])
        place = place_ref[:, c : c + 1]
        spot = (iota((TOK, 128), 1) == place) & (place < CAP)
        gate_grads.append(jnp.sum(jnp.where(spot, lines, 0.0), axis=1, keepdims=True))
    mean = gates[0] * gate_grads[0] + gates[1] * gate_grads[1]
    logit_grads = sum(
        jnp.where(n, g * (d - mean), 0.0) for n, g, d in zip(named, gates, gate_grads)
    )
    logit_ref[...] = logit_grads
    normed_grad = dot(logit_grads, router_ref[...], precision=HIGHEST)
    for gate, pick in zip(gates, slot_picks(routes_ref, place_ref)):
        normed_grad = normed_grad + gate * dot(pick.astype(F32).astype(BF16), rows_ref[...])
    middle = middle_ref[...]
    scale = lax.rsqrt(jnp.mean(middle * middle, axis=-1, keepdims=True) + EPSILON)
    unit = middle * scale
    gain_grad_ref[...] = jnp.sum(normed_grad * unit, axis=0, keepdims=True)
    weighted = normed_grad * gain_ref[...]
    middle_grad = cot_ref[...].astype(F32) + scale * (
        weighted - unit * jnp.mean(weighted * unit, axis=-1, keepdims=True)
    )
    middle_grad_ref[...] = middle_grad
    low = middle_grad.astype(BF16)
    low_ref[...] = low
    for n in range(8):
        heads_ref[n] = dot(low, wout_ref[n * 128 : (n + 1) * 128, :], NT).astype(BF16)


def combine_kernel(rows_ref, middle_ref, gates_ref, routes_ref, place_ref, layer_ref):
    layer = middle_ref[...]
    mixed = jnp.zeros_like(layer)
    for c, pick in enumerate(slot_picks(routes_ref, place_ref)):
        mixed = mixed + gates_ref[:, c : c + 1] * dot(pick.astype(F32).astype(BF16), rows_ref[...])
    layer_ref[...] = (layer + mixed).astype(BF16)


CUBIC = 0.044715
ROOT = math.sqrt(2.0 / math.pi)


def unpack_kernel(gated, blocks_ref, rows_ref):
    at = iota((ROWS, EXPERTS * SLOTS), 0)
    pick = (at // CAP) * SLOTS + at % CAP == iota((ROWS, EXPERTS * SLOTS), 1)
    rows_ref[:ROWS, :] = dot(pick.astype(F32).astype(BF16), blocks_ref[...]).astype(BF16)
    if gated:
        spots = iota((EXPERTS, EXPERTS * SLOTS), 1)
        first = iota((EXPERTS, EXPERTS * SLOTS), 0) * SLOTS + CAP
        lane = iota((128, ROWS), 1) % CAP == iota((128, ROWS), 0)
        mine = iota((EXPERTS, ROWS), 1) // CAP == iota((EXPERTS, ROWS), 0)
        rows_ref[ROWS:, :] = jnp.zeros((TILED - ROWS, WIDTH), BF16)
        terms = []
        for step in range(2):
            table = dot((spots == first + step).astype(BF16), blocks_ref[:, :128]).astype(BF16)
            spread = dot(table, lane.astype(F32).astype(BF16))
            terms.append(jnp.sum(jnp.where(mine, spread, 0.0), axis=0, keepdims=True))
        rows_ref[ROWS:, :ROWS] = stack_terms(*terms)


def stack_terms(high, low):
    step = iota((TILED - ROWS, ROWS), 0)
    return jnp.where(step == 0, high, jnp.where(step == 1, low, 0.0)).astype(BF16)


def unpack(blocks, gated):
    return call(
        functools.partial(unpack_kernel, gated),
        "unpack",
        [shape((TILED if gated else ROWS, WIDTH), BF16)],
        [blocks.reshape(EXPERTS * SLOTS, WIDTH)],
    )[0]


def expert_kernel(counts, *refs):
    groups = []
    for count in counts:
        groups.append(refs[: count + 1])
        refs = refs[count + 1 :]
    pair_ref, pair_new_ref, down_ref, down_new_ref = refs[:4]
    refs = refs[4:]
    for *rows_refs, grads_ref in groups:
        mid_ref, inner_ref, out_ref, back_top_ref, back_end_ref = refs[:5]
        refs = refs[5:]
        if len(rows_refs) == 1:
            rows = rows_refs[0][:ROWS, :]
        else:
            rows = jnp.concatenate([rows_refs[0][...], rows_refs[1][:HALF, :]], axis=0)
        one = dot(rows, pair_ref[...], NT)
        two = dot(rows, pair_new_ref[...], NT)
        gate = jnp.concatenate([one[:, :PADDED], two[:, :PADDED]], axis=1)
        up = jnp.concatenate([one[:, PADDED:], two[:, PADDED:]], axis=1)
        down = jnp.concatenate([down_ref[...], down_new_ref[...]], axis=0)
        mid_grad = dot(grads_ref[...], down, NT)
        square = gate * gate
        turned = jnp.tanh(ROOT * gate * (1.0 + CUBIC * square))
        half = 0.5 * (1.0 + turned)
        curved = gate * half
        slope = half + 0.5 * gate * (1.0 - turned * turned) * (ROOT * (1.0 + 3.0 * CUBIC * square))
        mid = (curved * up).astype(BF16)
        mid_ref[...] = mid
        gate_grad = (mid_grad * (up * slope)).astype(BF16)
        up_grad = (mid_grad * curved).astype(BF16)
        for part in range(2):
            cut = slice(part * PADDED, (part + 1) * PADDED)
            inner_ref[:, 2 * part * PADDED : (2 * part + 1) * PADDED] = gate_grad[:, cut]
            inner_ref[:, (2 * part + 1) * PADDED : (2 * part + 2) * PADDED] = up_grad[:, cut]
        product = (mid.astype(F32) * mid_grad).astype(BF16)
        line = dot(jnp.ones((8, FULL), BF16), product, NT)[0:1]
        high, low = split_low(line)
        back_end_ref[HALF:, :] = jnp.zeros((TILED - ROWS, WIDTH), BF16)
        back_end_ref[HALF:, :ROWS] = stack_terms(high.astype(F32), low.astype(F32))
        pair = jnp.concatenate([pair_ref[...], pair_new_ref[...]], axis=0)
        back = dot(inner_ref[...], pair).astype(BF16)
        back_top_ref[...] = back[:HALF]
        back_end_ref[:HALF, :] = back[HALF:]
        out_ref[...] = dot(mid_ref[...], down).astype(BF16)


def run_expert(chunks, weights):
    results = call(
        functools.partial(expert_kernel, [len(rows) for rows, _ in chunks]),
        "expert",
        [
            shape((ROWS, FULL), BF16),
            shape((ROWS, 2 * FULL), BF16),
            shape((ROWS, WIDTH), BF16),
            shape((HALF, WIDTH), BF16),
            shape((TILED - HALF, WIDTH), BF16),
        ]
        * len(chunks),
        [a for rows, grads in chunks for a in (*rows, grads)] + weights,
        micros=50,
        mib=40,
    )
    return [list(results[5 * i : 5 * i + 5]) for i in range(len(chunks))]


def join_kernel(
    own_top, own_end, near_top, near_end, left_top, far_top, right_end, far_end,
    left_out, right_out, part_top, part_end,
):
    left_out[...] = (left_top[...].astype(F32) + far_top[...].astype(F32)).astype(BF16)
    right_out[...] = (right_end[...].astype(F32) + far_end[...].astype(F32)).astype(BF16)
    part_top[...] = own_top[...].astype(F32) + near_top[...].astype(F32)
    part_end[...] = own_end[...].astype(F32) + near_end[...].astype(F32)


def join(*pieces):
    return call(
        join_kernel,
        "join",
        [shape(p.shape, t) for t, p in ((BF16, pieces[0]), (BF16, pieces[1]), (F32, pieces[0]), (F32, pieces[1]))],
        pieces,
    )


def spread_slots(rows, out_ref):
    at = iota((EXPERTS * SLOTS, ROWS), 1)
    pick = iota((EXPERTS * SLOTS, ROWS), 0) == (at // CAP) * SLOTS + at % CAP
    out_ref[...] = dot(pick.astype(F32).astype(BF16), rows.astype(BF16)).astype(BF16)


def collect_kernel(part_top, part_end, got_top, got_end, out_ref):
    end = part_end[...] + got_end[...].astype(F32)
    rows = jnp.concatenate([part_top[...] + got_top[...].astype(F32), end[:HALF]], axis=0)
    spread_slots(rows, out_ref)
    line = jnp.sum(end[HALF:, :ROWS], axis=0, keepdims=True)
    mine = iota((EXPERTS, ROWS), 1) // CAP == iota((EXPERTS, ROWS), 0)
    spot = (iota((ROWS, 128), 0) % CAP == iota((ROWS, 128), 1)).astype(F32).astype(BF16)
    table = jnp.zeros((EXPERTS, 128), F32)
    for term in split_low(line):
        table = table + dot(jnp.where(mine, term.astype(F32), 0.0).astype(BF16), spot)
    out_ref[:, :128] = (out_ref[:, :128].astype(F32) + embed(table)).astype(BF16)


def collect_out_kernel(own, left, right, over, out_ref):
    rows = (own[...].astype(F32) + left[...].astype(F32)) + (
        right[...].astype(F32) + over[...].astype(F32)
    )
    spread_slots(rows, out_ref)


def put_weight_grads(lefts, scaled, targets):
    width = 256
    for base in range(0, len(targets) * PADDED, width):
        total = jnp.zeros((width, WIDTH), F32)
        for chunk in range(4):
            at = slice(chunk * ROWS, (chunk + 1) * ROWS)
            total = total + dot(lefts[chunk][:, base : base + width], scaled[at, :], TN)
        for index, target in enumerate(targets):
            start = max(base, index * PADDED)
            stop = min(base + width, index * PADDED + HIDDEN)
            if start < stop:
                part = total[start - base : stop - base]
                to = slice(start - index * PADDED, stop - index * PADDED)
                target[to, :] = part.astype(target.dtype)


def scale_rows(part, gates, scaled, base):
    at = slice(base, base + part.shape[0])
    for cut in range(WIDTH // 128):
        lanes = slice(cut * 128, (cut + 1) * 128)
        scaled[at, lanes] = (part[:, lanes].astype(F32) * gates).astype(BF16)


def pair_grad_kernel(*refs):
    rights, lefts = refs[:5], refs[5:9]
    own_ref, low_ref, gates_ref, scaled = refs[9:]
    same = iota((ROWS, ROWS), 0) == iota((ROWS, ROWS), 1)
    ones = jnp.ones((ROWS, 128), BF16)
    for chunk in range(4):
        base = chunk * ROWS
        tile = rights[chunk][ROWS:, :ROWS] if chunk < 3 else rights[4][HALF:, :ROWS]
        gates = jnp.zeros((ROWS, 128), F32)
        for term in range(2):
            line = tile[term : term + 1, :].astype(F32)
            gates = gates + dot(jnp.where(same, line, 0.0).astype(BF16), ones)
        gates_ref[base : base + ROWS, :] = gates
        if chunk < 3:
            scale_rows(rights[chunk][:ROWS, :], gates, scaled, base)
        else:
            scale_rows(rights[3][...], gates[:HALF], scaled, base)
            scale_rows(rights[4][:HALF, :], gates[HALF:], scaled, base + HALF)
    put_weight_grads(lefts, scaled, [own_ref.at[0], own_ref.at[1], low_ref.at[0], low_ref.at[1]])


def down_grad_kernel(*refs):
    rights, lefts = refs[:4], refs[4:8]
    gates_ref, own_ref, low_ref, scaled = refs[8:]
    for chunk in range(4):
        at = slice(chunk * ROWS, (chunk + 1) * ROWS)
        scale_rows(rights[chunk][...], gates_ref[at, :], scaled, chunk * ROWS)
    put_weight_grads(lefts, scaled, [own_ref.at[0], low_ref.at[0]])


def assemble_kernel(core_ref, pair_ref, pair_got_ref, down_ref, down_got_ref, pair_out, down_out):
    core = core_ref[0]
    pair_out[core] = pair_ref[...]
    pair_out[1 - core] = pair_got_ref[...].astype(F32)
    down_out[core] = down_ref[0]
    down_out[1 - core] = down_got_ref[0].astype(F32)


def halves_kernel(core_ref, pair_ref, down_ref, *outs):
    for which in range(2):
        expert = core_ref[which]
        pair_out, down_out = outs[2 * which : 2 * which + 2]
        zeros = jnp.zeros((PADDED - HIDDEN, WIDTH), BF16)
        for part in range(2):
            base = part * PADDED
            pair_out[base : base + HIDDEN, :] = pair_ref[expert, part].astype(BF16)
            pair_out[base + HIDDEN : base + PADDED, :] = zeros
        down_out[:HIDDEN, :] = down_ref[expert].astype(BF16)
        down_out[HIDDEN:, :] = zeros


def outer_kernel(heads_ref, low_ref, logit_ref, middle_ref, gain_ref, out_ref, router_ref):
    for n in range(8):
        out_ref[n * 128 : (n + 1) * 128, :] = dot(heads_ref[n], low_ref[...], TN).astype(BF16)
    middle = middle_ref[...]
    scale = lax.rsqrt(jnp.mean(middle * middle, axis=-1, keepdims=True) + EPSILON)
    router_ref[...] = dot(logit_ref[...], middle * scale * gain_ref[...], TN, HIGHEST)


def projection_kernel(grads_ref, normed_ref, proj_ref, gain_ref, outer_ref, out_ref, gain_grad_ref):
    total = dot(grads_ref[...], normed_ref[...], TN)
    out_ref[:384, :] = total.astype(BF16)
    gain_grad_ref[...] = jnp.sum(total * proj_ref[...].astype(F32), axis=0, keepdims=True) / gain_ref[...]
    out_ref[384:, :] = outer_ref[...]


def sent_kernel(order_ref, grads_ref, proj_ref, out_ref):
    for step in range(4):
        at = pl.ds(pl.multiple_of(order_ref[4 + step] * TOK, TOK), TOK)
        out_ref[step] = dot(grads_ref[at, :], proj_ref[...]).astype(BF16)


def kept_kernel(order_ref, grads_ref, proj_ref, got_ref, *outs):
    for step, out in enumerate(outs):
        at = pl.ds(pl.multiple_of(order_ref[step] * TOK, TOK), TOK)
        out[...] = (dot(grads_ref[at, :], proj_ref[...]) + got_ref[step].astype(F32)).astype(BF16)


def input_grad_kernel(own_ref, left_ref, right_ref, over_ref, tok_ref, gain_ref, middle_ref, out_ref):
    total = (own_ref[...].astype(F32) + left_ref[...].astype(F32)) + (
        right_ref[...].astype(F32) + over_ref[...].astype(F32)
    )
    inputs = tok_ref[...].astype(F32)
    scale = lax.rsqrt(jnp.mean(inputs * inputs, axis=-1, keepdims=True) + EPSILON)
    unit = inputs * scale
    weighted = total * gain_ref[...]
    out_ref[...] = middle_ref[...] + scale * (
        weighted - unit * jnp.mean(weighted * unit, axis=-1, keepdims=True)
    )


def share_kernel(parts_ref, out_ref):
    total = parts_ref[0].astype(F32)
    for index in range(1, 16):
        total = total + parts_ref[index].astype(F32)
    total = total.astype(BF16)
    for index in range(16):
        out_ref[index] = total


def finish_kernel(rows_ref, qkv_ref, out_ref):
    for c in range(3):
        for block in range(WIDTH // 128):
            cut = slice(block * 128, (block + 1) * 128)
            qkv_ref[c, cut, :] = rows_ref[c * 128 : (c + 1) * 128, cut].astype(F32).T
    out_ref[...] = rows_ref[384:512, :].astype(F32)


def on_device(
    tokens,
    layer_cotangent,
    attn_gain,
    qkv_weight,
    out_weight,
    rel_bias,
    moe_gain,
    router_weight,
    expert_in,
    expert_out,
    routes,
    buckets,
):
    narrow = lax.axis_index("narrow")
    core = lax.rem(narrow, 2)
    x = lax.div(narrow, 2)

    barrier = lax.optimization_barrier

    def shift(value, step):
        return lax.ppermute(value, "narrow", [(i, (i + 2 * step) % 8) for i in range(8)])

    def swap(value):
        return lax.ppermute(value, "narrow", [(i, i ^ 1) for i in range(8)])

    def flip(value, axis, mask):
        size = lax.axis_size(axis)
        return lax.ppermute(value, axis, [(i, i ^ mask) for i in range(size)])

    def sum_four(value, axis, unit):
        low = barrier(value.astype(BF16))
        parts = [low] + [flip(low, axis, mask * unit) for mask in (1, 2, 3)]
        parts = [p.astype(F32) for p in parts]
        return (parts[0] + parts[1]) + (parts[2] + parts[3])

    exchange_groups = [
        [w * 8 + chip * 2 + c for w in range(16) for c in range(2)] for chip in range(4)
    ]

    def exchange(value):
        return lax.all_to_all(
            value, ("wide", "narrow"), 0, 0, tiled=True, axis_index_groups=exchange_groups
        )

    def blocks(send):
        return exchange(send.reshape(EXPERTS, SLOTS, WIDTH)).reshape(EXPERTS * SLOTS, WIDTH)

    picks, place, cot_rows = call(
        spread_kernel,
        "spread",
        [
            shape((EXPERTS * SLOTS, TOK), BF16),
            shape((TOK, TOP), jnp.int32),
            shape((EXPERTS * SLOTS, WIDTH), BF16),
        ],
        [routes.T, routes, layer_cotangent],
        micros=50,
    )
    wout = lax.all_gather(out_weight.astype(BF16), "narrow", axis=0, tiled=True)
    cot_arrived = blocks(cot_rows)
    near = [tokens, shift(tokens, 1), shift(tokens, -1), shift(tokens, 2)]
    shards = near + [swap(v) for v in near]

    pair, down, pair_other, down_other = call(
        halves_kernel,
        "halves",
        [shape((FULL, WIDTH), BF16), shape((PADDED, WIDTH), BF16)] * 2,
        [
            jnp.stack([core, 1 - core]).astype(jnp.int32),
            jnp.swapaxes(expert_in, 2, 3),
            expert_out,
        ],
        smem=1,
    )
    weights = [pair, swap(pair_other), down, swap(down_other)]
    chips = [x, lax.rem(x + 3, 4), lax.rem(x + 1, 4), lax.rem(x + 2, 4)]
    order = jnp.stack([2 * c + core for c in chips] + [2 * c + (1 - core) for c in chips])
    order = order.astype(jnp.int32)
    bias = rel_bias.astype(BF16).astype(F32)
    offsets = jnp.pad(buckets, (0, 1), constant_values=-1)[None]
    backward_offsets = jnp.pad(buckets[::-1], (0, 1), constant_values=-1)[None]
    gain_one = attn_gain[None]
    gain_two = moe_gain[None]
    router_rows = router_weight.T
    normed, q, k, v, proj = project(order, shards, gain_one, qkv_weight)
    q, k, v, cot_arrived, weights = barrier((q, k, v, cot_arrived, weights))
    cot_own = unpack(cot_arrived, False)
    q, cot_own = barrier((q, cot_own))
    cot_parts = [cot_own, shift(cot_own, 1), shift(cot_own, -1)]
    attended, logs = attend_forward(bias, q, k, v, offsets)
    heads = lax.all_to_all(attended.reshape(8, TOK, 128), "narrow", 0, 0, tiled=True)
    heads, cot_parts = barrier((heads, cot_parts))
    middle, gates, send_rows = call(
        dispatch_kernel,
        "dispatch",
        [
            shape((TOK, WIDTH), F32),
            shape((TOK, TOP), F32),
            shape((EXPERTS * SLOTS, WIDTH), BF16),
        ],
        [heads, wout, tokens, gain_two, router_rows, routes, place, picks],
    )

    send_rows, cot_far = barrier((send_rows, cot_own))
    cot_parts = cot_parts + [shift(cot_far, 2)]
    arrived = blocks(send_rows)

    row_own = unpack(arrived, True)
    row_left, row_right = shift(row_own, 1), shift(row_own, -1)
    results = run_expert([([row_own], cot_parts[0])], weights)
    row_left, row_right, results = barrier((row_left, row_right, results))
    over = [shift(row_left[:HALF], 1), shift(row_right[HALF:], -1)]
    row_parts = [row_own, row_left, row_right]
    results += run_expert([([row_left], cot_parts[1]), ([row_right], cot_parts[2])], weights)
    over, results = barrier((over, results))
    row_parts = row_parts + over
    results += run_expert([(over, cot_parts[3])], weights)
    mids, inners, outs = ([r[i] for r in results] for i in range(3))
    backs = [r[3:5] for r in results]

    def leave_far(over):
        return [shift(over[0], -1), shift(over[1], 1)]

    def leave_near(left, right):
        return [shift(right[0], 1), shift(left[1], -1)]

    def land(own, left, right, near, far):
        left_top, right_end, part_top, part_end = join(*own, *near, left[0], far[0], right[1], far[1])
        return [part_top, part_end, left_top, right_end]

    def arrive(parts):
        return [parts[0], parts[1], shift(parts[2], -1), shift(parts[3], 1)]

    far, near = leave_far(backs[3]), leave_near(*backs[1:3])
    pair_part, pair_low, gate_columns = call(
        pair_grad_kernel,
        "pair_grad",
        [
            shape((2, HIDDEN, WIDTH), F32),
            shape((2, HIDDEN, WIDTH), BF16),
            shape((4 * ROWS, 128), F32),
        ],
        [*row_parts, *inners],
        [pltpu.VMEM((4 * ROWS, WIDTH), BF16)],
    )
    far, near, pair_part, pair_low = barrier((far, near, pair_part, pair_low))
    back = call(
        collect_kernel,
        "collect",
        [shape((EXPERTS * SLOTS, WIDTH), BF16)],
        arrive(land(*backs[:3], near, far)),
    )[0]
    row_grads = blocks(back)
    outs, mids, back = barrier((outs, mids, back))
    outs = [outs[0], shift(outs[1], -1), shift(outs[2], 1), shift(outs[3], 2)]
    down_part, down_low = call(
        down_grad_kernel,
        "down_grad",
        [shape((1, HIDDEN, WIDTH), F32), shape((1, HIDDEN, WIDTH), BF16)],
        [*cot_parts, *mids, gate_columns],
        [pltpu.VMEM((4 * ROWS, WIDTH), BF16)],
        micros=50,
    )
    row_grads, down_part, down_low = barrier((row_grads, down_part, down_low))
    middle_grad, middle_low, send_heads, moe_gain_grad, logit_grads = call(
        middle_grad_kernel,
        "middle_grad",
        [
            shape((TOK, WIDTH), F32),
            shape((TOK, WIDTH), BF16),
            shape((8, TOK, 128), BF16),
            shape((1, WIDTH), F32),
            shape((TOK, EXPERTS), F32),
        ],
        [row_grads, gates, middle, layer_cotangent, routes, place, gain_two, router_rows, wout],
    )
    head_grads = lax.all_to_all(send_heads, "narrow", 0, 0, tiled=True).reshape(LEN, 128)
    outer, router_terms = call(
        outer_kernel,
        "outer",
        [shape((WIDTH, WIDTH), BF16), shape((EXPERTS, WIDTH), F32)],
        [heads, middle_low, logit_grads, middle, gain_two],
    )
    outer = lax.psum_scatter(outer, "narrow", scatter_dimension=0, tiled=True)
    back_out = call(
        collect_out_kernel, "collect_out", [shape((EXPERTS * SLOTS, WIDTH), BF16)], outs, micros=50
    )[0]
    head_grads, back_out, router_terms = barrier((head_grads, back_out, router_terms))
    returned = blocks(back_out)

    def to_chips(parts):
        return [parts[0]] + [shift(p, step) for p, step in zip(parts[1:], (-1, 1, 2))]

    projected_grads, bias_grad = attend_backward(
        bias, q, k, v, attended, head_grads, logs, backward_offsets
    )
    projected_grads, bias_grad, returned = barrier((projected_grads, bias_grad, returned))

    weight_grads, gain_grad = call(
        projection_kernel,
        "projection_grad",
        [shape((512, WIDTH), BF16), shape((1, WIDTH), F32)],
        [projected_grads, normed, proj, gain_one, outer],
    )
    arrived_grads = lax.all_to_all(weight_grads.reshape(16, 32, WIDTH), "wide", 0, 0, tiled=True)
    projected_grads, gain_grad, _ = barrier((projected_grads, gain_grad, weight_grads))

    sent = call(
        sent_kernel, "sent", [shape((4, TOK, WIDTH), BF16)], [order, projected_grads, proj], smem=1, micros=50
    )[0]
    kept = call(
        kept_kernel,
        "kept",
        [shape((TOK, WIDTH), BF16)] * 4,
        [order, projected_grads, proj, swap(sent)],
        smem=1,
    )
    gain_grad, _ = barrier((gain_grad, sent))
    small = jnp.concatenate(
        [
            router_terms,
            gain_grad,
            moe_gain_grad,
            jnp.pad(bias_grad.reshape(1, 64), ((0, 0), (0, WIDTH - 64))),
        ]
    )
    small = sum_four(sum_four(small, "wide", 1), "wide", 4)
    rel_bias_grad = small[EXPERTS + 2, : 2 * BUCKETS].reshape(2, BUCKETS)

    arrived_grads, kept = barrier((arrived_grads, kept))
    copies = call(share_kernel, "share", [shape((16, 32, WIDTH), BF16)], [arrived_grads])[0]
    gathered = lax.all_to_all(copies, "wide", 0, 0, tiled=True).reshape(512, WIDTH)
    returned, _ = barrier((returned, copies))
    layer_out = call(
        combine_kernel,
        "combine",
        [shape((TOK, WIDTH), BF16)],
        [returned, middle, gates, routes, place],
        micros=50,
    )[0]
    small, layer_out = barrier((small, layer_out))
    small = sum_four(small[: EXPERTS + 2], "narrow", 2)
    low = barrier(small.astype(BF16))
    small = low.astype(F32) + flip(low, "narrow", 1).astype(F32)
    pair_grads, down_grads = call(
        assemble_kernel,
        "assemble",
        [shape((2, 2, HIDDEN, WIDTH), F32), shape((2, HIDDEN, WIDTH), F32)],
        [core.astype(jnp.int32).reshape(1), pair_part, swap(pair_low), down_part, swap(down_low)],
        smem=1,
    )
    chip_parts = to_chips(kept)
    input_grad = call(
        input_grad_kernel,
        "input_grad",
        [shape((TOK, WIDTH), F32)],
        [*chip_parts, tokens, gain_one, middle_grad],
    )[0]
    qkv_weight_grad, out_weight_grad = call(
        finish_kernel,
        "finish",
        [shape((3, WIDTH, 128), F32), shape((128, WIDTH), F32)],
        [gathered],
    )
    return (
        layer_out,
        input_grad,
        small[EXPERTS],
        qkv_weight_grad,
        out_weight_grad,
        rel_bias_grad,
        small[EXPERTS + 1],
        small[:EXPERTS].T,
        jnp.swapaxes(pair_grads, 2, 3),
        down_grads,
    )


def solution(mesh):
    placed = (
        P(("wide", "narrow"), None),
        P(("wide", "narrow"), None),
        P(),
        P(None, None, "narrow"),
        P("narrow", None),
        P("narrow", None),
        P(),
        P(),
        P("wide", None, None, "narrow"),
        P("wide", "narrow", None),
        P(("wide", "narrow"), None),
        P(),
    )
    return jax.shard_map(
        on_device,
        mesh=mesh,
        in_specs=placed,
        out_specs=(
            P(("wide", "narrow"), None),
            P(("wide", "narrow"), None),
            P(),
            P(None, None, "narrow"),
            P("narrow", None),
            P("narrow", None),
            P(),
            P(),
            P("wide", None, None, "narrow"),
            P("wide", "narrow", None),
        ),
        check_vma=False,
    )
```

```python
import functools
import math

import jax
import jax.numpy as jnp
from jax import lax
from jax.experimental import pallas as pl
from jax.experimental.pallas import tpu as pltpu
from jax.sharding import PartitionSpec as P

HEAD_DIM = 64
EXPERTS = 32
BUCKETS = 32
TOP = 2
LEN = 1408
WIDTH = 1024
TOK = 176
CAP = 13
SLOTS = 16
EPSILON = 1e-06
BLOCK = 128
SPAN = 2816
LOG2E = math.log2(math.e)
HIGHEST = lax.Precision.HIGHEST
F32 = jnp.float32
BF16 = jnp.bfloat16
NT = (((1,), (1,)), ((), ()))
TN = (((0,), (0,)), ((), ()))
VMEM = pl.BlockSpec(memory_space=pltpu.VMEM)
SMEM = pl.BlockSpec(memory_space=pltpu.SMEM)
HIDDEN = 352
PADDED = 384
FULL = 2 * PADDED
ROWS = 416
HALF = 208
TILED = 432


def shape(dims, dtype):
    return jax.ShapeDtypeStruct(dims, dtype)


COSTS = {
    "dispatch": 50,
    "slots": 50,
    "collect": 50,
    "down_grad": 50,
    "halves": 50,
    "attend_forward": 4,
    "attend_backward": 50,
    "assemble": 50,
}


MEBIBYTES = {
    "attend_forward": 30,
    "dispatch": 56,
    "halves": 56,
    "expert": 40,
    "middle_grad": 56,
    "down_grad": 56,
    "assemble": 56,
}


def call(kernel, name, out_shape, ins, scratch=(), smem=0):
    outs = tuple(out_shape)
    return pl.pallas_call(
        kernel,
        out_shape=outs,
        in_specs=[SMEM] * smem + [VMEM] * (len(ins) - smem),
        out_specs=tuple([VMEM] * len(outs)),
        scratch_shapes=list(scratch),
        compiler_params=pltpu.CompilerParams(vmem_limit_bytes=MEBIBYTES.get(name, 24) << 20),
        cost_estimate=pl.CostEstimate(
            flops=int(COSTS.get(name, 0.1) * 1.15e9), bytes_accessed=0, transcendentals=0
        ),
        name=name,
    )(*ins)


def dot(a, b, dims=None, precision=None):
    if dims is None:
        dims = (((1,), (0,)), ((), ()))
    return lax.dot_general(a, b, dims, precision=precision, preferred_element_type=F32)


def block_of(i):
    return pl.ds(pl.multiple_of(i * BLOCK, BLOCK), BLOCK)


def offset_row(buckets, bias_ref, head):
    total = jnp.zeros(buckets.shape, F32)
    for bucket in range(BUCKETS):
        total = jnp.where(buckets == bucket, bias_ref[head, bucket], total)
    return total


def skew(row):
    return pltpu.roll(
        jnp.broadcast_to(row, (BLOCK, SPAN)), SPAN - (BLOCK - 1), 1, stride=1, stride_axis=0
    )


def attend_forward_kernel(place_ref, bias_ref, *refs):
    shards = refs[:8]
    (gain_ref, w_ref, buckets_ref, h_ref, qkv_ref, o_ref, lse_ref, proj_ref,
     band, key_parts, value_parts) = refs[8:]
    count = LEN // BLOCK
    for head in range(2):
        band[head] = skew(offset_row(buckets_ref[...], bias_ref, head) * LOG2E)
    weights = jnp.concatenate([w_ref[c].astype(BF16) for c in range(3)], axis=1)
    low_tok = lax.broadcasted_iota(jnp.int32, (TOK, 128), 1) < HEAD_DIM
    for index, shard in enumerate(shards):
        rows = pl.ds(pl.multiple_of(place_ref[index] * TOK, TOK), TOK)
        x = shard[...].astype(F32)
        scale = lax.rsqrt(jnp.mean(x * x, axis=-1, keepdims=True) + EPSILON)
        normed = (x * scale * gain_ref[...]).astype(BF16)
        h_ref[rows, :] = normed
        projected = dot(normed, weights).astype(BF16)
        qkv_ref[rows, :] = projected
        keys, values = projected[:, 128:256], projected[:, 256:]
        zero, one = jnp.zeros_like(keys), jnp.ones_like(values)
        key_parts[0, rows, :] = jnp.where(low_tok, keys, zero)
        key_parts[1, rows, :] = jnp.where(low_tok, zero, keys)
        value_parts[0, rows, :] = jnp.where(low_tok, values, one)
        value_parts[1, rows, :] = jnp.where(low_tok, one, values)
    for c in range(3):
        proj_ref[c * 128 : (c + 1) * 128, :] = w_ref[c].T.astype(BF16)
    low = lax.broadcasted_iota(jnp.int32, (BLOCK, 128), 1) < HEAD_DIM

    def attend(i, carry):
        rows = block_of(i)
        window = pl.ds(pl.multiple_of((count - 1 - i) * BLOCK, BLOCK), LEN)
        query = qkv_ref[rows, :128]
        parts = []
        peaks = []
        for head in range(2):
            scores = dot(query, key_parts[head], NT) * (LOG2E / 8) + band[head, :, window]
            peak = jnp.max(scores, axis=-1, keepdims=True)
            weights = jnp.exp2(scores - peak).astype(BF16)
            parts.append(dot(weights, value_parts[head]))
            peaks.append(peak)
        top = jnp.where(low, parts[0], parts[1])
        totals = pltpu.roll(jnp.where(low, parts[1], parts[0]), HEAD_DIM, 1)
        o_ref[rows, :] = (top / totals).astype(BF16)
        logs = (jnp.where(low, peaks[0], peaks[1]) + jnp.log2(totals)).T
        lse_ref[0:1, rows] = logs[0:1]
        lse_ref[1:2, rows] = logs[HEAD_DIM : HEAD_DIM + 1]
        return carry

    lax.fori_loop(0, count, attend, 0)


def attend_forward(places, bias, shards, gain, weights, buckets):
    head = (LEN, 128)
    return call(
        attend_forward_kernel,
        "attend_forward",
        [
            shape((LEN, WIDTH), BF16),
            shape((LEN, 384), BF16),
            shape(head, BF16),
            shape((2, LEN), F32),
            shape((384, WIDTH), BF16),
        ],
        [places, bias, *shards, gain, weights, buckets],
        [pltpu.VMEM((2, BLOCK, SPAN), F32), pltpu.VMEM((2,) + head, BF16), pltpu.VMEM((2,) + head, BF16)],
        smem=2,
    )


def attend_backward_kernel(
    bias_ref, qkv_ref, o_ref, do_ref, lse_ref, buckets_ref,
    out_ref, bias_grad_ref, band, band_grad, query_grad, sums,
):
    count = LEN // BLOCK
    for head in range(2):
        band[head] = skew(offset_row(buckets_ref[...], bias_ref, head) * LOG2E)
    band_grad[...] = jnp.zeros_like(band_grad)
    query_grad[...] = jnp.zeros_like(query_grad)
    low = lax.broadcasted_iota(jnp.int32, (BLOCK, 128), 1) < HEAD_DIM
    pick = (
        lax.broadcasted_iota(jnp.int32, (8, 128), 1) // HEAD_DIM
        == lax.broadcasted_iota(jnp.int32, (8, 128), 0)
    ).astype(F32)
    sums[...] = dot(pick, do_ref[...].astype(F32) * o_ref[...].astype(F32), NT, HIGHEST)

    def step(j, carry):
        rows = block_of(j)
        window = pl.ds(pl.multiple_of((count - 1 - j) * BLOCK, BLOCK), LEN)
        keys = qkv_ref[rows, 128:256]
        values = qkv_ref[rows, 256:]
        zero = jnp.zeros_like(keys)
        key_grads = []
        value_grads = []
        for head in range(2):
            mine = low if head == 0 else jnp.logical_not(low)
            key = jnp.where(mine, keys, zero)
            value = jnp.where(mine, values, zero)
            scores = dot(key, qkv_ref[:, :128], NT) * (LOG2E / 8) + band[head, :, window]
            probs = jnp.exp2(scores - lse_ref[head : head + 1, :])
            prob_grads = dot(value, do_ref[...], NT)
            score_grads = probs * (prob_grads - sums[head : head + 1, :])
            band_grad[head, :, window] += score_grads
            score_low = score_grads.astype(BF16)
            value_grads.append(dot(probs.astype(BF16), do_ref[...]))
            key_grads.append(dot(score_low, qkv_ref[:, :128]))
            query_grad[...] += dot(key, score_low, TN)
        out_ref[rows, 128:256] = (jnp.where(low, *key_grads) * 0.125).astype(BF16)
        out_ref[rows, 256:384] = jnp.where(low, *value_grads).astype(BF16)
        return carry

    lax.fori_loop(0, count, step, 0)

    def turn(j, carry):
        rows = block_of(j)
        out_ref[rows, 0:128] = (query_grad[:, rows].T * 0.125).astype(BF16)
        return carry

    lax.fori_loop(0, count, turn, 0)
    hot = buckets_ref[...] == lax.broadcasted_iota(jnp.int32, (BUCKETS, SPAN), 0)
    for head in range(2):
        total = jnp.zeros((8, SPAN), F32)
        for group in range(BLOCK // 8):
            total = total + pltpu.roll(
                band_grad[head, group * 8 : (group + 1) * 8, :], (BLOCK - 1 - 8 * group) % SPAN, 1
            )
        row = jnp.zeros((1, SPAN), F32)
        for part in range(8):
            row = row + pltpu.roll(total, (SPAN - part) % SPAN, 1)[part : part + 1]
        by_bucket = jnp.sum(jnp.where(hot, row, 0.0), axis=1, keepdims=True)
        bias_grad_ref[head : head + 1, :] = jnp.broadcast_to(by_bucket, (BUCKETS, 128)).T[0:1]


def attend_backward(bias, qkv, o, head_grads, logs, buckets):
    return call(
        attend_backward_kernel,
        "attend_backward",
        [shape((LEN, 384), BF16), shape((2, BUCKETS), F32)],
        [bias, qkv, o, head_grads, logs, buckets],
        [
            pltpu.VMEM((2, BLOCK, SPAN), F32),
            pltpu.VMEM((2, BLOCK, SPAN), F32),
            pltpu.VMEM((128, LEN), F32),
            pltpu.VMEM((8, LEN), F32),
        ],
        smem=1,
    )


def iota(dims, axis):
    return lax.broadcasted_iota(jnp.int32, dims, axis)


def spread_kernel(turned_ref, routes_ref, cot_ref, picks_ref, place_ref, grads_ref):
    down = iota((EXPERTS, TOK), 0)
    before = (iota((TOK, TOK), 0) < iota((TOK, TOK), 1)).astype(BF16)
    named = [turned_ref[c : c + 1, :] == down for c in range(TOP)]
    earlier = [dot(n.astype(BF16), before) for n in named]
    earlier[1] = earlier[1] + jnp.sum(named[0].astype(F32), axis=1, keepdims=True)
    cells = iota((EXPERTS * SLOTS, TOK), 0)
    picks = jnp.zeros((EXPERTS * SLOTS, TOK), F32)
    for c in range(TOP):
        place = jnp.sum(jnp.where(named[c], earlier[c], 0.0), axis=0, keepdims=True).astype(jnp.int32)
        slot = jnp.where(place < CAP, turned_ref[c : c + 1, :] * SLOTS + place, -1)
        picks = picks + (cells == slot).astype(F32)
    picks = picks.astype(BF16)
    picks_ref[...] = picks
    grads_ref[...] = dot(picks, cot_ref[...]).astype(BF16)
    across = iota((TOK, EXPERTS), 1)
    after = (iota((TOK, TOK), 1) < iota((TOK, TOK), 0)).astype(BF16)
    named = [routes_ref[:, c : c + 1] == across for c in range(TOP)]
    earlier = [dot(after, n.astype(BF16)) for n in named]
    earlier[1] = earlier[1] + jnp.sum(named[0].astype(F32), axis=0, keepdims=True)
    for c in range(TOP):
        place = jnp.sum(jnp.where(named[c], earlier[c], 0.0), axis=1, keepdims=True)
        place_ref[:, c : c + 1] = place.astype(jnp.int32)


def split_low(value):
    high = value.astype(BF16)
    return high, (value - high.astype(F32)).astype(BF16)


def embed(values):
    rows = iota((EXPERTS * SLOTS, EXPERTS), 0)
    first = iota((EXPERTS * SLOTS, EXPERTS), 1) * SLOTS + CAP
    high, low = split_low(values)
    return dot((rows == first).astype(BF16), high) + dot((rows == first + 1).astype(BF16), low)


def dispatch_kernel(order_ref, heads_ref, *refs):
    wouts = refs[:8]
    (tok_ref, gain_ref, router_ref, routes_ref, place_ref, picks_ref,
     middle_ref, gates_ref, rows_ref, all_ref) = refs[8:]
    for index, part in enumerate(wouts):
        at = pl.ds(pl.multiple_of(order_ref[index] * 128, 128), 128)
        all_ref[at, :] = part[...]
    heads = jnp.concatenate([heads_ref[n] for n in range(8)], axis=1)
    middle = tok_ref[...].astype(F32) + dot(heads, all_ref[...])
    middle_ref[...] = middle
    scale = lax.rsqrt(jnp.mean(middle * middle, axis=-1, keepdims=True) + EPSILON)
    normed = middle * scale * gain_ref[...]
    rows_ref[...] = dot(picks_ref[...], normed.astype(BF16)).astype(BF16)
    logits = dot(normed, router_ref[...], NT, HIGHEST)
    across = iota((TOK, EXPERTS), 1)
    named = [routes_ref[:, c : c + 1] == across for c in range(TOP)]
    picked = [jnp.sum(jnp.where(n, logits, 0.0), axis=1, keepdims=True) for n in named]
    peak = jnp.maximum(picked[0], picked[1])
    powers = [jnp.exp(p - peak) for p in picked]
    total = powers[0] + powers[1]
    table = jnp.zeros((EXPERTS, 128), F32)
    for c in range(TOP):
        gate = powers[c] / total
        gates_ref[:, c : c + 1] = gate
        spot = (iota((TOK, 128), 1) == place_ref[:, c : c + 1]) & (place_ref[:, c : c + 1] < CAP)
        expert = named[c].astype(F32).astype(BF16)
        high, low = split_low(gate)
        for term in (high, low):
            table = table + dot(expert, jnp.where(spot, term.astype(F32), 0.0).astype(BF16), TN)
    rows_ref[:, :128] = (rows_ref[:, :128].astype(F32) + embed(table)).astype(BF16)


def slots_kernel(routes_ref, place_ref, picks_ref):
    cells = iota((TOK, EXPERTS * SLOTS), 1)
    for c in range(TOP):
        place = place_ref[:, c : c + 1]
        slot = jnp.where(place < CAP, routes_ref[:, c : c + 1] * SLOTS + place, -1)
        picks_ref[c] = (cells == slot).astype(F32).astype(BF16)


def middle_grad_kernel(
    rows_ref, gates_ref, middle_ref, cot_ref, routes_ref, place_ref, picks_ref, gain_ref, router_ref, wout_ref,
    middle_grad_ref, low_ref, heads_ref, gain_grad_ref, logit_ref,
):
    spots = iota((EXPERTS, EXPERTS * SLOTS), 1)
    first = iota((EXPERTS, EXPERTS * SLOTS), 0) * SLOTS + CAP
    packed = rows_ref[:, :128]
    table = [dot((spots == first + step).astype(BF16), packed).astype(BF16) for step in range(2)]
    across = iota((TOK, EXPERTS), 1)
    named = [routes_ref[:, c : c + 1] == across for c in range(TOP)]
    gates = [gates_ref[:, c : c + 1] for c in range(TOP)]
    gate_grads = []
    for c in range(TOP):
        expert = named[c].astype(F32).astype(BF16)
        lines = dot(expert, table[0]) + dot(expert, table[1])
        place = place_ref[:, c : c + 1]
        spot = (iota((TOK, 128), 1) == place) & (place < CAP)
        gate_grads.append(jnp.sum(jnp.where(spot, lines, 0.0), axis=1, keepdims=True))
    mean = gates[0] * gate_grads[0] + gates[1] * gate_grads[1]
    logit_grads = sum(
        jnp.where(n, g * (d - mean), 0.0) for n, g, d in zip(named, gates, gate_grads)
    )
    logit_ref[...] = logit_grads
    normed_grad = dot(logit_grads, router_ref[...], precision=HIGHEST)
    for c, gate in enumerate(gates):
        normed_grad = normed_grad + gate * dot(picks_ref[c], rows_ref[...])
    middle = middle_ref[...]
    scale = lax.rsqrt(jnp.mean(middle * middle, axis=-1, keepdims=True) + EPSILON)
    unit = middle * scale
    gain_grad_ref[...] = jnp.sum(normed_grad * unit, axis=0, keepdims=True)
    weighted = normed_grad * gain_ref[...]
    middle_grad = cot_ref[...].astype(F32) + scale * (
        weighted - unit * jnp.mean(weighted * unit, axis=-1, keepdims=True)
    )
    middle_grad_ref[...] = middle_grad
    low = middle_grad.astype(BF16)
    low_ref[...] = low
    for n in range(8):
        heads_ref[n] = dot(low, wout_ref[n * 128 : (n + 1) * 128, :], NT).astype(BF16)


def combine_kernel(rows_ref, middle_ref, gates_ref, picks_ref, layer_ref):
    layer = middle_ref[...]
    mixed = jnp.zeros_like(layer)
    for c in range(TOP):
        mixed = mixed + gates_ref[:, c : c + 1] * dot(picks_ref[c], rows_ref[...])
    layer_ref[...] = (layer + mixed).astype(BF16)


CUBIC = 0.044715
ROOT = math.sqrt(2.0 / math.pi)


def unpack_kernel(gated, blocks_ref, rows_ref):
    at = iota((ROWS, EXPERTS * SLOTS), 0)
    pick = (at // CAP) * SLOTS + at % CAP == iota((ROWS, EXPERTS * SLOTS), 1)
    rows_ref[:ROWS, :] = dot(pick.astype(F32).astype(BF16), blocks_ref[...]).astype(BF16)
    if gated:
        spots = iota((EXPERTS, EXPERTS * SLOTS), 1)
        first = iota((EXPERTS, EXPERTS * SLOTS), 0) * SLOTS + CAP
        lane = iota((128, ROWS), 1) % CAP == iota((128, ROWS), 0)
        mine = iota((EXPERTS, ROWS), 1) // CAP == iota((EXPERTS, ROWS), 0)
        rows_ref[ROWS:, :] = jnp.zeros((TILED - ROWS, WIDTH), BF16)
        terms = []
        for step in range(2):
            table = dot((spots == first + step).astype(BF16), blocks_ref[:, :128]).astype(BF16)
            spread = dot(table, lane.astype(F32).astype(BF16))
            terms.append(jnp.sum(jnp.where(mine, spread, 0.0), axis=0, keepdims=True))
        rows_ref[ROWS:, :ROWS] = stack_terms(*terms)


def stack_terms(high, low):
    step = iota((TILED - ROWS, ROWS), 0)
    return jnp.where(step == 0, high, jnp.where(step == 1, low, 0.0)).astype(BF16)


def unpack(blocks, gated):
    return call(
        functools.partial(unpack_kernel, gated),
        "unpack",
        [shape((TILED if gated else ROWS, WIDTH), BF16)],
        [blocks.reshape(EXPERTS * SLOTS, WIDTH)],
    )[0]


def expert_kernel(counts, *refs):
    groups = []
    for count in counts:
        groups.append(refs[: count + 1])
        refs = refs[count + 1 :]
    pair_ref, pair_new_ref, down_ref, down_new_ref = refs[:4]
    refs = refs[4:]
    for *rows_refs, grads_ref in groups:
        mid_ref, inner_ref, out_top_ref, out_end_ref, back_top_ref, back_end_ref = refs[:6]
        refs = refs[6:]
        if len(rows_refs) == 1:
            rows = rows_refs[0][:ROWS, :]
        else:
            rows = jnp.concatenate([rows_refs[0][...], rows_refs[1][:HALF, :]], axis=0)
        one = dot(rows, pair_ref[...], NT)
        two = dot(rows, pair_new_ref[...], NT)
        gate = jnp.concatenate([one[:, :PADDED], two[:, :PADDED]], axis=1)
        up = jnp.concatenate([one[:, PADDED:], two[:, PADDED:]], axis=1)
        down = jnp.concatenate([down_ref[...], down_new_ref[...]], axis=0)
        mid_grad = dot(grads_ref[...], down, NT)
        square = gate * gate
        turned = jnp.tanh(ROOT * gate * (1.0 + CUBIC * square))
        half = 0.5 * (1.0 + turned)
        curved = gate * half
        slope = half + 0.5 * gate * (1.0 - turned * turned) * (ROOT * (1.0 + 3.0 * CUBIC * square))
        mid = (curved * up).astype(BF16)
        mid_ref[...] = mid
        gate_grad = (mid_grad * (up * slope)).astype(BF16)
        up_grad = (mid_grad * curved).astype(BF16)
        for part in range(2):
            cut = slice(part * PADDED, (part + 1) * PADDED)
            inner_ref[:, 2 * part * PADDED : (2 * part + 1) * PADDED] = gate_grad[:, cut]
            inner_ref[:, (2 * part + 1) * PADDED : (2 * part + 2) * PADDED] = up_grad[:, cut]
        product = (mid.astype(F32) * mid_grad).astype(BF16)
        line = dot(jnp.ones((8, FULL), BF16), product, NT)[0:1]
        high, low = split_low(line)
        back_end_ref[HALF:, :] = jnp.zeros((TILED - ROWS, WIDTH), BF16)
        back_end_ref[HALF:, :ROWS] = stack_terms(high.astype(F32), low.astype(F32))
        pair = jnp.concatenate([pair_ref[...], pair_new_ref[...]], axis=0)
        back = dot(inner_ref[...], pair).astype(BF16)
        back_top_ref[...] = back[:HALF]
        back_end_ref[:HALF, :] = back[HALF:]
        out = dot(mid_ref[...], down).astype(BF16)
        out_top_ref[...] = out[:HALF]
        out_end_ref[...] = out[HALF:]


def run_expert(chunks, weights):
    results = call(
        functools.partial(expert_kernel, [len(rows) for rows, _ in chunks]),
        "expert",
        [
            shape((ROWS, FULL), BF16),
            shape((ROWS, 2 * FULL), BF16),
            shape((HALF, WIDTH), BF16),
            shape((HALF, WIDTH), BF16),
            shape((HALF, WIDTH), BF16),
            shape((TILED - HALF, WIDTH), BF16),
        ]
        * len(chunks),
        [a for rows, grads in chunks for a in (*rows, grads)] + weights,
    )
    return [list(results[6 * i : 6 * i + 6]) for i in range(len(chunks))]


def join_kernel(
    own_top, own_end, near_top, near_end, left_top, far_top, right_end, far_end,
    left_out, right_out, part_top, part_end,
):
    left_out[...] = (left_top[...].astype(F32) + far_top[...].astype(F32)).astype(BF16)
    right_out[...] = (right_end[...].astype(F32) + far_end[...].astype(F32)).astype(BF16)
    part_top[...] = own_top[...].astype(F32) + near_top[...].astype(F32)
    part_end[...] = own_end[...].astype(F32) + near_end[...].astype(F32)


def join(*pieces):
    return call(
        join_kernel,
        "join",
        [shape(p.shape, t) for t, p in ((BF16, pieces[0]), (BF16, pieces[1]), (F32, pieces[0]), (F32, pieces[1]))],
        pieces,
    )


def spread_slots(rows, out_ref):
    at = iota((EXPERTS * SLOTS, ROWS), 1)
    pick = iota((EXPERTS * SLOTS, ROWS), 0) == (at // CAP) * SLOTS + at % CAP
    out_ref[...] = dot(pick.astype(F32).astype(BF16), rows.astype(BF16)).astype(BF16)


def collect_kernel(part_top, part_end, got_top, got_end, out_ref):
    end = part_end[...] + got_end[...].astype(F32)
    rows = jnp.concatenate([part_top[...] + got_top[...].astype(F32), end[:HALF]], axis=0)
    spread_slots(rows, out_ref)
    line = jnp.sum(end[HALF:, :ROWS], axis=0, keepdims=True)
    mine = iota((EXPERTS, ROWS), 1) // CAP == iota((EXPERTS, ROWS), 0)
    spot = (iota((ROWS, 128), 0) % CAP == iota((ROWS, 128), 1)).astype(F32).astype(BF16)
    table = jnp.zeros((EXPERTS, 128), F32)
    for term in split_low(line):
        table = table + dot(jnp.where(mine, term.astype(F32), 0.0).astype(BF16), spot)
    out_ref[:, :128] = (out_ref[:, :128].astype(F32) + embed(table)).astype(BF16)


def collect_out_kernel(part_top, part_end, got_top, got_end, out_ref):
    top = part_top[...] + got_top[...].astype(F32)
    end = part_end[...] + got_end[...].astype(F32)
    spread_slots(jnp.concatenate([top, end], axis=0), out_ref)


def put_weight_grads(lefts, scaled, targets):
    width = 256
    for base in range(0, len(targets) * PADDED, width):
        total = jnp.zeros((width, WIDTH), F32)
        for chunk in range(4):
            at = slice(chunk * ROWS, (chunk + 1) * ROWS)
            total = total + dot(lefts[chunk][:, base : base + width], scaled[at, :], TN)
        for index, target in enumerate(targets):
            start = max(base, index * PADDED)
            stop = min(base + width, index * PADDED + HIDDEN)
            if start < stop:
                part = total[start - base : stop - base]
                to = slice(start - index * PADDED, stop - index * PADDED)
                target[to, :] = part.astype(target.dtype)


def scale_rows(part, gates, scaled, base):
    at = slice(base, base + part.shape[0])
    for cut in range(WIDTH // 128):
        lanes = slice(cut * 128, (cut + 1) * 128)
        scaled[at, lanes] = (part[:, lanes].astype(F32) * gates).astype(BF16)


def pair_grad_kernel(*refs):
    rights, lefts = refs[:5], refs[5:9]
    own_ref, low_ref, gates_ref, scaled = refs[9:]
    same = iota((ROWS, ROWS), 0) == iota((ROWS, ROWS), 1)
    ones = jnp.ones((ROWS, 128), BF16)
    for chunk in range(4):
        base = chunk * ROWS
        tile = rights[chunk][ROWS:, :ROWS] if chunk < 3 else rights[4][HALF:, :ROWS]
        gates = jnp.zeros((ROWS, 128), F32)
        for term in range(2):
            line = tile[term : term + 1, :].astype(F32)
            gates = gates + dot(jnp.where(same, line, 0.0).astype(BF16), ones)
        gates_ref[base : base + ROWS, :] = gates
        if chunk < 3:
            scale_rows(rights[chunk][:ROWS, :], gates, scaled, base)
        else:
            scale_rows(rights[3][...], gates[:HALF], scaled, base)
            scale_rows(rights[4][:HALF, :], gates[HALF:], scaled, base + HALF)
    put_weight_grads(lefts, scaled, [own_ref.at[0], own_ref.at[1], low_ref.at[0], low_ref.at[1]])


def down_grad_kernel(*refs):
    rights, lefts = refs[:4], refs[4:8]
    gates_ref, own_ref, low_ref, scaled = refs[8:]
    for chunk in range(4):
        at = slice(chunk * ROWS, (chunk + 1) * ROWS)
        scale_rows(rights[chunk][...], gates_ref[at, :], scaled, chunk * ROWS)
    put_weight_grads(lefts, scaled, [own_ref.at[0], low_ref.at[0]])


def assemble_kernel(core_ref, pair_ref, pair_got_ref, down_ref, down_got_ref, pair_out, down_out):
    core = core_ref[0]
    pair_out[core] = pair_ref[...]
    pair_out[1 - core] = pair_got_ref[...].astype(F32)
    down_out[core] = down_ref[0]
    down_out[1 - core] = down_got_ref[0].astype(F32)


def halves_kernel(core_ref, pair_ref, down_ref, *outs):
    for which in range(2):
        expert = core_ref[which]
        pair_out, down_out = outs[2 * which : 2 * which + 2]
        zeros = jnp.zeros((PADDED - HIDDEN, WIDTH), BF16)
        for part in range(2):
            base = part * PADDED
            pair_out[base : base + HIDDEN, :] = pair_ref[expert, part].astype(BF16)
            pair_out[base + HIDDEN : base + PADDED, :] = zeros
        down_out[:HIDDEN, :] = down_ref[expert].astype(BF16)
        down_out[HIDDEN:, :] = zeros


def outer_sent_kernel(order_ref, heads_ref, low_ref, out_ref):
    for step in range(4):
        out_ref[step] = dot(heads_ref[order_ref[4 + step]], low_ref[...], TN).astype(BF16)


def outer_kept_kernel(order_ref, heads_ref, low_ref, got_ref, logit_ref, middle_ref, gain_ref, router_ref, *outs):
    for step, out in enumerate(outs):
        own = dot(heads_ref[order_ref[step]], low_ref[...], TN)
        out[...] = (own + got_ref[step].astype(F32)).astype(BF16)
    middle = middle_ref[...]
    scale = lax.rsqrt(jnp.mean(middle * middle, axis=-1, keepdims=True) + EPSILON)
    router_ref[...] = dot(logit_ref[...], middle * scale * gain_ref[...], TN, HIGHEST)


def projection_kernel(grads_ref, normed_ref, proj_ref, gain_ref, *refs):
    parts, (out_ref, gain_grad_ref) = refs[:4], refs[4:]
    total = dot(grads_ref[...], normed_ref[...], TN)
    out_ref[:384, :] = total.astype(BF16)
    gain_grad_ref[...] = jnp.sum(total * proj_ref[...].astype(F32), axis=0, keepdims=True) / gain_ref[...]
    out_ref[384:, :] = sum(p[...].astype(F32) for p in parts).astype(BF16)


def sent_kernel(order_ref, grads_ref, proj_ref, out_ref):
    for step in range(4):
        at = pl.ds(pl.multiple_of(order_ref[4 + step] * TOK, TOK), TOK)
        out_ref[step] = dot(grads_ref[at, :], proj_ref[...]).astype(BF16)


def kept_kernel(order_ref, grads_ref, proj_ref, got_ref, *outs):
    for step, out in enumerate(outs):
        at = pl.ds(pl.multiple_of(order_ref[step] * TOK, TOK), TOK)
        out[...] = (dot(grads_ref[at, :], proj_ref[...]) + got_ref[step].astype(F32)).astype(BF16)


def input_grad_kernel(own_ref, left_ref, right_ref, over_ref, tok_ref, gain_ref, middle_ref, out_ref):
    total = (own_ref[...].astype(F32) + left_ref[...].astype(F32)) + (
        right_ref[...].astype(F32) + over_ref[...].astype(F32)
    )
    inputs = tok_ref[...].astype(F32)
    scale = lax.rsqrt(jnp.mean(inputs * inputs, axis=-1, keepdims=True) + EPSILON)
    unit = inputs * scale
    weighted = total * gain_ref[...]
    out_ref[...] = middle_ref[...] + scale * (
        weighted - unit * jnp.mean(weighted * unit, axis=-1, keepdims=True)
    )


def share_kernel(parts_ref, out_ref):
    total = parts_ref[0].astype(F32)
    for index in range(1, 16):
        total = total + parts_ref[index].astype(F32)
    total = total.astype(BF16)
    for index in range(16):
        out_ref[index] = total


def finish_kernel(rows_ref, qkv_ref, out_ref):
    for c in range(3):
        for block in range(WIDTH // 128):
            cut = slice(block * 128, (block + 1) * 128)
            qkv_ref[c, cut, :] = rows_ref[c * 128 : (c + 1) * 128, cut].astype(F32).T
    out_ref[...] = rows_ref[384:512, :].astype(F32)


def on_device(
    tokens,
    layer_cotangent,
    attn_gain,
    qkv_weight,
    out_weight,
    rel_bias,
    moe_gain,
    router_weight,
    expert_in,
    expert_out,
    routes,
    buckets,
):
    narrow = lax.axis_index("narrow")
    core = lax.rem(narrow, 2)
    x = lax.div(narrow, 2)

    barrier = lax.optimization_barrier

    def shift(value, step):
        return lax.ppermute(value, "narrow", [(i, (i + 2 * step) % 8) for i in range(8)])

    def swap(value):
        return lax.ppermute(value, "narrow", [(i, i ^ 1) for i in range(8)])

    def flip(value, axis, mask):
        size = lax.axis_size(axis)
        return lax.ppermute(value, axis, [(i, i ^ mask) for i in range(size)])

    def sum_four(value, axis, unit):
        low = barrier(value.astype(BF16))
        parts = [low] + [flip(low, axis, mask * unit) for mask in (1, 2, 3)]
        parts = [p.astype(F32) for p in parts]
        return (parts[0] + parts[1]) + (parts[2] + parts[3])

    exchange_groups = [
        [w * 8 + chip * 2 + c for w in range(16) for c in range(2)] for chip in range(4)
    ]

    def exchange(value):
        return lax.all_to_all(
            value, ("wide", "narrow"), 0, 0, tiled=True, axis_index_groups=exchange_groups
        )

    def blocks(send):
        return exchange(send.reshape(EXPERTS, SLOTS, WIDTH)).reshape(EXPERTS * SLOTS, WIDTH)

    picks, place, cot_rows = call(
        spread_kernel,
        "spread",
        [
            shape((EXPERTS * SLOTS, TOK), BF16),
            shape((TOK, TOP), jnp.int32),
            shape((EXPERTS * SLOTS, WIDTH), BF16),
        ],
        [routes.T, routes, layer_cotangent],
    )
    cot_arrived = blocks(cot_rows)

    def everywhere(value):
        near = [value, shift(value, 1), shift(value, -1), shift(value, 2)]
        return near + [swap(v) for v in near]

    shards = everywhere(tokens)

    chips = [x, lax.rem(x + 3, 4), lax.rem(x + 1, 4), lax.rem(x + 2, 4)]
    order = jnp.stack([2 * c + core for c in chips] + [2 * c + (1 - core) for c in chips])
    order = order.astype(jnp.int32)
    bias = rel_bias.astype(BF16).astype(F32)
    offsets = jnp.pad(buckets, (0, 1), constant_values=-1)[None]
    backward_offsets = jnp.pad(buckets[::-1], (0, 1), constant_values=-1)[None]
    gain_one = attn_gain[None]
    gain_two = moe_gain[None]
    router_rows = router_weight.T
    wout_low, shards = barrier((out_weight.astype(BF16), shards))
    wouts = [wout_low, shift(wout_low, 1), shift(wout_low, -1), shift(wout_low, 2)]
    normed, qkv, attended, logs, proj = attend_forward(
        order, bias, shards, gain_one, qkv_weight, offsets
    )
    attended, cot_arrived, wouts = barrier((attended, cot_arrived, wouts))
    wouts = wouts + [swap(w) for w in wouts]
    heads = lax.all_to_all(attended.reshape(8, TOK, 128), "narrow", 0, 0, tiled=True)
    cot_own = unpack(cot_arrived, False)
    cot_own, expert_in, expert_out = barrier((cot_own, expert_in, expert_out))

    pair, down, pair_other, down_other = call(
        halves_kernel,
        "halves",
        [shape((FULL, WIDTH), BF16), shape((PADDED, WIDTH), BF16)] * 2,
        [
            jnp.stack([core, 1 - core]).astype(jnp.int32),
            jnp.swapaxes(expert_in, 2, 3),
            expert_out,
        ],
        smem=1,
    )
    heads, pair, down, pair_other, down_other, cot_own = barrier(
        (heads, pair, down, pair_other, down_other, cot_own)
    )
    cot_parts = [cot_own, shift(cot_own, 1), shift(cot_own, -1), shift(cot_own, 2)]
    weights = [pair, swap(pair_other), down, swap(down_other)]
    middle, gates, send_rows, wout = call(
        dispatch_kernel,
        "dispatch",
        [
            shape((TOK, WIDTH), F32),
            shape((TOK, TOP), F32),
            shape((EXPERTS * SLOTS, WIDTH), BF16),
            shape((WIDTH, WIDTH), BF16),
        ],
        [order, heads, *wouts, tokens, gain_two, router_rows, routes, place, picks],
        smem=1,
    )

    arrived = blocks(send_rows)
    place, cot_parts = barrier((place, cot_parts))
    token_picks = call(
        slots_kernel,
        "slots",
        [shape((TOP, TOK, EXPERTS * SLOTS), BF16)],
        [routes, place],
    )[0]
    arrived, token_picks = barrier((arrived, token_picks))

    row_own = unpack(arrived, True)
    row_left, row_right = shift(row_own, 1), shift(row_own, -1)
    results = run_expert([([row_own], cot_parts[0])], weights)
    row_left, row_right, results = barrier((row_left, row_right, results))
    over = [shift(row_left[:HALF], 1), shift(row_right[HALF:], -1)]
    row_parts = [row_own, row_left, row_right]
    results += run_expert([([row_left], cot_parts[1]), ([row_right], cot_parts[2])], weights)
    over, results = barrier((over, results))
    row_parts = row_parts + over
    results += run_expert([(over, cot_parts[3])], weights)
    mids, inners = ([r[i] for r in results] for i in range(2))
    outs, backs = [r[2:4] for r in results], [r[4:6] for r in results]

    def leave_far(over):
        return [shift(over[0], -1), shift(over[1], 1)]

    def leave_near(left, right):
        return [shift(right[0], 1), shift(left[1], -1)]

    def land(own, left, right, near, far):
        left_top, right_end, part_top, part_end = join(*own, *near, left[0], far[0], right[1], far[1])
        return [part_top, part_end, left_top, right_end]

    def arrive(parts):
        return [parts[0], parts[1], shift(parts[2], -1), shift(parts[3], 1)]

    far, near = leave_far(backs[3]), leave_near(*backs[1:3])
    pair_part, pair_low, gate_columns = call(
        pair_grad_kernel,
        "pair_grad",
        [
            shape((2, HIDDEN, WIDTH), F32),
            shape((2, HIDDEN, WIDTH), BF16),
            shape((4 * ROWS, 128), F32),
        ],
        [*row_parts, *inners],
        [pltpu.VMEM((4 * ROWS, WIDTH), BF16)],
    )
    far, near, pair_part, pair_low = barrier((far, near, pair_part, pair_low))
    pieces, outs, mids = barrier((arrive(land(*backs[:3], near, far)), outs, mids))
    out_far, out_near = leave_far(outs[3]), leave_near(*outs[1:3])
    back = call(collect_kernel, "collect", [shape((EXPERTS * SLOTS, WIDTH), BF16)], pieces)[0]
    row_grads = blocks(back)
    mids, out_far, out_near, _ = barrier((mids, out_far, out_near, back))
    out_parts = arrive(land(*outs[:3], out_near, out_far))
    down_part, down_low = call(
        down_grad_kernel,
        "down_grad",
        [shape((1, HIDDEN, WIDTH), F32), shape((1, HIDDEN, WIDTH), BF16)],
        [*cot_parts, *mids, gate_columns],
        [pltpu.VMEM((4 * ROWS, WIDTH), BF16)],
    )
    row_grads, down_part = barrier((row_grads, down_part))
    middle_grad, middle_low, send_heads, moe_gain_grad, logit_grads = call(
        middle_grad_kernel,
        "middle_grad",
        [
            shape((TOK, WIDTH), F32),
            shape((TOK, WIDTH), BF16),
            shape((8, TOK, 128), BF16),
            shape((1, WIDTH), F32),
            shape((TOK, EXPERTS), F32),
        ],
        [
            row_grads, gates, middle, layer_cotangent, routes, place, token_picks, gain_two,
            router_rows, wout,
        ],
    )
    head_grads = lax.all_to_all(send_heads, "narrow", 0, 0, tiled=True).reshape(LEN, 128)
    middle_low, out_parts = barrier((middle_low, out_parts))
    outer_sent = call(
        outer_sent_kernel,
        "outer_sent",
        [shape((4, 128, WIDTH), BF16)],
        [order, heads, middle_low],
        smem=1,
    )[0]
    back_out = call(collect_out_kernel, "collect_out", [shape((EXPERTS * SLOTS, WIDTH), BF16)], out_parts)[0]
    outer_got, head_grads, back_out = barrier((swap(outer_sent), head_grads, back_out))
    router_terms, *outer_parts = call(
        outer_kept_kernel,
        "outer_kept",
        [shape((EXPERTS, WIDTH), F32)] + [shape((128, WIDTH), BF16)] * 4,
        [order, heads, middle_low, outer_got, logit_grads, middle, gain_two],
        smem=1,
    )
    head_grads, back_out, outer_parts = barrier((head_grads, back_out, outer_parts))
    returned = blocks(back_out)

    def to_chips(parts):
        return [parts[0]] + [shift(p, step) for p, step in zip(parts[1:], (-1, 1, 2))]

    outer_parts = to_chips(outer_parts)
    projected_grads, bias_grad = attend_backward(
        bias, qkv, attended, head_grads, logs, backward_offsets
    )
    projected_grads, bias_grad, returned, outer_parts = barrier(
        (projected_grads, bias_grad, returned, outer_parts)
    )

    weight_grads, gain_grad = call(
        projection_kernel,
        "projection_grad",
        [shape((512, WIDTH), BF16), shape((1, WIDTH), F32)],
        [projected_grads, normed, proj, gain_one, *outer_parts],
    )
    arrived_grads = lax.all_to_all(weight_grads.reshape(16, 32, WIDTH), "wide", 0, 0, tiled=True)
    projected_grads, gain_grad, _ = barrier((projected_grads, gain_grad, weight_grads))

    small = sum_four(jnp.concatenate([router_terms, gain_grad, moe_gain_grad]), "narrow", 2)
    sent = call(
        sent_kernel, "sent", [shape((4, TOK, WIDTH), BF16)], [order, projected_grads, proj], smem=1
    )[0]
    got, small, returned = barrier((swap(sent), small, returned))
    kept = call(
        kept_kernel,
        "kept",
        [shape((TOK, WIDTH), BF16)] * 4,
        [order, projected_grads, proj, got],
        smem=1,
    )
    layer_out = call(
        combine_kernel,
        "combine",
        [shape((TOK, WIDTH), BF16)],
        [returned, middle, gates, token_picks],
    )[0]
    low = barrier(small.astype(BF16))
    small = low.astype(F32) + flip(low, "narrow", 1).astype(F32)
    small = jnp.concatenate(
        [small, jnp.pad(bias_grad.reshape(1, 64), ((0, 0), (0, WIDTH - 64)))]
    )
    arrived_grads, kept, layer_out = barrier((arrived_grads, kept, layer_out))
    copies = call(
        share_kernel, "share", [shape((16, 32, WIDTH), BF16)], [arrived_grads]
    )[0]
    gathered = lax.all_to_all(copies, "wide", 0, 0, tiled=True).reshape(512, WIDTH)
    small = sum_four(small, "wide", 1)
    pair_part, small, _ = barrier((pair_part, small, copies))
    pair_grads, down_grads = call(
        assemble_kernel,
        "assemble",
        [shape((2, 2, HIDDEN, WIDTH), F32), shape((2, HIDDEN, WIDTH), F32)],
        [core.astype(jnp.int32).reshape(1), pair_part, swap(pair_low), down_part, swap(down_low)],
        smem=1,
    )
    chip_parts = to_chips(kept)
    small, chip_parts, pair_grads, down_grads = barrier((small, chip_parts, pair_grads, down_grads))
    small = sum_four(small, "wide", 4)
    rel_bias_grad = small[EXPERTS + 2, : 2 * BUCKETS].reshape(2, BUCKETS)
    input_grad = call(
        input_grad_kernel,
        "input_grad",
        [shape((TOK, WIDTH), F32)],
        [*chip_parts, tokens, gain_one, middle_grad],
    )[0]
    qkv_weight_grad, out_weight_grad = call(
        finish_kernel,
        "finish",
        [shape((3, WIDTH, 128), F32), shape((128, WIDTH), F32)],
        [gathered],
    )
    return (
        layer_out,
        input_grad,
        small[EXPERTS],
        qkv_weight_grad,
        out_weight_grad,
        rel_bias_grad,
        small[EXPERTS + 1],
        small[:EXPERTS].T,
        jnp.swapaxes(pair_grads, 2, 3),
        down_grads,
    )


def solution(mesh):
    placed = (
        P(("wide", "narrow"), None),
        P(("wide", "narrow"), None),
        P(),
        P(None, None, "narrow"),
        P("narrow", None),
        P("narrow", None),
        P(),
        P(),
        P("wide", None, None, "narrow"),
        P("wide", "narrow", None),
        P(("wide", "narrow"), None),
        P(),
    )
    return jax.shard_map(
        on_device,
        mesh=mesh,
        in_specs=placed,
        out_specs=(
            P(("wide", "narrow"), None),
            P(("wide", "narrow"), None),
            P(),
            P(None, None, "narrow"),
            P("narrow", None),
            P("narrow", None),
            P(),
            P(),
            P("wide", None, None, "narrow"),
            P("wide", "narrow", None),
        ),
        check_vma=False,
    )
```

```python
import functools
import math

import jax
import jax.numpy as jnp
from jax import lax
from jax.experimental import pallas as pl
from jax.experimental.pallas import tpu as pltpu
from jax.sharding import PartitionSpec as P

HEAD_DIM = 64
EXPERTS = 32
BUCKETS = 32
TOP = 2
LEN = 1408
WIDTH = 1024
TOK = 176
CAP = 13
SLOTS = 16
EPSILON = 1e-06
BLOCK = 128
SPAN = 2816
LOG2E = math.log2(math.e)
SCORE = LOG2E / 8
HIGHEST = lax.Precision.HIGHEST
F32 = jnp.float32
BF16 = jnp.bfloat16
NT = (((1,), (1,)), ((), ()))
TN = (((0,), (0,)), ((), ()))
VMEM = pl.BlockSpec(memory_space=pltpu.VMEM)
SMEM = pl.BlockSpec(memory_space=pltpu.SMEM)
HBM = pl.BlockSpec(memory_space=pl.ANY)
HIDDEN = 352
PADDED = 384
FULL = 2 * PADDED
ROWS = 416
HALF = 208
TILED = 432


def shape(dims, dtype):
    return jax.ShapeDtypeStruct(dims, dtype)


COSTS = {
    "dispatch": 50,
    "slots": 50,
    "collect": 50,
    "down_grad": 50,
    "halves": 50,
    "attend_forward": 4,
    "attend_backward": 50,
    "assemble_down": 50,
    "expert": 50,
    "pair_grad": 3,
    "share": 50,
}


MEBIBYTES = {
    "attend_forward": 30,
    "attend_backward": 56,
    "dispatch": 56,
    "halves": 56,
    "expert": 40,
    "middle_grad": 56,
    "down_grad": 56,
    "assemble_pair": 56,
    "assemble_down": 56,
}


def call(kernel, name, out_shape, ins, scratch=(), smem=0, hbm=0):
    outs = tuple(out_shape)
    return pl.pallas_call(
        kernel,
        out_shape=outs,
        in_specs=[SMEM] * smem + [HBM] * hbm + [VMEM] * (len(ins) - smem - hbm),
        out_specs=tuple([VMEM] * len(outs)),
        scratch_shapes=list(scratch),
        compiler_params=pltpu.CompilerParams(vmem_limit_bytes=MEBIBYTES.get(name, 24) << 20),
        cost_estimate=pl.CostEstimate(
            flops=int(COSTS.get(name, 0.1) * 1.15e9), bytes_accessed=0, transcendentals=0
        ),
        name=name,
    )(*ins)


def dot(a, b, dims=None, precision=None):
    if dims is None:
        dims = (((1,), (0,)), ((), ()))
    return lax.dot_general(a, b, dims, precision=precision, preferred_element_type=F32)


def block_of(i):
    return pl.ds(pl.multiple_of(i * BLOCK, BLOCK), BLOCK)


def offset_row(buckets, bias_ref, head):
    total = jnp.zeros(buckets.shape, F32)
    for bucket in range(BUCKETS):
        total = jnp.where(buckets == bucket, bias_ref[head, bucket], total)
    return total


def skew(row):
    return pltpu.roll(
        jnp.broadcast_to(row, (BLOCK, SPAN)), SPAN - (BLOCK - 1), 1, stride=1, stride_axis=0
    )


def spread_terms(value):
    lane = iota(value.shape, 1) % HEAD_DIM
    high = value.astype(BF16).astype(F32)
    rest = value - high
    middle = rest.astype(BF16).astype(F32)
    terms = jnp.where(lane == 0, high, jnp.where(lane == 1, middle, rest - middle))
    return jnp.where(lane < 3, terms, 0.0).astype(BF16)


def by_head(value, low):
    zero = jnp.zeros_like(value)
    return jnp.concatenate([jnp.where(low, value, zero), jnp.where(low, zero, value)], axis=0)


def attend_forward_kernel(place_ref, bias_ref, *refs):
    shards = refs[:8]
    (gain_ref, w_ref, buckets_ref, h_ref, qkv_ref, o_ref, proj_ref,
     band, value_parts) = refs[8:]
    count = LEN // BLOCK
    for head in range(2):
        band[head * BLOCK : (head + 1) * BLOCK, :] = skew(
            offset_row(buckets_ref[...], bias_ref, head) * LOG2E
        )
    weights = jnp.concatenate([w_ref[c].astype(BF16) for c in range(3)], axis=1)
    value_parts[:, 128:] = jnp.ones((LEN, 128), BF16)
    for index, shard in enumerate(shards):
        rows = pl.ds(pl.multiple_of(place_ref[index] * TOK, TOK), TOK)
        x = shard[...].astype(F32)
        scale = lax.rsqrt(jnp.mean(x * x, axis=-1, keepdims=True) + EPSILON)
        normed = (x * scale * gain_ref[...]).astype(BF16)
        h_ref[rows, :] = normed
        projected = dot(normed, weights).astype(BF16)
        qkv_ref[rows, :128] = (projected[:, :128].astype(F32) * SCORE).astype(BF16)
        qkv_ref[rows, 256:] = projected[:, 128:]
        value_parts[rows, :128] = projected[:, 256:]
    for c in range(3):
        proj_ref[c * 128 : (c + 1) * 128, :] = w_ref[c].T.astype(BF16)
    low = iota((BLOCK, 128), 1) < HEAD_DIM

    def attend(i, carry):
        rows = block_of(i)
        window = pl.ds(pl.multiple_of((count - 1 - i) * BLOCK, BLOCK), LEN)
        query = by_head(qkv_ref[rows, :128], low)
        scores = dot(query, qkv_ref[:, 256:384], NT) + band[:, window]
        peaks = jnp.max(scores, axis=-1, keepdims=True)
        weights = jnp.exp2(scores - peaks).astype(BF16)
        both = dot(weights, value_parts[...])
        parts = [both[:BLOCK], both[BLOCK:]]
        peaks = [peaks[:BLOCK], peaks[BLOCK:]]
        top = jnp.where(low, parts[0][:, :128], parts[1][:, :128])
        totals = jnp.where(low, parts[0][:, 128:], parts[1][:, 128:])
        o_ref[rows, :] = (top / totals).astype(BF16)
        logs = jnp.where(low, peaks[0], peaks[1]) + jnp.log2(totals)
        qkv_ref[rows, 128:256] = spread_terms(-logs)
        return carry

    lax.fori_loop(0, count, attend, 0, unroll=True)


def attend_forward(places, bias, shards, gain, weights, buckets):
    head = (LEN, 128)
    return call(
        attend_forward_kernel,
        "attend_forward",
        [
            shape((LEN, WIDTH), BF16),
            shape((LEN, 512), BF16),
            shape(head, BF16),
            shape((384, WIDTH), BF16),
        ],
        [places, bias, *shards, gain, weights, buckets],
        [pltpu.VMEM((2 * BLOCK, SPAN), F32), pltpu.VMEM((LEN, 256), BF16)],
        smem=2,
    )


def attend_backward_kernel(
    order_ref, bias_ref, normed_hbm, qkv_ref, o_ref, do_ref, buckets_ref, proj_ref, gain_ref,
    bias_grad_ref, weight_ref, gain_grad_ref, sent_ref, kept_ref,
    band, band_grad, query_grad, outs, low_grads, normed, sem,
):
    fetch = pltpu.make_async_copy(normed_hbm, normed, sem)
    fetch.start()
    count = LEN // BLOCK
    for head in range(2):
        band[head * BLOCK : (head + 1) * BLOCK, :] = skew(
            offset_row(buckets_ref[...], bias_ref, head) * LOG2E
        )
    band_grad[...] = jnp.zeros_like(band_grad)
    query_grad[...] = jnp.zeros_like(query_grad)
    low = iota((BLOCK, 128), 1) < HEAD_DIM

    def prepare(i, carry):
        rows = block_of(i)
        grads = do_ref[rows, :]
        products = grads.astype(F32) * o_ref[rows, :].astype(F32)
        one = jnp.sum(jnp.where(low, products, 0.0), axis=1, keepdims=True)
        two = jnp.sum(jnp.where(low, 0.0, products), axis=1, keepdims=True)
        low_grads[rows, :128] = grads
        low_grads[rows, 128:] = spread_terms(-jnp.where(low, one, two))
        return carry

    lax.fori_loop(0, count, prepare, 0)
    lane = iota((2 * BLOCK, 128), 1) - HEAD_DIM * (iota((2 * BLOCK, 128), 0) // BLOCK)
    terms = ((lane >= 0) & (lane < 3)).astype(F32).astype(BF16)

    def step(j, carry):
        rows = block_of(j)
        window = pl.ds(pl.multiple_of((count - 1 - j) * BLOCK, BLOCK), LEN)
        keys = by_head(qkv_ref[rows, 256:384], low)
        values = by_head(qkv_ref[rows, 384:], low)
        scores = dot(jnp.concatenate([keys, terms], axis=1), qkv_ref[:, :256], NT)
        probs = jnp.exp2(scores + band[:, window])
        score_grads = probs * dot(jnp.concatenate([values, terms], axis=1), low_grads[...], NT)
        band_grad[:, window] += score_grads
        score_low = score_grads.astype(BF16)
        value_grad = dot(probs.astype(BF16), low_grads[:, :128])
        key_grad = dot(score_low, qkv_ref[:, :128])
        query_grad[...] += dot(keys, score_low, TN)
        key_grad = jnp.where(low, key_grad[:BLOCK], key_grad[BLOCK:])
        outs[rows, 128:256] = (key_grad * (1.0 / LOG2E)).astype(BF16)
        outs[rows, 256:384] = jnp.where(low, value_grad[:BLOCK], value_grad[BLOCK:]).astype(BF16)
        return carry

    lax.fori_loop(0, count, step, 0, unroll=True)

    def turn(j, carry):
        rows = block_of(j)
        outs[rows, 0:128] = (query_grad[:, rows].T * 0.125).astype(BF16)
        return carry

    lax.fori_loop(0, count, turn, 0)
    for step, ref in enumerate([kept_ref] * 4 + [sent_ref] * 4):
        at = pl.ds(pl.multiple_of(order_ref[step] * TOK, TOK), TOK)
        ref[step % 4] = dot(outs[at, :], proj_ref[...]).astype(BF16)
    fetch.wait()
    total = dot(outs[...], normed[...], TN)
    weight_ref[:384, :] = total.astype(BF16)
    gain_grad_ref[...] = jnp.sum(total * proj_ref[...].astype(F32), axis=0, keepdims=True) / gain_ref[...]
    hot = buckets_ref[...] == iota((BUCKETS, SPAN), 0)
    for head in range(2):
        total = jnp.zeros((8, SPAN), F32)
        for group in range(BLOCK // 8):
            total = total + pltpu.roll(
                band_grad[head * BLOCK + group * 8 : head * BLOCK + (group + 1) * 8, :],
                (BLOCK - 1 - 8 * group) % SPAN,
                1,
            )
        row = jnp.zeros((1, SPAN), F32)
        for part in range(8):
            row = row + pltpu.roll(total, (SPAN - part) % SPAN, 1)[part : part + 1]
        by_bucket = jnp.sum(jnp.where(hot, row, 0.0), axis=1, keepdims=True)
        bias_grad_ref[head : head + 1, :] = jnp.broadcast_to(by_bucket, (BUCKETS, 128)).T[0:1]


def attend_backward(order, bias, normed, qkv, o, head_grads, buckets, proj, gain):
    return call(
        attend_backward_kernel,
        "attend_backward",
        [
            shape((2, BUCKETS), F32),
            shape((512, WIDTH), BF16),
            shape((1, WIDTH), F32),
            shape((4, TOK, WIDTH), BF16),
            shape((4, TOK, WIDTH), BF16),
        ],
        [order, bias, normed, qkv, o, head_grads, buckets, proj, gain],
        [
            pltpu.VMEM((2 * BLOCK, SPAN), F32),
            pltpu.VMEM((2 * BLOCK, SPAN), F32),
            pltpu.VMEM((128, LEN), F32),
            pltpu.VMEM((LEN, 384), BF16),
            pltpu.VMEM((LEN, 256), BF16),
            pltpu.VMEM((LEN, WIDTH), BF16),
            pltpu.SemaphoreType.DMA(()),
        ],
        smem=2,
        hbm=1,
    )


def iota(dims, axis):
    return lax.broadcasted_iota(jnp.int32, dims, axis)


def spread_kernel(turned_ref, routes_ref, cot_ref, picks_ref, place_ref, grads_ref):
    down = iota((EXPERTS, TOK), 0)
    before = (iota((TOK, TOK), 0) < iota((TOK, TOK), 1)).astype(BF16)
    named = [turned_ref[c : c + 1, :] == down for c in range(TOP)]
    earlier = [dot(n.astype(BF16), before) for n in named]
    earlier[1] = earlier[1] + jnp.sum(named[0].astype(F32), axis=1, keepdims=True)
    cells = iota((EXPERTS * SLOTS, TOK), 0)
    picks = jnp.zeros((EXPERTS * SLOTS, TOK), F32)
    for c in range(TOP):
        place = jnp.sum(jnp.where(named[c], earlier[c], 0.0), axis=0, keepdims=True).astype(jnp.int32)
        slot = jnp.where(place < CAP, turned_ref[c : c + 1, :] * SLOTS + place, -1)
        picks = picks + (cells == slot).astype(F32)
    picks = picks.astype(BF16)
    picks_ref[...] = picks
    grads_ref[...] = dot(picks, cot_ref[...]).astype(BF16)
    across = iota((TOK, EXPERTS), 1)
    after = (iota((TOK, TOK), 1) < iota((TOK, TOK), 0)).astype(BF16)
    named = [routes_ref[:, c : c + 1] == across for c in range(TOP)]
    earlier = [dot(after, n.astype(BF16)) for n in named]
    earlier[1] = earlier[1] + jnp.sum(named[0].astype(F32), axis=0, keepdims=True)
    for c in range(TOP):
        place = jnp.sum(jnp.where(named[c], earlier[c], 0.0), axis=1, keepdims=True)
        place_ref[:, c : c + 1] = place.astype(jnp.int32)


def split_low(value):
    high = value.astype(BF16)
    return high, (value - high.astype(F32)).astype(BF16)


def embed(values):
    rows = iota((EXPERTS * SLOTS, EXPERTS), 0)
    first = iota((EXPERTS * SLOTS, EXPERTS), 1) * SLOTS + CAP
    high, low = split_low(values)
    return dot((rows == first).astype(BF16), high) + dot((rows == first + 1).astype(BF16), low)


def dispatch_kernel(order_ref, heads_ref, *refs):
    wouts = refs[:8]
    (tok_ref, gain_ref, router_ref, routes_ref, place_ref, picks_ref,
     middle_ref, gates_ref, rows_ref, all_ref) = refs[8:]
    for index, part in enumerate(wouts):
        at = pl.ds(pl.multiple_of(order_ref[index] * 128, 128), 128)
        all_ref[at, :] = part[...]
    heads = jnp.concatenate([heads_ref[n] for n in range(8)], axis=1)
    middle = tok_ref[...].astype(F32) + dot(heads, all_ref[...])
    middle_ref[...] = middle
    scale = lax.rsqrt(jnp.mean(middle * middle, axis=-1, keepdims=True) + EPSILON)
    normed = middle * scale * gain_ref[...]
    rows_ref[...] = dot(picks_ref[...], normed.astype(BF16)).astype(BF16)
    logits = dot(normed, router_ref[...], NT, HIGHEST)
    across = iota((TOK, EXPERTS), 1)
    named = [routes_ref[:, c : c + 1] == across for c in range(TOP)]
    picked = [jnp.sum(jnp.where(n, logits, 0.0), axis=1, keepdims=True) for n in named]
    peak = jnp.maximum(picked[0], picked[1])
    powers = [jnp.exp(p - peak) for p in picked]
    total = powers[0] + powers[1]
    table = jnp.zeros((EXPERTS, 128), F32)
    for c in range(TOP):
        gate = powers[c] / total
        gates_ref[:, c : c + 1] = gate
        spot = (iota((TOK, 128), 1) == place_ref[:, c : c + 1]) & (place_ref[:, c : c + 1] < CAP)
        expert = named[c].astype(F32).astype(BF16)
        high, low = split_low(gate)
        for term in (high, low):
            table = table + dot(expert, jnp.where(spot, term.astype(F32), 0.0).astype(BF16), TN)
    rows_ref[:, :128] = (rows_ref[:, :128].astype(F32) + embed(table)).astype(BF16)


def slots_kernel(routes_ref, place_ref, picks_ref):
    cells = iota((TOK, EXPERTS * SLOTS), 1)
    for c in range(TOP):
        place = place_ref[:, c : c + 1]
        slot = jnp.where(place < CAP, routes_ref[:, c : c + 1] * SLOTS + place, -1)
        picks_ref[c] = (cells == slot).astype(F32).astype(BF16)


def middle_grad_kernel(
    rows_ref, gates_ref, middle_ref, cot_ref, routes_ref, place_ref, picks_ref, gain_ref, router_ref, wout_ref,
    middle_grad_ref, low_ref, heads_ref, gain_grad_ref, logit_ref,
):
    spots = iota((EXPERTS, EXPERTS * SLOTS), 1)
    first = iota((EXPERTS, EXPERTS * SLOTS), 0) * SLOTS + CAP
    packed = rows_ref[:, :128]
    table = [dot((spots == first + step).astype(BF16), packed).astype(BF16) for step in range(2)]
    across = iota((TOK, EXPERTS), 1)
    named = [routes_ref[:, c : c + 1] == across for c in range(TOP)]
    gates = [gates_ref[:, c : c + 1] for c in range(TOP)]
    gate_grads = []
    for c in range(TOP):
        expert = named[c].astype(F32).astype(BF16)
        lines = dot(expert, table[0]) + dot(expert, table[1])
        place = place_ref[:, c : c + 1]
        spot = (iota((TOK, 128), 1) == place) & (place < CAP)
        gate_grads.append(jnp.sum(jnp.where(spot, lines, 0.0), axis=1, keepdims=True))
    mean = gates[0] * gate_grads[0] + gates[1] * gate_grads[1]
    logit_grads = sum(
        jnp.where(n, g * (d - mean), 0.0) for n, g, d in zip(named, gates, gate_grads)
    )
    logit_ref[...] = logit_grads
    normed_grad = dot(logit_grads, router_ref[...], precision=HIGHEST)
    for c, gate in enumerate(gates):
        normed_grad = normed_grad + gate * dot(picks_ref[c], rows_ref[...])
    middle = middle_ref[...]
    scale = lax.rsqrt(jnp.mean(middle * middle, axis=-1, keepdims=True) + EPSILON)
    unit = middle * scale
    gain_grad_ref[...] = jnp.sum(normed_grad * unit, axis=0, keepdims=True)
    weighted = normed_grad * gain_ref[...]
    middle_grad = cot_ref[...].astype(F32) + scale * (
        weighted - unit * jnp.mean(weighted * unit, axis=-1, keepdims=True)
    )
    middle_grad_ref[...] = middle_grad
    low = middle_grad.astype(BF16)
    low_ref[...] = low
    for n in range(8):
        heads_ref[n] = dot(low, wout_ref[n * 128 : (n + 1) * 128, :], NT).astype(BF16)


def combine_kernel(rows_ref, middle_ref, gates_ref, picks_ref, layer_ref):
    layer = middle_ref[...]
    mixed = jnp.zeros_like(layer)
    for c in range(TOP):
        mixed = mixed + gates_ref[:, c : c + 1] * dot(picks_ref[c], rows_ref[...])
    layer_ref[...] = (layer + mixed).astype(BF16)


CUBIC = 0.044715
ROOT = math.sqrt(2.0 / math.pi)


def unpack_kernel(gated, blocks_ref, rows_ref):
    at = iota((ROWS, EXPERTS * SLOTS), 0)
    pick = (at // CAP) * SLOTS + at % CAP == iota((ROWS, EXPERTS * SLOTS), 1)
    rows_ref[:ROWS, :] = dot(pick.astype(F32).astype(BF16), blocks_ref[...]).astype(BF16)
    if gated:
        spots = iota((EXPERTS, EXPERTS * SLOTS), 1)
        first = iota((EXPERTS, EXPERTS * SLOTS), 0) * SLOTS + CAP
        lane = iota((128, ROWS), 1) % CAP == iota((128, ROWS), 0)
        mine = iota((EXPERTS, ROWS), 1) // CAP == iota((EXPERTS, ROWS), 0)
        rows_ref[ROWS:, :] = jnp.zeros((TILED - ROWS, WIDTH), BF16)
        terms = []
        for step in range(2):
            table = dot((spots == first + step).astype(BF16), blocks_ref[:, :128]).astype(BF16)
            spread = dot(table, lane.astype(F32).astype(BF16))
            terms.append(jnp.sum(jnp.where(mine, spread, 0.0), axis=0, keepdims=True))
        rows_ref[ROWS:, :ROWS] = stack_terms(*terms)


def stack_terms(high, low):
    step = iota((TILED - ROWS, ROWS), 0)
    return jnp.where(step == 0, high, jnp.where(step == 1, low, 0.0)).astype(BF16)


def unpack(blocks, gated):
    return call(
        functools.partial(unpack_kernel, gated),
        "unpack",
        [shape((TILED if gated else ROWS, WIDTH), BF16)],
        [blocks.reshape(EXPERTS * SLOTS, WIDTH)],
    )[0]


def expert_kernel(counts, *refs):
    groups = []
    for count in counts:
        groups.append(refs[: count + 1])
        refs = refs[count + 1 :]
    pair_ref, pair_new_ref, down_ref, down_new_ref = refs[:4]
    refs = refs[4:]
    for *rows_refs, grads_ref in groups:
        mid_ref, inner_ref, out_top_ref, out_end_ref, back_top_ref, back_end_ref = refs[:6]
        refs = refs[6:]
        if len(rows_refs) == 1:
            rows = rows_refs[0][:ROWS, :]
        else:
            rows = jnp.concatenate([rows_refs[0][...], rows_refs[1][:HALF, :]], axis=0)
        one = dot(rows, pair_ref[...], NT)
        two = dot(rows, pair_new_ref[...], NT)
        gate = jnp.concatenate([one[:, :PADDED], two[:, :PADDED]], axis=1)
        up = jnp.concatenate([one[:, PADDED:], two[:, PADDED:]], axis=1)
        down = jnp.concatenate([down_ref[...], down_new_ref[...]], axis=0)
        mid_grad = dot(grads_ref[...], down, NT)
        square = gate * gate
        turned = jnp.tanh(ROOT * gate * (1.0 + CUBIC * square))
        half = 0.5 * (1.0 + turned)
        curved = gate * half
        slope = half + 0.5 * gate * (1.0 - turned * turned) * (ROOT * (1.0 + 3.0 * CUBIC * square))
        mid = (curved * up).astype(BF16)
        mid_ref[...] = mid
        gate_grad = (mid_grad * (up * slope)).astype(BF16)
        up_grad = (mid_grad * curved).astype(BF16)
        for part in range(2):
            cut = slice(part * PADDED, (part + 1) * PADDED)
            inner_ref[:, 2 * part * PADDED : (2 * part + 1) * PADDED] = gate_grad[:, cut]
            inner_ref[:, (2 * part + 1) * PADDED : (2 * part + 2) * PADDED] = up_grad[:, cut]
        product = (mid.astype(F32) * mid_grad).astype(BF16)
        line = dot(jnp.ones((8, FULL), BF16), product, NT)[0:1]
        high, low = split_low(line)
        back_end_ref[HALF:, :] = jnp.zeros((TILED - ROWS, WIDTH), BF16)
        back_end_ref[HALF:, :ROWS] = stack_terms(high.astype(F32), low.astype(F32))
        pair = jnp.concatenate([pair_ref[...], pair_new_ref[...]], axis=0)
        back = dot(inner_ref[...], pair).astype(BF16)
        back_top_ref[...] = back[:HALF]
        back_end_ref[:HALF, :] = back[HALF:]
        out = dot(mid_ref[...], down).astype(BF16)
        out_top_ref[...] = out[:HALF]
        out_end_ref[...] = out[HALF:]


def run_expert(chunks, weights):
    results = call(
        functools.partial(expert_kernel, [len(rows) for rows, _ in chunks]),
        "expert",
        [
            shape((ROWS, FULL), BF16),
            shape((ROWS, 2 * FULL), BF16),
            shape((HALF, WIDTH), BF16),
            shape((HALF, WIDTH), BF16),
            shape((HALF, WIDTH), BF16),
            shape((TILED - HALF, WIDTH), BF16),
        ]
        * len(chunks),
        [a for rows, grads in chunks for a in (*rows, grads)] + weights,
    )
    return [list(results[6 * i : 6 * i + 6]) for i in range(len(chunks))]


def join_kernel(
    own_top, own_end, near_top, near_end, left_top, far_top, right_end, far_end,
    left_out, right_out, part_top, part_end,
):
    left_out[...] = (left_top[...].astype(F32) + far_top[...].astype(F32)).astype(BF16)
    right_out[...] = (right_end[...].astype(F32) + far_end[...].astype(F32)).astype(BF16)
    part_top[...] = own_top[...].astype(F32) + near_top[...].astype(F32)
    part_end[...] = own_end[...].astype(F32) + near_end[...].astype(F32)


def join(*pieces):
    return call(
        join_kernel,
        "join",
        [shape(p.shape, t) for t, p in ((BF16, pieces[0]), (BF16, pieces[1]), (F32, pieces[0]), (F32, pieces[1]))],
        pieces,
    )


def spread_slots(rows, out_ref):
    at = iota((EXPERTS * SLOTS, ROWS), 1)
    pick = iota((EXPERTS * SLOTS, ROWS), 0) == (at // CAP) * SLOTS + at % CAP
    out_ref[...] = dot(pick.astype(F32).astype(BF16), rows.astype(BF16)).astype(BF16)


def collect_kernel(part_top, part_end, got_top, got_end, out_ref):
    end = part_end[...] + got_end[...].astype(F32)
    rows = jnp.concatenate([part_top[...] + got_top[...].astype(F32), end[:HALF]], axis=0)
    spread_slots(rows, out_ref)
    line = jnp.sum(end[HALF:, :ROWS], axis=0, keepdims=True)
    mine = iota((EXPERTS, ROWS), 1) // CAP == iota((EXPERTS, ROWS), 0)
    spot = (iota((ROWS, 128), 0) % CAP == iota((ROWS, 128), 1)).astype(F32).astype(BF16)
    table = jnp.zeros((EXPERTS, 128), F32)
    for term in split_low(line):
        table = table + dot(jnp.where(mine, term.astype(F32), 0.0).astype(BF16), spot)
    out_ref[:, :128] = (out_ref[:, :128].astype(F32) + embed(table)).astype(BF16)


def collect_out_kernel(part_top, part_end, got_top, got_end, out_ref):
    top = part_top[...] + got_top[...].astype(F32)
    end = part_end[...] + got_end[...].astype(F32)
    spread_slots(jnp.concatenate([top, end], axis=0), out_ref)


def put_weight_grads(lefts, scaled, targets):
    width = 256
    for base in range(0, len(targets) * PADDED, width):
        total = jnp.zeros((width, WIDTH), F32)
        for chunk in range(4):
            at = slice(chunk * ROWS, (chunk + 1) * ROWS)
            total = total + dot(lefts[chunk][:, base : base + width], scaled[at, :], TN)
        for index, target in enumerate(targets):
            start = max(base, index * PADDED)
            stop = min(base + width, index * PADDED + HIDDEN)
            if start < stop:
                part = total[start - base : stop - base]
                to = slice(start - index * PADDED, stop - index * PADDED)
                target[to, :] = part.astype(target.dtype)


def scale_rows(part, gates, scaled, base):
    at = slice(base, base + part.shape[0])
    for cut in range(WIDTH // 128):
        lanes = slice(cut * 128, (cut + 1) * 128)
        scaled[at, lanes] = (part[:, lanes].astype(F32) * gates).astype(BF16)


def pair_grad_kernel(*refs):
    rights, lefts = refs[:5], refs[5:9]
    own_ref, low_ref, gates_ref, scaled = refs[9:]
    same = iota((ROWS, ROWS), 0) == iota((ROWS, ROWS), 1)
    ones = jnp.ones((ROWS, 128), BF16)
    for chunk in range(4):
        base = chunk * ROWS
        tile = rights[chunk][ROWS:, :ROWS] if chunk < 3 else rights[4][HALF:, :ROWS]
        gates = jnp.zeros((ROWS, 128), F32)
        for term in range(2):
            line = tile[term : term + 1, :].astype(F32)
            gates = gates + dot(jnp.where(same, line, 0.0).astype(BF16), ones)
        gates_ref[base : base + ROWS, :] = gates
        if chunk < 3:
            scale_rows(rights[chunk][:ROWS, :], gates, scaled, base)
        else:
            scale_rows(rights[3][...], gates[:HALF], scaled, base)
            scale_rows(rights[4][:HALF, :], gates[HALF:], scaled, base + HALF)
    put_weight_grads(lefts, scaled, [own_ref.at[0], own_ref.at[1], low_ref.at[0], low_ref.at[1]])


def down_grad_kernel(*refs):
    rights, lefts = refs[:4], refs[4:8]
    gates_ref, own_ref, low_ref, scaled = refs[8:]
    for chunk in range(4):
        at = slice(chunk * ROWS, (chunk + 1) * ROWS)
        scale_rows(rights[chunk][...], gates_ref[at, :], scaled, chunk * ROWS)
    put_weight_grads(lefts, scaled, [own_ref.at[0], low_ref.at[0]])


def assemble_kernel(core_ref, own_ref, got_ref, out_ref):
    core = core_ref[0]
    out_ref[core] = own_ref[...]
    out_ref[1 - core] = got_ref[...].astype(F32)


def halves_kernel(core_ref, pair_ref, down_ref, *outs):
    for which in range(2):
        expert = core_ref[which]
        pair_out, down_out = outs[2 * which : 2 * which + 2]
        zeros = jnp.zeros((PADDED - HIDDEN, WIDTH), BF16)
        for part in range(2):
            base = part * PADDED
            pair_out[base : base + HIDDEN, :] = pair_ref[expert, part].astype(BF16)
            pair_out[base + HIDDEN : base + PADDED, :] = zeros
        down_out[:HIDDEN, :] = down_ref[expert].astype(BF16)
        down_out[HIDDEN:, :] = zeros


def outer_sent_kernel(order_ref, heads_ref, low_ref, out_ref):
    for step in range(4):
        out_ref[step] = dot(heads_ref[order_ref[4 + step]], low_ref[...], TN).astype(BF16)


def outer_kept_kernel(order_ref, heads_ref, low_ref, got_ref, logit_ref, middle_ref, gain_ref, router_ref, *outs):
    for step, out in enumerate(outs):
        own = dot(heads_ref[order_ref[step]], low_ref[...], TN)
        out[...] = (own + got_ref[step].astype(F32)).astype(BF16)
    middle = middle_ref[...]
    scale = lax.rsqrt(jnp.mean(middle * middle, axis=-1, keepdims=True) + EPSILON)
    router_ref[...] = dot(logit_ref[...], middle * scale * gain_ref[...], TN, HIGHEST)


def fill_kernel(whole_hbm, *refs):
    parts, (out_hbm, total, sem) = refs[:4], refs[4:]
    total[...] = sum(p[...].astype(F32) for p in parts).astype(BF16)
    copy = pltpu.make_async_copy(total, out_hbm.at[384:512], sem)
    copy.start()
    copy.wait()


def fill(whole, parts):
    return pl.pallas_call(
        fill_kernel,
        out_shape=shape((512, WIDTH), BF16),
        in_specs=[HBM] + [VMEM] * 4,
        out_specs=HBM,
        scratch_shapes=[pltpu.VMEM((128, WIDTH), BF16), pltpu.SemaphoreType.DMA(())],
        input_output_aliases={0: 0},
        compiler_params=pltpu.CompilerParams(vmem_limit_bytes=24 << 20),
        cost_estimate=pl.CostEstimate(flops=100000000, bytes_accessed=0, transcendentals=0),
        name="fill",
    )(whole, *parts)


def kept_kernel(kept_ref, got_ref, *outs):
    for step, out in enumerate(outs):
        out[...] = (kept_ref[step].astype(F32) + got_ref[step].astype(F32)).astype(BF16)


def input_grad_kernel(own_ref, left_ref, right_ref, over_ref, tok_ref, gain_ref, middle_ref, out_ref):
    total = (own_ref[...].astype(F32) + left_ref[...].astype(F32)) + (
        right_ref[...].astype(F32) + over_ref[...].astype(F32)
    )
    inputs = tok_ref[...].astype(F32)
    scale = lax.rsqrt(jnp.mean(inputs * inputs, axis=-1, keepdims=True) + EPSILON)
    unit = inputs * scale
    weighted = total * gain_ref[...]
    out_ref[...] = middle_ref[...] + scale * (
        weighted - unit * jnp.mean(weighted * unit, axis=-1, keepdims=True)
    )


def share_kernel(parts_ref, out_ref):
    total = parts_ref[0].astype(F32)
    for index in range(1, 16):
        total = total + parts_ref[index].astype(F32)
    total = total.astype(BF16)
    for index in range(16):
        out_ref[index] = total


def finish_kernel(rows_ref, qkv_ref, out_ref):
    for c in range(3):
        for block in range(WIDTH // 128):
            cut = slice(block * 128, (block + 1) * 128)
            qkv_ref[c, cut, :] = rows_ref[c * 128 : (c + 1) * 128, cut].astype(F32).T
    out_ref[...] = rows_ref[384:512, :].astype(F32)


def on_device(
    tokens,
    layer_cotangent,
    attn_gain,
    qkv_weight,
    out_weight,
    rel_bias,
    moe_gain,
    router_weight,
    expert_in,
    expert_out,
    routes,
    buckets,
):
    narrow = lax.axis_index("narrow")
    core = lax.rem(narrow, 2)
    x = lax.div(narrow, 2)

    barrier = lax.optimization_barrier

    def shift(value, step):
        return lax.ppermute(value, "narrow", [(i, (i + 2 * step) % 8) for i in range(8)])

    def swap(value):
        return lax.ppermute(value, "narrow", [(i, i ^ 1) for i in range(8)])

    def flip(value, axis, mask):
        size = lax.axis_size(axis)
        return lax.ppermute(value, axis, [(i, i ^ mask) for i in range(size)])

    def sum_four(value, axis, unit):
        low = barrier(value.astype(BF16))
        parts = [low] + [flip(low, axis, mask * unit) for mask in (1, 2, 3)]
        parts = [p.astype(F32) for p in parts]
        return (parts[0] + parts[1]) + (parts[2] + parts[3])

    exchange_groups = [
        [w * 8 + chip * 2 + c for w in range(16) for c in range(2)] for chip in range(4)
    ]

    def exchange(value):
        return lax.all_to_all(
            value, ("wide", "narrow"), 0, 0, tiled=True, axis_index_groups=exchange_groups
        )

    def blocks(send):
        return exchange(send.reshape(EXPERTS, SLOTS, WIDTH)).reshape(EXPERTS * SLOTS, WIDTH)

    picks, place, cot_rows = call(
        spread_kernel,
        "spread",
        [
            shape((EXPERTS * SLOTS, TOK), BF16),
            shape((TOK, TOP), jnp.int32),
            shape((EXPERTS * SLOTS, WIDTH), BF16),
        ],
        [routes.T, routes, layer_cotangent],
    )
    cot_arrived = blocks(cot_rows)

    def everywhere(value):
        near = [value, shift(value, 1), shift(value, -1), shift(value, 2)]
        return near + [swap(v) for v in near]

    shards = everywhere(tokens)

    chips = [x, lax.rem(x + 3, 4), lax.rem(x + 1, 4), lax.rem(x + 2, 4)]
    order = jnp.stack([2 * c + core for c in chips] + [2 * c + (1 - core) for c in chips])
    order = order.astype(jnp.int32)
    bias = rel_bias.astype(BF16).astype(F32)
    offsets = jnp.pad(buckets, (0, 1), constant_values=-1)[None]
    backward_offsets = jnp.pad(buckets[::-1], (0, 1), constant_values=-1)[None]
    gain_one = attn_gain[None]
    gain_two = moe_gain[None]
    router_rows = router_weight.T
    wout_low, shards = barrier((out_weight.astype(BF16), shards))
    wouts = [wout_low, shift(wout_low, 1), shift(wout_low, -1), shift(wout_low, 2)]
    normed, qkv, attended, proj = attend_forward(
        order, bias, shards, gain_one, qkv_weight, offsets
    )
    attended, cot_arrived, wouts = barrier((attended, cot_arrived, wouts))
    wouts = wouts + [swap(w) for w in wouts]
    heads = lax.all_to_all(attended.reshape(8, TOK, 128), "narrow", 0, 0, tiled=True)
    cot_arrived, expert_in, expert_out = barrier((cot_arrived, expert_in, expert_out))

    pair, down, pair_other, down_other = call(
        halves_kernel,
        "halves",
        [shape((FULL, WIDTH), BF16), shape((PADDED, WIDTH), BF16)] * 2,
        [
            jnp.stack([core, 1 - core]).astype(jnp.int32),
            jnp.swapaxes(expert_in, 2, 3),
            expert_out,
        ],
        smem=1,
    )
    cot_arrived, pair = barrier((cot_arrived, pair))
    cot_own = unpack(cot_arrived, False)
    heads, pair, down, pair_other, down_other, cot_own = barrier(
        (heads, pair, down, pair_other, down_other, cot_own)
    )
    cot_parts = [cot_own, shift(cot_own, 1), shift(cot_own, -1), shift(cot_own, 2)]
    weights = [pair, swap(pair_other), down, swap(down_other)]
    middle, gates, send_rows, wout = call(
        dispatch_kernel,
        "dispatch",
        [
            shape((TOK, WIDTH), F32),
            shape((TOK, TOP), F32),
            shape((EXPERTS * SLOTS, WIDTH), BF16),
            shape((WIDTH, WIDTH), BF16),
        ],
        [order, heads, *wouts, tokens, gain_two, router_rows, routes, place, picks],
        smem=1,
    )

    arrived = blocks(send_rows)
    place, cot_parts = barrier((place, cot_parts))
    token_picks = call(
        slots_kernel,
        "slots",
        [shape((TOP, TOK, EXPERTS * SLOTS), BF16)],
        [routes, place],
    )[0]
    arrived, token_picks = barrier((arrived, token_picks))

    row_own = unpack(arrived, True)
    row_left, row_right = shift(row_own, 1), shift(row_own, -1)
    results = run_expert([([row_own], cot_parts[0])], weights)
    row_left, row_right, results = barrier((row_left, row_right, results))
    over = [shift(row_left[:HALF], 1), shift(row_right[HALF:], -1)]
    row_parts = [row_own, row_left, row_right]
    results += run_expert([([row_left], cot_parts[1]), ([row_right], cot_parts[2])], weights)
    over, results = barrier((over, results))
    row_parts = row_parts + over
    results += run_expert([(over, cot_parts[3])], weights)
    mids, inners = ([r[i] for r in results] for i in range(2))
    outs, backs = [r[2:4] for r in results], [r[4:6] for r in results]

    def leave_far(over):
        return [shift(over[0], -1), shift(over[1], 1)]

    def leave_near(left, right):
        return [shift(right[0], 1), shift(left[1], -1)]

    def land(own, left, right, near, far):
        left_top, right_end, part_top, part_end = join(*own, *near, left[0], far[0], right[1], far[1])
        return [part_top, part_end, left_top, right_end]

    def arrive(parts):
        return [parts[0], parts[1], shift(parts[2], -1), shift(parts[3], 1)]

    far, near = leave_far(backs[3]), leave_near(*backs[1:3])
    near, inners = barrier((near, inners))
    pair_part, pair_low, gate_columns = call(
        pair_grad_kernel,
        "pair_grad",
        [
            shape((2, HIDDEN, WIDTH), F32),
            shape((2, HIDDEN, WIDTH), BF16),
            shape((4 * ROWS, 128), F32),
        ],
        [*row_parts, *inners],
        [pltpu.VMEM((4 * ROWS, WIDTH), BF16)],
    )
    far, near, pair_part, pair_low = barrier((far, near, pair_part, pair_low))
    landed = land(*backs[:3], near, far)
    pair_part, landed = barrier((pair_part, landed))
    pair_grads = call(
        assemble_kernel,
        "assemble_pair",
        [shape((2, 2, HIDDEN, WIDTH), F32)],
        [core.astype(jnp.int32).reshape(1), pair_part, swap(pair_low)],
        smem=1,
    )[0]
    pieces, outs, mids, pair_grads = barrier((arrive(landed), outs, mids, pair_grads))
    out_far, out_near = leave_far(outs[3]), leave_near(*outs[1:3])
    back = call(collect_kernel, "collect", [shape((EXPERTS * SLOTS, WIDTH), BF16)], pieces)[0]
    row_grads = blocks(back)
    mids, out_far, out_near, _ = barrier((mids, out_far, out_near, back))
    out_parts = arrive(land(*outs[:3], out_near, out_far))
    down_part, down_low = call(
        down_grad_kernel,
        "down_grad",
        [shape((1, HIDDEN, WIDTH), F32), shape((1, HIDDEN, WIDTH), BF16)],
        [*cot_parts, *mids, gate_columns],
        [pltpu.VMEM((4 * ROWS, WIDTH), BF16)],
    )
    row_grads, down_part = barrier((row_grads, down_part))
    middle_grad, middle_low, send_heads, moe_gain_grad, logit_grads = call(
        middle_grad_kernel,
        "middle_grad",
        [
            shape((TOK, WIDTH), F32),
            shape((TOK, WIDTH), BF16),
            shape((8, TOK, 128), BF16),
            shape((1, WIDTH), F32),
            shape((TOK, EXPERTS), F32),
        ],
        [
            row_grads, gates, middle, layer_cotangent, routes, place, token_picks, gain_two,
            router_rows, wout,
        ],
    )
    head_grads = lax.all_to_all(send_heads, "narrow", 0, 0, tiled=True).reshape(LEN, 128)
    middle_low, out_parts = barrier((middle_low, out_parts))
    outer_sent = call(
        outer_sent_kernel,
        "outer_sent",
        [shape((4, 128, WIDTH), BF16)],
        [order, heads, middle_low],
        smem=1,
    )[0]
    back_out = call(collect_out_kernel, "collect_out", [shape((EXPERTS * SLOTS, WIDTH), BF16)], out_parts)[0]
    outer_got, head_grads, back_out = barrier((swap(outer_sent), head_grads, back_out))
    router_terms, *outer_parts = call(
        outer_kept_kernel,
        "outer_kept",
        [shape((EXPERTS, WIDTH), F32)] + [shape((128, WIDTH), BF16)] * 4,
        [order, heads, middle_low, outer_got, logit_grads, middle, gain_two],
        smem=1,
    )
    head_grads, back_out, outer_parts = barrier((head_grads, back_out, outer_parts))
    returned = blocks(back_out)

    def to_chips(parts):
        return [parts[0]] + [shift(p, step) for p, step in zip(parts[1:], (-1, 1, 2))]

    outer_parts = to_chips(outer_parts)
    bias_grad, weight_grads, gain_grad, sent, kept = attend_backward(
        order, bias, normed, qkv, attended, head_grads, backward_offsets, proj, gain_one
    )
    bias_grad, weight_grads, returned, outer_parts = barrier(
        (bias_grad, weight_grads, returned, outer_parts)
    )

    weight_grads = fill(weight_grads, outer_parts)
    arrived_grads = lax.all_to_all(weight_grads.reshape(16, 32, WIDTH), "wide", 0, 0, tiled=True)
    gain_grad, sent, _ = barrier((gain_grad, sent, weight_grads))

    small = sum_four(jnp.concatenate([router_terms, gain_grad, moe_gain_grad]), "narrow", 2)
    got, small, returned = barrier((swap(sent), small, returned))
    kept = call(
        kept_kernel,
        "kept",
        [shape((TOK, WIDTH), BF16)] * 4,
        [kept, got],
    )
    layer_out = call(
        combine_kernel,
        "combine",
        [shape((TOK, WIDTH), BF16)],
        [returned, middle, gates, token_picks],
    )[0]
    low = barrier(small.astype(BF16))
    small = low.astype(F32) + flip(low, "narrow", 1).astype(F32)
    small = jnp.concatenate(
        [small, jnp.pad(bias_grad.reshape(1, 64), ((0, 0), (0, WIDTH - 64)))]
    )
    arrived_grads, kept, layer_out = barrier((arrived_grads, kept, layer_out))
    copies = call(
        share_kernel, "share", [shape((16, 32, WIDTH), BF16)], [arrived_grads]
    )[0]
    gathered = lax.all_to_all(copies, "wide", 0, 0, tiled=True).reshape(512, WIDTH)
    small = sum_four(small, "wide", 1)
    chip_parts = to_chips(kept)
    down_part, small, chip_parts, _ = barrier((down_part, small, chip_parts, copies))
    down_grads = call(
        assemble_kernel,
        "assemble_down",
        [shape((2, 1, HIDDEN, WIDTH), F32)],
        [core.astype(jnp.int32).reshape(1), down_part, swap(down_low)],
        smem=1,
    )[0].reshape(2, HIDDEN, WIDTH)
    small = sum_four(small, "wide", 4)
    rel_bias_grad = small[EXPERTS + 2, : 2 * BUCKETS].reshape(2, BUCKETS)
    input_grad = call(
        input_grad_kernel,
        "input_grad",
        [shape((TOK, WIDTH), F32)],
        [*chip_parts, tokens, gain_one, middle_grad],
    )[0]
    qkv_weight_grad, out_weight_grad = call(
        finish_kernel,
        "finish",
        [shape((3, WIDTH, 128), F32), shape((128, WIDTH), F32)],
        [gathered],
    )
    return (
        layer_out,
        input_grad,
        small[EXPERTS],
        qkv_weight_grad,
        out_weight_grad,
        rel_bias_grad,
        small[EXPERTS + 1],
        small[:EXPERTS].T,
        jnp.swapaxes(pair_grads, 2, 3),
        down_grads,
    )


def solution(mesh):
    placed = (
        P(("wide", "narrow"), None),
        P(("wide", "narrow"), None),
        P(),
        P(None, None, "narrow"),
        P("narrow", None),
        P("narrow", None),
        P(),
        P(),
        P("wide", None, None, "narrow"),
        P("wide", "narrow", None),
        P(("wide", "narrow"), None),
        P(),
    )
    return jax.shard_map(
        on_device,
        mesh=mesh,
        in_specs=placed,
        out_specs=(
            P(("wide", "narrow"), None),
            P(("wide", "narrow"), None),
            P(),
            P(None, None, "narrow"),
            P("narrow", None),
            P("narrow", None),
            P(),
            P(),
            P("wide", None, None, "narrow"),
            P("wide", "narrow", None),
        ),
        check_vma=False,
    )
```

```python
import functools
import math

import jax
import jax.numpy as jnp
from jax import lax
from jax.experimental import pallas as pl
from jax.experimental.pallas import tpu as pltpu
from jax.sharding import PartitionSpec as P

HEAD_DIM = 64
EXPERTS = 32
BUCKETS = 32
TOP = 2
LEN = 1408
WIDTH = 1024
TOK = 176
CAP = 13
SLOTS = 16
EPSILON = 1e-06
BLOCK = 128
SPAN = 2816
LOG2E = math.log2(math.e)
SCORE = LOG2E / 8
HIGHEST = lax.Precision.HIGHEST
F32 = jnp.float32
BF16 = jnp.bfloat16
NT = (((1,), (1,)), ((), ()))
TN = (((0,), (0,)), ((), ()))
VMEM = pl.BlockSpec(memory_space=pltpu.VMEM)
SMEM = pl.BlockSpec(memory_space=pltpu.SMEM)
HBM = pl.BlockSpec(memory_space=pl.ANY)
HIDDEN = 352
PADDED = 384
FULL = 2 * PADDED
ROWS = 416
HALF = 208
TILED = 432


def shape(dims, dtype):
    return jax.ShapeDtypeStruct(dims, dtype)


COSTS = {
    "dispatch": 50,
    "slots": 50,
    "collect": 50,
    "down_grad": 50,
    "halves": 50,
    "attend_forward": 4,
    "attend_backward": 50,
    "assemble_down": 50,
    "expert": 50,
    "pair_grad": 3,
    "share": 50,
}


MEBIBYTES = {
    "attend_forward": 56,
    "attend_backward": 56,
    "dispatch": 56,
    "halves": 56,
    "expert": 40,
    "middle_grad": 56,
    "down_grad": 56,
    "assemble_pair": 56,
    "assemble_down": 56,
}


def call(kernel, name, out_shape, ins, scratch=(), smem=0, hbm=0):
    outs = tuple(out_shape)
    return pl.pallas_call(
        kernel,
        out_shape=outs,
        in_specs=[SMEM] * smem + [HBM] * hbm + [VMEM] * (len(ins) - smem - hbm),
        out_specs=tuple([VMEM] * len(outs)),
        scratch_shapes=list(scratch),
        compiler_params=pltpu.CompilerParams(vmem_limit_bytes=MEBIBYTES.get(name, 24) << 20),
        cost_estimate=pl.CostEstimate(
            flops=int(COSTS.get(name, 0.1) * 1.15e9), bytes_accessed=0, transcendentals=0
        ),
        name=name,
    )(*ins)


def dot(a, b, dims=None, precision=None):
    if dims is None:
        dims = (((1,), (0,)), ((), ()))
    return lax.dot_general(a, b, dims, precision=precision, preferred_element_type=F32)


def block_of(i):
    return pl.ds(pl.multiple_of(i * BLOCK, BLOCK), BLOCK)


def offset_row(buckets, bias_ref, head):
    total = jnp.zeros(buckets.shape, F32)
    for bucket in range(BUCKETS):
        total = jnp.where(buckets == bucket, bias_ref[head, bucket], total)
    return total


def skew(row):
    return pltpu.roll(
        jnp.broadcast_to(row, (BLOCK, SPAN)), SPAN - (BLOCK - 1), 1, stride=1, stride_axis=0
    )


def spread_terms(value):
    lane = iota(value.shape, 1) % HEAD_DIM
    high = value.astype(BF16).astype(F32)
    rest = value - high
    middle = rest.astype(BF16).astype(F32)
    terms = jnp.where(lane == 0, high, jnp.where(lane == 1, middle, rest - middle))
    return jnp.where(lane < 3, terms, 0.0).astype(BF16)


def by_head(value, low):
    zero = jnp.zeros_like(value)
    return jnp.concatenate([jnp.where(low, value, zero), jnp.where(low, zero, value)], axis=0)


def attend_forward_kernel(place_ref, bias_ref, *refs):
    shards = refs[:8]
    (gain_ref, w_ref, buckets_ref, h_ref, qkv_ref, o_ref, proj_ref,
     band, value_parts) = refs[8:]
    count = LEN // BLOCK
    for head in range(2):
        band[head * BLOCK : (head + 1) * BLOCK, :] = skew(
            offset_row(buckets_ref[...], bias_ref, head) * LOG2E
        )
    weights = jnp.concatenate([w_ref[c].astype(BF16) for c in range(3)], axis=1)
    value_parts[:, 128:] = jnp.ones((LEN, 128), BF16)
    for index, shard in enumerate(shards):
        rows = pl.ds(pl.multiple_of(place_ref[index] * TOK, TOK), TOK)
        x = shard[...].astype(F32)
        scale = lax.rsqrt(jnp.mean(x * x, axis=-1, keepdims=True) + EPSILON)
        normed = (x * scale * gain_ref[...]).astype(BF16)
        h_ref[rows, :] = normed
        projected = dot(normed, weights).astype(BF16)
        qkv_ref[rows, :128] = (projected[:, :128].astype(F32) * SCORE).astype(BF16)
        qkv_ref[rows, 256:] = projected[:, 128:]
        value_parts[rows, :128] = projected[:, 256:]
    for c in range(3):
        proj_ref[c * 128 : (c + 1) * 128, :] = w_ref[c].T.astype(BF16)
    low = iota((BLOCK, 128), 1) < HEAD_DIM

    def attend(i, carry):
        rows = block_of(i)
        window = pl.ds(pl.multiple_of((count - 1 - i) * BLOCK, BLOCK), LEN)
        query = by_head(qkv_ref[rows, :128], low)
        scores = dot(query, qkv_ref[:, 256:384], NT) + band[:, window]
        peaks = jnp.max(scores, axis=-1, keepdims=True)
        weights = jnp.exp2(scores - peaks).astype(BF16)
        both = dot(weights, value_parts[...])
        parts = [both[:BLOCK], both[BLOCK:]]
        peaks = [peaks[:BLOCK], peaks[BLOCK:]]
        top = jnp.where(low, parts[0][:, :128], parts[1][:, :128])
        totals = jnp.where(low, parts[0][:, 128:], parts[1][:, 128:])
        o_ref[rows, :] = (top / totals).astype(BF16)
        logs = jnp.where(low, peaks[0], peaks[1]) + jnp.log2(totals)
        qkv_ref[rows, 128:256] = spread_terms(-logs)
        return carry

    lax.fori_loop(0, count, attend, 0, unroll=True)


def attend_forward(places, bias, shards, gain, weights, buckets):
    head = (LEN, 128)
    return call(
        attend_forward_kernel,
        "attend_forward",
        [
            shape((LEN, WIDTH), BF16),
            shape((LEN, 512), BF16),
            shape(head, BF16),
            shape((384, WIDTH), BF16),
        ],
        [places, bias, *shards, gain, weights, buckets],
        [pltpu.VMEM((2 * BLOCK, SPAN), F32), pltpu.VMEM((LEN, 256), BF16)],
        smem=2,
    )


def attend_backward_kernel(
    order_ref, bias_ref, normed_hbm, qkv_ref, o_ref, do_ref, buckets_ref, proj_ref, gain_ref,
    bias_grad_ref, weight_ref, gain_grad_ref, sent_ref, kept_ref,
    band, band_grad, query_grad, outs, low_grads, normed, sem,
):
    fetch = pltpu.make_async_copy(normed_hbm, normed, sem)
    fetch.start()
    count = LEN // BLOCK
    for head in range(2):
        band[head * BLOCK : (head + 1) * BLOCK, :] = skew(
            offset_row(buckets_ref[...], bias_ref, head) * LOG2E
        )
    band_grad[...] = jnp.zeros_like(band_grad)
    query_grad[...] = jnp.zeros_like(query_grad)
    low = iota((BLOCK, 128), 1) < HEAD_DIM

    def prepare(i, carry):
        rows = block_of(i)
        grads = do_ref[rows, :]
        products = grads.astype(F32) * o_ref[rows, :].astype(F32)
        one = jnp.sum(jnp.where(low, products, 0.0), axis=1, keepdims=True)
        two = jnp.sum(jnp.where(low, 0.0, products), axis=1, keepdims=True)
        low_grads[rows, :128] = grads
        low_grads[rows, 128:] = spread_terms(-jnp.where(low, one, two))
        return carry

    lax.fori_loop(0, count, prepare, 0)
    lane = iota((2 * BLOCK, 128), 1) - HEAD_DIM * (iota((2 * BLOCK, 128), 0) // BLOCK)
    terms = ((lane >= 0) & (lane < 3)).astype(F32).astype(BF16)

    def step(j, carry):
        rows = block_of(j)
        window = pl.ds(pl.multiple_of((count - 1 - j) * BLOCK, BLOCK), LEN)
        keys = by_head(qkv_ref[rows, 256:384], low)
        values = by_head(qkv_ref[rows, 384:], low)
        scores = dot(jnp.concatenate([keys, terms], axis=1), qkv_ref[:, :256], NT)
        probs = jnp.exp2(scores + band[:, window])
        score_grads = probs * dot(jnp.concatenate([values, terms], axis=1), low_grads[...], NT)
        band_grad[:, window] += score_grads
        score_low = score_grads.astype(BF16)
        value_grad = dot(probs.astype(BF16), low_grads[:, :128])
        key_grad = dot(score_low, qkv_ref[:, :128])
        query_grad[...] += dot(keys, score_low, TN)
        key_grad = jnp.where(low, key_grad[:BLOCK], key_grad[BLOCK:])
        outs[rows, 128:256] = (key_grad * (1.0 / LOG2E)).astype(BF16)
        outs[rows, 256:384] = jnp.where(low, value_grad[:BLOCK], value_grad[BLOCK:]).astype(BF16)
        return carry

    lax.fori_loop(0, count, step, 0, unroll=True)

    def turn(j, carry):
        rows = block_of(j)
        outs[rows, 0:128] = (query_grad[:, rows].T * 0.125).astype(BF16)
        return carry

    lax.fori_loop(0, count, turn, 0)
    for step, ref in enumerate([kept_ref] * 4 + [sent_ref] * 4):
        at = pl.ds(pl.multiple_of(order_ref[step] * TOK, TOK), TOK)
        ref[step % 4] = dot(outs[at, :], proj_ref[...]).astype(BF16)
    fetch.wait()
    total = dot(outs[...], normed[...], TN)
    weight_ref[:384, :] = total.astype(BF16)
    gain_grad_ref[...] = jnp.sum(total * proj_ref[...].astype(F32), axis=0, keepdims=True) / gain_ref[...]
    hot = buckets_ref[...] == iota((BUCKETS, SPAN), 0)
    for head in range(2):
        total = jnp.zeros((8, SPAN), F32)
        for group in range(BLOCK // 8):
            total = total + pltpu.roll(
                band_grad[head * BLOCK + group * 8 : head * BLOCK + (group + 1) * 8, :],
                (BLOCK - 1 - 8 * group) % SPAN,
                1,
            )
        row = jnp.zeros((1, SPAN), F32)
        for part in range(8):
            row = row + pltpu.roll(total, (SPAN - part) % SPAN, 1)[part : part + 1]
        by_bucket = jnp.sum(jnp.where(hot, row, 0.0), axis=1, keepdims=True)
        bias_grad_ref[head : head + 1, :] = jnp.broadcast_to(by_bucket, (BUCKETS, 128)).T[0:1]


def attend_backward(order, bias, normed, qkv, o, head_grads, buckets, proj, gain):
    return call(
        attend_backward_kernel,
        "attend_backward",
        [
            shape((2, BUCKETS), F32),
            shape((512, WIDTH), BF16),
            shape((1, WIDTH), F32),
            shape((4, TOK, WIDTH), BF16),
            shape((4, TOK, WIDTH), BF16),
        ],
        [order, bias, normed, qkv, o, head_grads, buckets, proj, gain],
        [
            pltpu.VMEM((2 * BLOCK, SPAN), F32),
            pltpu.VMEM((2 * BLOCK, SPAN), F32),
            pltpu.VMEM((128, LEN), F32),
            pltpu.VMEM((LEN, 384), BF16),
            pltpu.VMEM((LEN, 256), BF16),
            pltpu.VMEM((LEN, WIDTH), BF16),
            pltpu.SemaphoreType.DMA(()),
        ],
        smem=2,
        hbm=1,
    )


def iota(dims, axis):
    return lax.broadcasted_iota(jnp.int32, dims, axis)


def spread_kernel(turned_ref, routes_ref, cot_ref, picks_ref, place_ref, grads_ref):
    down = iota((EXPERTS, TOK), 0)
    before = (iota((TOK, TOK), 0) < iota((TOK, TOK), 1)).astype(BF16)
    named = [turned_ref[c : c + 1, :] == down for c in range(TOP)]
    earlier = [dot(n.astype(BF16), before) for n in named]
    earlier[1] = earlier[1] + jnp.sum(named[0].astype(F32), axis=1, keepdims=True)
    cells = iota((EXPERTS * SLOTS, TOK), 0)
    picks = jnp.zeros((EXPERTS * SLOTS, TOK), F32)
    for c in range(TOP):
        place = jnp.sum(jnp.where(named[c], earlier[c], 0.0), axis=0, keepdims=True).astype(jnp.int32)
        slot = jnp.where(place < CAP, turned_ref[c : c + 1, :] * SLOTS + place, -1)
        picks = picks + (cells == slot).astype(F32)
    picks = picks.astype(BF16)
    picks_ref[...] = picks
    grads_ref[...] = dot(picks, cot_ref[...]).astype(BF16)
    across = iota((TOK, EXPERTS), 1)
    after = (iota((TOK, TOK), 1) < iota((TOK, TOK), 0)).astype(BF16)
    named = [routes_ref[:, c : c + 1] == across for c in range(TOP)]
    earlier = [dot(after, n.astype(BF16)) for n in named]
    earlier[1] = earlier[1] + jnp.sum(named[0].astype(F32), axis=0, keepdims=True)
    for c in range(TOP):
        place = jnp.sum(jnp.where(named[c], earlier[c], 0.0), axis=1, keepdims=True)
        place_ref[:, c : c + 1] = place.astype(jnp.int32)


def split_low(value):
    high = value.astype(BF16)
    return high, (value - high.astype(F32)).astype(BF16)


def embed(values):
    rows = iota((EXPERTS * SLOTS, EXPERTS), 0)
    first = iota((EXPERTS * SLOTS, EXPERTS), 1) * SLOTS + CAP
    high, low = split_low(values)
    return dot((rows == first).astype(BF16), high) + dot((rows == first + 1).astype(BF16), low)


def dispatch_kernel(order_ref, heads_ref, *refs):
    wouts = refs[:8]
    (tok_ref, gain_ref, router_ref, routes_ref, place_ref, picks_ref,
     middle_ref, gates_ref, rows_ref, all_ref) = refs[8:]
    for index, part in enumerate(wouts):
        at = pl.ds(pl.multiple_of(order_ref[index] * 128, 128), 128)
        all_ref[at, :] = part[...]
    heads = jnp.concatenate([heads_ref[n] for n in range(8)], axis=1)
    middle = tok_ref[...].astype(F32) + dot(heads, all_ref[...])
    middle_ref[...] = middle
    scale = lax.rsqrt(jnp.mean(middle * middle, axis=-1, keepdims=True) + EPSILON)
    normed = middle * scale * gain_ref[...]
    rows_ref[...] = dot(picks_ref[...], normed.astype(BF16)).astype(BF16)
    logits = dot(normed, router_ref[...], NT, HIGHEST)
    across = iota((TOK, EXPERTS), 1)
    named = [routes_ref[:, c : c + 1] == across for c in range(TOP)]
    picked = [jnp.sum(jnp.where(n, logits, 0.0), axis=1, keepdims=True) for n in named]
    peak = jnp.maximum(picked[0], picked[1])
    powers = [jnp.exp(p - peak) for p in picked]
    total = powers[0] + powers[1]
    table = jnp.zeros((EXPERTS, 128), F32)
    for c in range(TOP):
        gate = powers[c] / total
        gates_ref[:, c : c + 1] = gate
        spot = (iota((TOK, 128), 1) == place_ref[:, c : c + 1]) & (place_ref[:, c : c + 1] < CAP)
        expert = named[c].astype(F32).astype(BF16)
        high, low = split_low(gate)
        for term in (high, low):
            table = table + dot(expert, jnp.where(spot, term.astype(F32), 0.0).astype(BF16), TN)
    rows_ref[:, :128] = (rows_ref[:, :128].astype(F32) + embed(table)).astype(BF16)


def slots_kernel(routes_ref, place_ref, picks_ref):
    cells = iota((TOK, EXPERTS * SLOTS), 1)
    for c in range(TOP):
        place = place_ref[:, c : c + 1]
        slot = jnp.where(place < CAP, routes_ref[:, c : c + 1] * SLOTS + place, -1)
        picks_ref[c] = (cells == slot).astype(F32).astype(BF16)


def middle_grad_kernel(
    rows_ref, gates_ref, middle_ref, cot_ref, routes_ref, place_ref, picks_ref, gain_ref, router_ref, wout_ref,
    middle_grad_ref, low_ref, heads_ref, gain_grad_ref, logit_ref,
):
    spots = iota((EXPERTS, EXPERTS * SLOTS), 1)
    first = iota((EXPERTS, EXPERTS * SLOTS), 0) * SLOTS + CAP
    packed = rows_ref[:, :128]
    table = [dot((spots == first + step).astype(BF16), packed).astype(BF16) for step in range(2)]
    across = iota((TOK, EXPERTS), 1)
    named = [routes_ref[:, c : c + 1] == across for c in range(TOP)]
    gates = [gates_ref[:, c : c + 1] for c in range(TOP)]
    gate_grads = []
    for c in range(TOP):
        expert = named[c].astype(F32).astype(BF16)
        lines = dot(expert, table[0]) + dot(expert, table[1])
        place = place_ref[:, c : c + 1]
        spot = (iota((TOK, 128), 1) == place) & (place < CAP)
        gate_grads.append(jnp.sum(jnp.where(spot, lines, 0.0), axis=1, keepdims=True))
    mean = gates[0] * gate_grads[0] + gates[1] * gate_grads[1]
    logit_grads = sum(
        jnp.where(n, g * (d - mean), 0.0) for n, g, d in zip(named, gates, gate_grads)
    )
    logit_ref[...] = logit_grads
    normed_grad = dot(logit_grads, router_ref[...], precision=HIGHEST)
    for c, gate in enumerate(gates):
        normed_grad = normed_grad + gate * dot(picks_ref[c], rows_ref[...])
    middle = middle_ref[...]
    scale = lax.rsqrt(jnp.mean(middle * middle, axis=-1, keepdims=True) + EPSILON)
    unit = middle * scale
    gain_grad_ref[...] = jnp.sum(normed_grad * unit, axis=0, keepdims=True)
    weighted = normed_grad * gain_ref[...]
    middle_grad = cot_ref[...].astype(F32) + scale * (
        weighted - unit * jnp.mean(weighted * unit, axis=-1, keepdims=True)
    )
    middle_grad_ref[...] = middle_grad
    low = middle_grad.astype(BF16)
    low_ref[...] = low
    for n in range(8):
        heads_ref[n] = dot(low, wout_ref[n * 128 : (n + 1) * 128, :], NT).astype(BF16)


def combine_kernel(rows_ref, middle_ref, gates_ref, picks_ref, layer_ref):
    layer = middle_ref[...]
    mixed = jnp.zeros_like(layer)
    for c in range(TOP):
        mixed = mixed + gates_ref[:, c : c + 1] * dot(picks_ref[c], rows_ref[...])
    layer_ref[...] = (layer + mixed).astype(BF16)


CUBIC = 0.044715
ROOT = math.sqrt(2.0 / math.pi)


def unpack_kernel(gated, blocks_ref, rows_ref):
    at = iota((ROWS, EXPERTS * SLOTS), 0)
    pick = (at // CAP) * SLOTS + at % CAP == iota((ROWS, EXPERTS * SLOTS), 1)
    rows_ref[:ROWS, :] = dot(pick.astype(F32).astype(BF16), blocks_ref[...]).astype(BF16)
    if gated:
        spots = iota((EXPERTS, EXPERTS * SLOTS), 1)
        first = iota((EXPERTS, EXPERTS * SLOTS), 0) * SLOTS + CAP
        lane = iota((128, ROWS), 1) % CAP == iota((128, ROWS), 0)
        mine = iota((EXPERTS, ROWS), 1) // CAP == iota((EXPERTS, ROWS), 0)
        rows_ref[ROWS:, :] = jnp.zeros((TILED - ROWS, WIDTH), BF16)
        terms = []
        for step in range(2):
            table = dot((spots == first + step).astype(BF16), blocks_ref[:, :128]).astype(BF16)
            spread = dot(table, lane.astype(F32).astype(BF16))
            terms.append(jnp.sum(jnp.where(mine, spread, 0.0), axis=0, keepdims=True))
        rows_ref[ROWS:, :ROWS] = stack_terms(*terms)


def stack_terms(high, low):
    step = iota((TILED - ROWS, ROWS), 0)
    return jnp.where(step == 0, high, jnp.where(step == 1, low, 0.0)).astype(BF16)


def unpack(blocks, gated):
    return call(
        functools.partial(unpack_kernel, gated),
        "unpack",
        [shape((TILED if gated else ROWS, WIDTH), BF16)],
        [blocks.reshape(EXPERTS * SLOTS, WIDTH)],
    )[0]


def expert_kernel(counts, *refs):
    groups = []
    for count in counts:
        groups.append(refs[: count + 1])
        refs = refs[count + 1 :]
    pair_ref, pair_new_ref, down_ref, down_new_ref = refs[:4]
    refs = refs[4:]
    for *rows_refs, grads_ref in groups:
        mid_ref, inner_ref, out_top_ref, out_end_ref, back_top_ref, back_end_ref = refs[:6]
        refs = refs[6:]
        if len(rows_refs) == 1:
            rows = rows_refs[0][:ROWS, :]
        else:
            rows = jnp.concatenate([rows_refs[0][...], rows_refs[1][:HALF, :]], axis=0)
        one = dot(rows, pair_ref[...], NT)
        two = dot(rows, pair_new_ref[...], NT)
        gate = jnp.concatenate([one[:, :PADDED], two[:, :PADDED]], axis=1)
        up = jnp.concatenate([one[:, PADDED:], two[:, PADDED:]], axis=1)
        down = jnp.concatenate([down_ref[...], down_new_ref[...]], axis=0)
        mid_grad = dot(grads_ref[...], down, NT)
        square = gate * gate
        turned = jnp.tanh(ROOT * gate * (1.0 + CUBIC * square))
        half = 0.5 * (1.0 + turned)
        curved = gate * half
        slope = half + 0.5 * gate * (1.0 - turned * turned) * (ROOT * (1.0 + 3.0 * CUBIC * square))
        mid = (curved * up).astype(BF16)
        mid_ref[...] = mid
        gate_grad = (mid_grad * (up * slope)).astype(BF16)
        up_grad = (mid_grad * curved).astype(BF16)
        for part in range(2):
            cut = slice(part * PADDED, (part + 1) * PADDED)
            inner_ref[:, 2 * part * PADDED : (2 * part + 1) * PADDED] = gate_grad[:, cut]
            inner_ref[:, (2 * part + 1) * PADDED : (2 * part + 2) * PADDED] = up_grad[:, cut]
        product = (mid.astype(F32) * mid_grad).astype(BF16)
        line = dot(jnp.ones((8, FULL), BF16), product, NT)[0:1]
        high, low = split_low(line)
        back_end_ref[HALF:, :] = jnp.zeros((TILED - ROWS, WIDTH), BF16)
        back_end_ref[HALF:, :ROWS] = stack_terms(high.astype(F32), low.astype(F32))
        pair = jnp.concatenate([pair_ref[...], pair_new_ref[...]], axis=0)
        back = dot(inner_ref[...], pair).astype(BF16)
        back_top_ref[...] = back[:HALF]
        back_end_ref[:HALF, :] = back[HALF:]
        out = dot(mid_ref[...], down).astype(BF16)
        out_top_ref[...] = out[:HALF]
        out_end_ref[...] = out[HALF:]


def run_expert(chunks, weights):
    results = call(
        functools.partial(expert_kernel, [len(rows) for rows, _ in chunks]),
        "expert",
        [
            shape((ROWS, FULL), BF16),
            shape((ROWS, 2 * FULL), BF16),
            shape((HALF, WIDTH), BF16),
            shape((HALF, WIDTH), BF16),
            shape((HALF, WIDTH), BF16),
            shape((TILED - HALF, WIDTH), BF16),
        ]
        * len(chunks),
        [a for rows, grads in chunks for a in (*rows, grads)] + weights,
    )
    return [list(results[6 * i : 6 * i + 6]) for i in range(len(chunks))]


def join_kernel(
    own_top, own_end, near_top, near_end, left_top, far_top, right_end, far_end,
    left_out, right_out, part_top, part_end,
):
    left_out[...] = (left_top[...].astype(F32) + far_top[...].astype(F32)).astype(BF16)
    right_out[...] = (right_end[...].astype(F32) + far_end[...].astype(F32)).astype(BF16)
    part_top[...] = own_top[...].astype(F32) + near_top[...].astype(F32)
    part_end[...] = own_end[...].astype(F32) + near_end[...].astype(F32)


def join(*pieces):
    return call(
        join_kernel,
        "join",
        [shape(p.shape, t) for t, p in ((BF16, pieces[0]), (BF16, pieces[1]), (F32, pieces[0]), (F32, pieces[1]))],
        pieces,
    )


def spread_slots(rows, out_ref):
    at = iota((EXPERTS * SLOTS, ROWS), 1)
    pick = iota((EXPERTS * SLOTS, ROWS), 0) == (at // CAP) * SLOTS + at % CAP
    out_ref[...] = dot(pick.astype(F32).astype(BF16), rows.astype(BF16)).astype(BF16)


def collect_kernel(part_top, part_end, got_top, got_end, out_ref):
    end = part_end[...] + got_end[...].astype(F32)
    rows = jnp.concatenate([part_top[...] + got_top[...].astype(F32), end[:HALF]], axis=0)
    spread_slots(rows, out_ref)
    line = jnp.sum(end[HALF:, :ROWS], axis=0, keepdims=True)
    mine = iota((EXPERTS, ROWS), 1) // CAP == iota((EXPERTS, ROWS), 0)
    spot = (iota((ROWS, 128), 0) % CAP == iota((ROWS, 128), 1)).astype(F32).astype(BF16)
    table = jnp.zeros((EXPERTS, 128), F32)
    for term in split_low(line):
        table = table + dot(jnp.where(mine, term.astype(F32), 0.0).astype(BF16), spot)
    out_ref[:, :128] = (out_ref[:, :128].astype(F32) + embed(table)).astype(BF16)


def collect_out_kernel(part_top, part_end, got_top, got_end, out_ref):
    top = part_top[...] + got_top[...].astype(F32)
    end = part_end[...] + got_end[...].astype(F32)
    spread_slots(jnp.concatenate([top, end], axis=0), out_ref)


def put_weight_grads(lefts, scaled, targets):
    width = 256
    for base in range(0, len(targets) * PADDED, width):
        total = jnp.zeros((width, WIDTH), F32)
        for chunk in range(4):
            at = slice(chunk * ROWS, (chunk + 1) * ROWS)
            total = total + dot(lefts[chunk][:, base : base + width], scaled[at, :], TN)
        for index, target in enumerate(targets):
            start = max(base, index * PADDED)
            stop = min(base + width, index * PADDED + HIDDEN)
            if start < stop:
                part = total[start - base : stop - base]
                to = slice(start - index * PADDED, stop - index * PADDED)
                target[to, :] = part.astype(target.dtype)


def scale_rows(part, gates, scaled, base):
    at = slice(base, base + part.shape[0])
    for cut in range(WIDTH // 128):
        lanes = slice(cut * 128, (cut + 1) * 128)
        scaled[at, lanes] = (part[:, lanes].astype(F32) * gates).astype(BF16)


def pair_grad_kernel(*refs):
    rights, lefts = refs[:5], refs[5:9]
    own_ref, low_ref, gates_ref, scaled = refs[9:]
    same = iota((ROWS, ROWS), 0) == iota((ROWS, ROWS), 1)
    ones = jnp.ones((ROWS, 128), BF16)
    for chunk in range(4):
        base = chunk * ROWS
        tile = rights[chunk][ROWS:, :ROWS] if chunk < 3 else rights[4][HALF:, :ROWS]
        gates = jnp.zeros((ROWS, 128), F32)
        for term in range(2):
            line = tile[term : term + 1, :].astype(F32)
            gates = gates + dot(jnp.where(same, line, 0.0).astype(BF16), ones)
        gates_ref[base : base + ROWS, :] = gates
        if chunk < 3:
            scale_rows(rights[chunk][:ROWS, :], gates, scaled, base)
        else:
            scale_rows(rights[3][...], gates[:HALF], scaled, base)
            scale_rows(rights[4][:HALF, :], gates[HALF:], scaled, base + HALF)
    put_weight_grads(lefts, scaled, [own_ref.at[0], own_ref.at[1], low_ref.at[0], low_ref.at[1]])


def down_grad_kernel(*refs):
    rights, lefts = refs[:4], refs[4:8]
    gates_ref, own_ref, low_ref, scaled = refs[8:]
    for chunk in range(4):
        at = slice(chunk * ROWS, (chunk + 1) * ROWS)
        scale_rows(rights[chunk][...], gates_ref[at, :], scaled, chunk * ROWS)
    put_weight_grads(lefts, scaled, [own_ref.at[0], low_ref.at[0]])


def assemble_kernel(core_ref, own_ref, got_ref, out_ref):
    core = core_ref[0]
    out_ref[core] = own_ref[...]
    out_ref[1 - core] = got_ref[...].astype(F32)


def halves_kernel(core_ref, pair_ref, down_ref, *outs):
    for which in range(2):
        expert = core_ref[which]
        pair_out, down_out = outs[2 * which : 2 * which + 2]
        zeros = jnp.zeros((PADDED - HIDDEN, WIDTH), BF16)
        for part in range(2):
            base = part * PADDED
            pair_out[base : base + HIDDEN, :] = pair_ref[expert, part].astype(BF16)
            pair_out[base + HIDDEN : base + PADDED, :] = zeros
        down_out[:HIDDEN, :] = down_ref[expert].astype(BF16)
        down_out[HIDDEN:, :] = zeros


def outer_sent_kernel(order_ref, heads_ref, low_ref, out_ref):
    for step in range(4):
        out_ref[step] = dot(heads_ref[order_ref[4 + step]], low_ref[...], TN).astype(BF16)


def outer_kept_kernel(order_ref, heads_ref, low_ref, got_ref, logit_ref, middle_ref, gain_ref, router_ref, *outs):
    for step, out in enumerate(outs):
        own = dot(heads_ref[order_ref[step]], low_ref[...], TN)
        out[...] = (own + got_ref[step].astype(F32)).astype(BF16)
    middle = middle_ref[...]
    scale = lax.rsqrt(jnp.mean(middle * middle, axis=-1, keepdims=True) + EPSILON)
    router_ref[...] = dot(logit_ref[...], middle * scale * gain_ref[...], TN, HIGHEST)


def fill_kernel(whole_hbm, *refs):
    parts, (out_hbm, total, sem) = refs[:4], refs[4:]
    total[...] = sum(p[...].astype(F32) for p in parts).astype(BF16)
    copy = pltpu.make_async_copy(total, out_hbm.at[384:512], sem)
    copy.start()
    copy.wait()


def fill(whole, parts):
    return pl.pallas_call(
        fill_kernel,
        out_shape=shape((512, WIDTH), BF16),
        in_specs=[HBM] + [VMEM] * 4,
        out_specs=HBM,
        scratch_shapes=[pltpu.VMEM((128, WIDTH), BF16), pltpu.SemaphoreType.DMA(())],
        input_output_aliases={0: 0},
        compiler_params=pltpu.CompilerParams(vmem_limit_bytes=24 << 20),
        cost_estimate=pl.CostEstimate(flops=100000000, bytes_accessed=0, transcendentals=0),
        name="fill",
    )(whole, *parts)


def kept_kernel(kept_ref, got_ref, *outs):
    for step, out in enumerate(outs):
        out[...] = (kept_ref[step].astype(F32) + got_ref[step].astype(F32)).astype(BF16)


def input_grad_kernel(own_ref, left_ref, right_ref, over_ref, tok_ref, gain_ref, middle_ref, out_ref):
    total = (own_ref[...].astype(F32) + left_ref[...].astype(F32)) + (
        right_ref[...].astype(F32) + over_ref[...].astype(F32)
    )
    inputs = tok_ref[...].astype(F32)
    scale = lax.rsqrt(jnp.mean(inputs * inputs, axis=-1, keepdims=True) + EPSILON)
    unit = inputs * scale
    weighted = total * gain_ref[...]
    out_ref[...] = middle_ref[...] + scale * (
        weighted - unit * jnp.mean(weighted * unit, axis=-1, keepdims=True)
    )


def share_kernel(parts_ref, out_ref):
    total = parts_ref[0].astype(F32)
    for index in range(1, 16):
        total = total + parts_ref[index].astype(F32)
    total = total.astype(BF16)
    for index in range(16):
        out_ref[index] = total


def finish_kernel(rows_ref, qkv_ref, out_ref):
    for c in range(3):
        for block in range(WIDTH // 128):
            cut = slice(block * 128, (block + 1) * 128)
            qkv_ref[c, cut, :] = rows_ref[c * 128 : (c + 1) * 128, cut].astype(F32).T
    out_ref[...] = rows_ref[384:512, :].astype(F32)


def on_device(
    tokens,
    layer_cotangent,
    attn_gain,
    qkv_weight,
    out_weight,
    rel_bias,
    moe_gain,
    router_weight,
    expert_in,
    expert_out,
    routes,
    buckets,
):
    narrow = lax.axis_index("narrow")
    core = lax.rem(narrow, 2)
    x = lax.div(narrow, 2)

    barrier = lax.optimization_barrier

    def shift(value, step):
        return lax.ppermute(value, "narrow", [(i, (i + 2 * step) % 8) for i in range(8)])

    def swap(value):
        return lax.ppermute(value, "narrow", [(i, i ^ 1) for i in range(8)])

    def flip(value, axis, mask):
        size = lax.axis_size(axis)
        return lax.ppermute(value, axis, [(i, i ^ mask) for i in range(size)])

    def sum_pairs(parts):
        parts = [p.astype(F32) for p in parts]
        return (parts[0] + parts[1]) + (parts[2] + parts[3])

    def sum_four(value, axis, unit):
        low = barrier(value.astype(BF16))
        parts = [low] + [flip(low, axis, mask * unit) for mask in (1, 2, 3)]
        return sum_pairs(parts)

    exchange_groups = [
        [w * 8 + chip * 2 + c for w in range(16) for c in range(2)] for chip in range(4)
    ]

    def exchange(value):
        return lax.all_to_all(
            value, ("wide", "narrow"), 0, 0, tiled=True, axis_index_groups=exchange_groups
        )

    def blocks(send):
        return exchange(send.reshape(EXPERTS, SLOTS, WIDTH)).reshape(EXPERTS * SLOTS, WIDTH)

    picks, place, cot_rows = call(
        spread_kernel,
        "spread",
        [
            shape((EXPERTS * SLOTS, TOK), BF16),
            shape((TOK, TOP), jnp.int32),
            shape((EXPERTS * SLOTS, WIDTH), BF16),
        ],
        [routes.T, routes, layer_cotangent],
    )
    cot_arrived = blocks(cot_rows)

    def everywhere(value):
        near = [value, shift(value, 1), shift(value, -1), shift(value, 2)]
        return near + [swap(v) for v in near]

    shards = everywhere(tokens)

    chips = [x, lax.rem(x + 3, 4), lax.rem(x + 1, 4), lax.rem(x + 2, 4)]
    order = jnp.stack([2 * c + core for c in chips] + [2 * c + (1 - core) for c in chips])
    order = order.astype(jnp.int32)
    bias = rel_bias.astype(BF16).astype(F32)
    offsets = jnp.pad(buckets, (0, 1), constant_values=-1)[None]
    backward_offsets = jnp.pad(buckets[::-1], (0, 1), constant_values=-1)[None]
    gain_one = attn_gain[None]
    gain_two = moe_gain[None]
    router_rows = router_weight.T
    wout_low, shards = barrier((out_weight.astype(BF16), shards))
    wouts = [wout_low, shift(wout_low, 1), shift(wout_low, -1), shift(wout_low, 2)]
    normed, qkv, attended, proj = attend_forward(
        order, bias, shards, gain_one, qkv_weight, offsets
    )
    attended, cot_arrived, wouts = barrier((attended, cot_arrived, wouts))
    wouts = wouts + [swap(w) for w in wouts]
    heads = lax.all_to_all(attended.reshape(8, TOK, 128), "narrow", 0, 0, tiled=True)
    cot_arrived, expert_in, expert_out = barrier((cot_arrived, expert_in, expert_out))

    pair, down, pair_other, down_other = call(
        halves_kernel,
        "halves",
        [shape((FULL, WIDTH), BF16), shape((PADDED, WIDTH), BF16)] * 2,
        [
            jnp.stack([core, 1 - core]).astype(jnp.int32),
            jnp.swapaxes(expert_in, 2, 3),
            expert_out,
        ],
        smem=1,
    )
    cot_arrived, pair = barrier((cot_arrived, pair))
    cot_own = unpack(cot_arrived, False)
    heads, pair, down, pair_other, down_other, cot_own = barrier(
        (heads, pair, down, pair_other, down_other, cot_own)
    )
    cot_parts = [cot_own, shift(cot_own, 1), shift(cot_own, -1), shift(cot_own, 2)]
    weights = [pair, swap(pair_other), down, swap(down_other)]
    middle, gates, send_rows, wout = call(
        dispatch_kernel,
        "dispatch",
        [
            shape((TOK, WIDTH), F32),
            shape((TOK, TOP), F32),
            shape((EXPERTS * SLOTS, WIDTH), BF16),
            shape((WIDTH, WIDTH), BF16),
        ],
        [order, heads, *wouts, tokens, gain_two, router_rows, routes, place, picks],
        smem=1,
    )

    arrived = blocks(send_rows)
    place, cot_parts = barrier((place, cot_parts))
    token_picks = call(
        slots_kernel,
        "slots",
        [shape((TOP, TOK, EXPERTS * SLOTS), BF16)],
        [routes, place],
    )[0]
    arrived, token_picks = barrier((arrived, token_picks))

    row_own = unpack(arrived, True)
    row_left, row_right = shift(row_own, 1), shift(row_own, -1)
    results = run_expert([([row_own], cot_parts[0])], weights)
    row_left, row_right, results = barrier((row_left, row_right, results))
    over = [shift(row_left[:HALF], 1), shift(row_right[HALF:], -1)]
    row_parts = [row_own, row_left, row_right]
    results += run_expert([([row_left], cot_parts[1]), ([row_right], cot_parts[2])], weights)
    over, results = barrier((over, results))
    row_parts = row_parts + over
    results += run_expert([(over, cot_parts[3])], weights)
    mids, inners = ([r[i] for r in results] for i in range(2))
    outs, backs = [r[2:4] for r in results], [r[4:6] for r in results]

    def leave_far(over):
        return [shift(over[0], -1), shift(over[1], 1)]

    def leave_near(left, right):
        return [shift(right[0], 1), shift(left[1], -1)]

    def land(own, left, right, near, far):
        left_top, right_end, part_top, part_end = join(*own, *near, left[0], far[0], right[1], far[1])
        return [part_top, part_end, left_top, right_end]

    def arrive(parts):
        return [parts[0], parts[1], shift(parts[2], -1), shift(parts[3], 1)]

    far, near = leave_far(backs[3]), leave_near(*backs[1:3])
    near, inners = barrier((near, inners))
    pair_part, pair_low, gate_columns = call(
        pair_grad_kernel,
        "pair_grad",
        [
            shape((2, HIDDEN, WIDTH), F32),
            shape((2, HIDDEN, WIDTH), BF16),
            shape((4 * ROWS, 128), F32),
        ],
        [*row_parts, *inners],
        [pltpu.VMEM((4 * ROWS, WIDTH), BF16)],
    )
    far, near, pair_part, pair_low = barrier((far, near, pair_part, pair_low))
    landed = land(*backs[:3], near, far)
    pair_part, landed = barrier((pair_part, landed))
    pair_grads = call(
        assemble_kernel,
        "assemble_pair",
        [shape((2, 2, HIDDEN, WIDTH), F32)],
        [core.astype(jnp.int32).reshape(1), pair_part, swap(pair_low)],
        smem=1,
    )[0]
    pieces, outs, mids, pair_grads = barrier((arrive(landed), outs, mids, pair_grads))
    out_far, out_near = leave_far(outs[3]), leave_near(*outs[1:3])
    back = call(collect_kernel, "collect", [shape((EXPERTS * SLOTS, WIDTH), BF16)], pieces)[0]
    row_grads = blocks(back)
    mids, out_far, out_near, _ = barrier((mids, out_far, out_near, back))
    out_parts = arrive(land(*outs[:3], out_near, out_far))
    down_part, down_low = call(
        down_grad_kernel,
        "down_grad",
        [shape((1, HIDDEN, WIDTH), F32), shape((1, HIDDEN, WIDTH), BF16)],
        [*cot_parts, *mids, gate_columns],
        [pltpu.VMEM((4 * ROWS, WIDTH), BF16)],
    )
    row_grads, down_part = barrier((row_grads, down_part))
    middle_grad, middle_low, send_heads, moe_gain_grad, logit_grads = call(
        middle_grad_kernel,
        "middle_grad",
        [
            shape((TOK, WIDTH), F32),
            shape((TOK, WIDTH), BF16),
            shape((8, TOK, 128), BF16),
            shape((1, WIDTH), F32),
            shape((TOK, EXPERTS), F32),
        ],
        [
            row_grads, gates, middle, layer_cotangent, routes, place, token_picks, gain_two,
            router_rows, wout,
        ],
    )
    head_grads = lax.all_to_all(send_heads, "narrow", 0, 0, tiled=True).reshape(LEN, 128)
    middle_low, out_parts = barrier((middle_low, out_parts))
    outer_sent = call(
        outer_sent_kernel,
        "outer_sent",
        [shape((4, 128, WIDTH), BF16)],
        [order, heads, middle_low],
        smem=1,
    )[0]
    back_out = call(collect_out_kernel, "collect_out", [shape((EXPERTS * SLOTS, WIDTH), BF16)], out_parts)[0]
    outer_got, head_grads, back_out = barrier((swap(outer_sent), head_grads, back_out))
    router_terms, *outer_parts = call(
        outer_kept_kernel,
        "outer_kept",
        [shape((EXPERTS, WIDTH), F32)] + [shape((128, WIDTH), BF16)] * 4,
        [order, heads, middle_low, outer_got, logit_grads, middle, gain_two],
        smem=1,
    )
    head_grads, back_out, outer_parts = barrier((head_grads, back_out, outer_parts))
    returned = blocks(back_out)

    def to_chips(parts):
        return [parts[0]] + [shift(p, step) for p, step in zip(parts[1:], (-1, 1, 2))]

    outer_parts = to_chips(outer_parts)
    bias_grad, weight_grads, gain_grad, sent, kept = attend_backward(
        order, bias, normed, qkv, attended, head_grads, backward_offsets, proj, gain_one
    )
    bias_grad, weight_grads, returned, outer_parts = barrier(
        (bias_grad, weight_grads, returned, outer_parts)
    )

    weight_grads = fill(weight_grads, outer_parts)
    arrived_grads = lax.all_to_all(weight_grads.reshape(16, 32, WIDTH), "wide", 0, 0, tiled=True)
    gain_grad, sent, _ = barrier((gain_grad, sent, weight_grads))

    low = barrier(jnp.concatenate([router_terms, gain_grad, moe_gain_grad]).astype(BF16))
    parts = [low] + [flip(low, "narrow", 2 * mask) for mask in (1, 2, 3)]
    kept = call(
        kept_kernel,
        "kept",
        [shape((TOK, WIDTH), BF16)] * 4,
        [kept, swap(sent)],
    )
    parts, kept = barrier((parts, kept))
    small = sum_pairs(parts)
    low = barrier(small.astype(BF16))
    small = low.astype(F32) + flip(low, "narrow", 1).astype(F32)
    small = jnp.concatenate(
        [small, jnp.pad(bias_grad.reshape(1, 64), ((0, 0), (0, WIDTH - 64)))]
    )
    arrived_grads, kept = barrier((arrived_grads, kept))
    copies = call(
        share_kernel, "share", [shape((16, 32, WIDTH), BF16)], [arrived_grads]
    )[0]
    returned, _ = barrier((returned, copies))
    layer_out = call(
        combine_kernel,
        "combine",
        [shape((TOK, WIDTH), BF16)],
        [returned, middle, gates, token_picks],
    )[0]
    gathered = lax.all_to_all(copies, "wide", 0, 0, tiled=True).reshape(512, WIDTH)
    small = sum_four(small, "wide", 1)
    chip_parts = to_chips(kept)
    down_part, small, chip_parts, _ = barrier((down_part, small, chip_parts, copies))
    down_grads = call(
        assemble_kernel,
        "assemble_down",
        [shape((2, 1, HIDDEN, WIDTH), F32)],
        [core.astype(jnp.int32).reshape(1), down_part, swap(down_low)],
        smem=1,
    )[0].reshape(2, HIDDEN, WIDTH)
    small = sum_four(small, "wide", 4)
    rel_bias_grad = small[EXPERTS + 2, : 2 * BUCKETS].reshape(2, BUCKETS)
    input_grad = call(
        input_grad_kernel,
        "input_grad",
        [shape((TOK, WIDTH), F32)],
        [*chip_parts, tokens, gain_one, middle_grad],
    )[0]
    qkv_weight_grad, out_weight_grad = call(
        finish_kernel,
        "finish",
        [shape((3, WIDTH, 128), F32), shape((128, WIDTH), F32)],
        [gathered],
    )
    return (
        layer_out,
        input_grad,
        small[EXPERTS],
        qkv_weight_grad,
        out_weight_grad,
        rel_bias_grad,
        small[EXPERTS + 1],
        small[:EXPERTS].T,
        jnp.swapaxes(pair_grads, 2, 3),
        down_grads,
    )


def solution(mesh):
    placed = (
        P(("wide", "narrow"), None),
        P(("wide", "narrow"), None),
        P(),
        P(None, None, "narrow"),
        P("narrow", None),
        P("narrow", None),
        P(),
        P(),
        P("wide", None, None, "narrow"),
        P("wide", "narrow", None),
        P(("wide", "narrow"), None),
        P(),
    )
    return jax.shard_map(
        on_device,
        mesh=mesh,
        in_specs=placed,
        out_specs=(
            P(("wide", "narrow"), None),
            P(("wide", "narrow"), None),
            P(),
            P(None, None, "narrow"),
            P("narrow", None),
            P("narrow", None),
            P(),
            P(),
            P("wide", None, None, "narrow"),
            P("wide", "narrow", None),
        ),
        check_vma=False,
    )
```

```python
import functools
import math

import jax
import jax.numpy as jnp
from jax import lax
from jax.experimental import pallas as pl
from jax.experimental.pallas import tpu as pltpu
from jax.sharding import PartitionSpec as P

HEAD_DIM = 64
EXPERTS = 32
BUCKETS = 32
TOP = 2
LEN = 1408
WIDTH = 1024
TOK = 176
CAP = 13
SLOTS = 16
EPSILON = 1e-06
BLOCK = 128
SPAN = 2816
LOG2E = math.log2(math.e)
SCORE = LOG2E / 8
HIGHEST = lax.Precision.HIGHEST
F32 = jnp.float32
BF16 = jnp.bfloat16
NT = (((1,), (1,)), ((), ()))
TN = (((0,), (0,)), ((), ()))
VMEM = pl.BlockSpec(memory_space=pltpu.VMEM)
SMEM = pl.BlockSpec(memory_space=pltpu.SMEM)
HBM = pl.BlockSpec(memory_space=pl.ANY)
HIDDEN = 352
PADDED = 384
FULL = 2 * PADDED
ROWS = 416
HALF = 208
TILED = 432


def shape(dims, dtype):
    return jax.ShapeDtypeStruct(dims, dtype)


COSTS = {
    "dispatch": 50,
    "slots": 50,
    "collect": 50,
    "halves": 50,
    "attend_forward": 4,
    "attend_backward": 50,
    "assemble_down": 50,
    "expert": 50,
    "pair_grad": 3,
    "share": 50,
}


MEBIBYTES = {
    "attend_forward": 56,
    "attend_backward": 56,
    "dispatch": 56,
    "halves": 56,
    "expert": 40,
    "middle_grad": 56,
    "down_grad": 56,
    "assemble_pair": 56,
    "assemble_down": 56,
}


def call(kernel, name, out_shape, ins, scratch=(), smem=0, hbm=0):
    outs = tuple(out_shape)
    return pl.pallas_call(
        kernel,
        out_shape=outs,
        in_specs=[SMEM] * smem + [HBM] * hbm + [VMEM] * (len(ins) - smem - hbm),
        out_specs=tuple([VMEM] * len(outs)),
        scratch_shapes=list(scratch),
        compiler_params=pltpu.CompilerParams(vmem_limit_bytes=MEBIBYTES.get(name, 24) << 20),
        cost_estimate=pl.CostEstimate(
            flops=int(COSTS.get(name, 0.1) * 1.15e9), bytes_accessed=0, transcendentals=0
        ),
        name=name,
    )(*ins)


def dot(a, b, dims=None, precision=None):
    if dims is None:
        dims = (((1,), (0,)), ((), ()))
    return lax.dot_general(a, b, dims, precision=precision, preferred_element_type=F32)


def block_of(i):
    return pl.ds(pl.multiple_of(i * BLOCK, BLOCK), BLOCK)


def offset_row(buckets, bias_ref, head):
    total = jnp.zeros(buckets.shape, F32)
    for bucket in range(BUCKETS):
        total = jnp.where(buckets == bucket, bias_ref[head, bucket], total)
    return total


def skew(row):
    return pltpu.roll(
        jnp.broadcast_to(row, (BLOCK, SPAN)), SPAN - (BLOCK - 1), 1, stride=1, stride_axis=0
    )


def spread_terms(value):
    lane = iota(value.shape, 1) % HEAD_DIM
    high = value.astype(BF16).astype(F32)
    rest = value - high
    middle = rest.astype(BF16).astype(F32)
    terms = jnp.where(lane == 0, high, jnp.where(lane == 1, middle, rest - middle))
    return jnp.where(lane < 3, terms, 0.0).astype(BF16)


def by_head(value, low):
    zero = jnp.zeros_like(value)
    return jnp.concatenate([jnp.where(low, value, zero), jnp.where(low, zero, value)], axis=0)


def attend_forward_kernel(place_ref, bias_ref, *refs):
    shards = refs[:8]
    (gain_ref, w_ref, buckets_ref, h_ref, qkv_ref, o_ref, proj_ref,
     band, value_parts) = refs[8:]
    count = LEN // BLOCK
    for head in range(2):
        band[head * BLOCK : (head + 1) * BLOCK, :] = skew(
            offset_row(buckets_ref[...], bias_ref, head) * LOG2E
        )
    weights = jnp.concatenate([w_ref[c].astype(BF16) for c in range(3)], axis=1)
    value_parts[:, 128:] = jnp.ones((LEN, 128), BF16)
    for index, shard in enumerate(shards):
        rows = pl.ds(pl.multiple_of(place_ref[index] * TOK, TOK), TOK)
        x = shard[...].astype(F32)
        scale = lax.rsqrt(jnp.mean(x * x, axis=-1, keepdims=True) + EPSILON)
        normed = (x * scale * gain_ref[...]).astype(BF16)
        h_ref[rows, :] = normed
        projected = dot(normed, weights).astype(BF16)
        qkv_ref[rows, :128] = (projected[:, :128].astype(F32) * SCORE).astype(BF16)
        qkv_ref[rows, 256:] = projected[:, 128:]
        value_parts[rows, :128] = projected[:, 256:]
    for c in range(3):
        proj_ref[c * 128 : (c + 1) * 128, :] = w_ref[c].T.astype(BF16)
    low = iota((BLOCK, 128), 1) < HEAD_DIM

    def attend(i, carry):
        rows = block_of(i)
        window = pl.ds(pl.multiple_of((count - 1 - i) * BLOCK, BLOCK), LEN)
        query = by_head(qkv_ref[rows, :128], low)
        scores = dot(query, qkv_ref[:, 256:384], NT) + band[:, window]
        peaks = jnp.max(scores, axis=-1, keepdims=True)
        weights = jnp.exp2(scores - peaks).astype(BF16)
        both = dot(weights, value_parts[...])
        parts = [both[:BLOCK], both[BLOCK:]]
        peaks = [peaks[:BLOCK], peaks[BLOCK:]]
        top = jnp.where(low, parts[0][:, :128], parts[1][:, :128])
        totals = jnp.where(low, parts[0][:, 128:], parts[1][:, 128:])
        o_ref[rows, :] = (top / totals).astype(BF16)
        logs = jnp.where(low, peaks[0], peaks[1]) + jnp.log2(totals)
        qkv_ref[rows, 128:256] = spread_terms(-logs)
        return carry

    lax.fori_loop(0, count, attend, 0, unroll=True)


def attend_forward(places, bias, shards, gain, weights, buckets):
    head = (LEN, 128)
    return call(
        attend_forward_kernel,
        "attend_forward",
        [
            shape((LEN, WIDTH), BF16),
            shape((LEN, 512), BF16),
            shape(head, BF16),
            shape((384, WIDTH), BF16),
        ],
        [places, bias, *shards, gain, weights, buckets],
        [pltpu.VMEM((2 * BLOCK, SPAN), F32), pltpu.VMEM((LEN, 256), BF16)],
        smem=2,
    )


def attend_backward_kernel(
    order_ref, bias_ref, normed_hbm, qkv_ref, o_ref, do_ref, buckets_ref, proj_ref, gain_ref,
    bias_grad_ref, weight_ref, gain_grad_ref, sent_ref, kept_ref,
    band, band_grad, query_grad, outs, low_grads, normed, sem,
):
    fetch = pltpu.make_async_copy(normed_hbm, normed, sem)
    fetch.start()
    count = LEN // BLOCK
    for head in range(2):
        band[head * BLOCK : (head + 1) * BLOCK, :] = skew(
            offset_row(buckets_ref[...], bias_ref, head) * LOG2E
        )
    band_grad[...] = jnp.zeros_like(band_grad)
    query_grad[...] = jnp.zeros_like(query_grad)
    low = iota((BLOCK, 128), 1) < HEAD_DIM

    def prepare(i, carry):
        rows = block_of(i)
        grads = do_ref[rows, :]
        products = grads.astype(F32) * o_ref[rows, :].astype(F32)
        one = jnp.sum(jnp.where(low, products, 0.0), axis=1, keepdims=True)
        two = jnp.sum(jnp.where(low, 0.0, products), axis=1, keepdims=True)
        low_grads[rows, :128] = grads
        low_grads[rows, 128:] = spread_terms(-jnp.where(low, one, two))
        return carry

    lax.fori_loop(0, count, prepare, 0)
    lane = iota((2 * BLOCK, 128), 1) - HEAD_DIM * (iota((2 * BLOCK, 128), 0) // BLOCK)
    terms = ((lane >= 0) & (lane < 3)).astype(F32).astype(BF16)

    def step(j, carry):
        rows = block_of(j)
        window = pl.ds(pl.multiple_of((count - 1 - j) * BLOCK, BLOCK), LEN)
        keys = by_head(qkv_ref[rows, 256:384], low)
        values = by_head(qkv_ref[rows, 384:], low)
        scores = dot(jnp.concatenate([keys, terms], axis=1), qkv_ref[:, :256], NT)
        probs = jnp.exp2(scores + band[:, window])
        score_grads = probs * dot(jnp.concatenate([values, terms], axis=1), low_grads[...], NT)
        band_grad[:, window] += score_grads
        score_low = score_grads.astype(BF16)
        value_grad = dot(probs.astype(BF16), low_grads[:, :128])
        key_grad = dot(score_low, qkv_ref[:, :128])
        query_grad[...] += dot(keys, score_low, TN)
        key_grad = jnp.where(low, key_grad[:BLOCK], key_grad[BLOCK:])
        outs[rows, 128:256] = (key_grad * (1.0 / LOG2E)).astype(BF16)
        outs[rows, 256:384] = jnp.where(low, value_grad[:BLOCK], value_grad[BLOCK:]).astype(BF16)
        return carry

    lax.fori_loop(0, count, step, 0, unroll=True)

    def turn(j, carry):
        rows = block_of(j)
        outs[rows, 0:128] = (query_grad[:, rows].T * 0.125).astype(BF16)
        return carry

    lax.fori_loop(0, count, turn, 0)
    for step, ref in enumerate([kept_ref] * 4 + [sent_ref] * 4):
        at = pl.ds(pl.multiple_of(order_ref[step] * TOK, TOK), TOK)
        ref[step % 4] = dot(outs[at, :], proj_ref[...]).astype(BF16)
    fetch.wait()
    total = dot(outs[...], normed[...], TN)
    weight_ref[:384, :] = total.astype(BF16)
    gain_grad_ref[...] = jnp.sum(total * proj_ref[...].astype(F32), axis=0, keepdims=True) / gain_ref[...]
    hot = buckets_ref[...] == iota((BUCKETS, SPAN), 0)
    for head in range(2):
        total = jnp.zeros((8, SPAN), F32)
        for group in range(BLOCK // 8):
            total = total + pltpu.roll(
                band_grad[head * BLOCK + group * 8 : head * BLOCK + (group + 1) * 8, :],
                (BLOCK - 1 - 8 * group) % SPAN,
                1,
            )
        row = jnp.zeros((1, SPAN), F32)
        for part in range(8):
            row = row + pltpu.roll(total, (SPAN - part) % SPAN, 1)[part : part + 1]
        by_bucket = jnp.sum(jnp.where(hot, row, 0.0), axis=1, keepdims=True)
        bias_grad_ref[head : head + 1, :] = jnp.broadcast_to(by_bucket, (BUCKETS, 128)).T[0:1]


def attend_backward(order, bias, normed, qkv, o, head_grads, buckets, proj, gain):
    return call(
        attend_backward_kernel,
        "attend_backward",
        [
            shape((2, BUCKETS), F32),
            shape((512, WIDTH), BF16),
            shape((1, WIDTH), F32),
            shape((4, TOK, WIDTH), BF16),
            shape((4, TOK, WIDTH), BF16),
        ],
        [order, bias, normed, qkv, o, head_grads, buckets, proj, gain],
        [
            pltpu.VMEM((2 * BLOCK, SPAN), F32),
            pltpu.VMEM((2 * BLOCK, SPAN), F32),
            pltpu.VMEM((128, LEN), F32),
            pltpu.VMEM((LEN, 384), BF16),
            pltpu.VMEM((LEN, 256), BF16),
            pltpu.VMEM((LEN, WIDTH), BF16),
            pltpu.SemaphoreType.DMA(()),
        ],
        smem=2,
        hbm=1,
    )


def iota(dims, axis):
    return lax.broadcasted_iota(jnp.int32, dims, axis)


def spread_kernel(turned_ref, routes_ref, cot_ref, picks_ref, place_ref, grads_ref):
    down = iota((EXPERTS, TOK), 0)
    before = (iota((TOK, TOK), 0) < iota((TOK, TOK), 1)).astype(BF16)
    named = [turned_ref[c : c + 1, :] == down for c in range(TOP)]
    earlier = [dot(n.astype(BF16), before) for n in named]
    earlier[1] = earlier[1] + jnp.sum(named[0].astype(F32), axis=1, keepdims=True)
    cells = iota((EXPERTS * SLOTS, TOK), 0)
    picks = jnp.zeros((EXPERTS * SLOTS, TOK), F32)
    for c in range(TOP):
        place = jnp.sum(jnp.where(named[c], earlier[c], 0.0), axis=0, keepdims=True).astype(jnp.int32)
        slot = jnp.where(place < CAP, turned_ref[c : c + 1, :] * SLOTS + place, -1)
        picks = picks + (cells == slot).astype(F32)
    picks = picks.astype(BF16)
    picks_ref[...] = picks
    grads_ref[...] = dot(picks, cot_ref[...]).astype(BF16)
    across = iota((TOK, EXPERTS), 1)
    after = (iota((TOK, TOK), 1) < iota((TOK, TOK), 0)).astype(BF16)
    named = [routes_ref[:, c : c + 1] == across for c in range(TOP)]
    earlier = [dot(after, n.astype(BF16)) for n in named]
    earlier[1] = earlier[1] + jnp.sum(named[0].astype(F32), axis=0, keepdims=True)
    for c in range(TOP):
        place = jnp.sum(jnp.where(named[c], earlier[c], 0.0), axis=1, keepdims=True)
        place_ref[:, c : c + 1] = place.astype(jnp.int32)


def split_low(value):
    high = value.astype(BF16)
    return high, (value - high.astype(F32)).astype(BF16)


def embed(values):
    rows = iota((EXPERTS * SLOTS, EXPERTS), 0)
    first = iota((EXPERTS * SLOTS, EXPERTS), 1) * SLOTS + CAP
    high, low = split_low(values)
    return dot((rows == first).astype(BF16), high) + dot((rows == first + 1).astype(BF16), low)


def dispatch_kernel(order_ref, heads_ref, *refs):
    wouts = refs[:8]
    (tok_ref, gain_ref, router_ref, routes_ref, place_ref, picks_ref,
     middle_ref, gates_ref, rows_ref, all_ref) = refs[8:]
    for index, part in enumerate(wouts):
        at = pl.ds(pl.multiple_of(order_ref[index] * 128, 128), 128)
        all_ref[at, :] = part[...]
    heads = jnp.concatenate([heads_ref[n] for n in range(8)], axis=1)
    middle = tok_ref[...].astype(F32) + dot(heads, all_ref[...])
    middle_ref[...] = middle
    scale = lax.rsqrt(jnp.mean(middle * middle, axis=-1, keepdims=True) + EPSILON)
    normed = middle * scale * gain_ref[...]
    rows_ref[...] = dot(picks_ref[...], normed.astype(BF16)).astype(BF16)
    logits = dot(normed, router_ref[...], NT, HIGHEST)
    across = iota((TOK, EXPERTS), 1)
    named = [routes_ref[:, c : c + 1] == across for c in range(TOP)]
    picked = [jnp.sum(jnp.where(n, logits, 0.0), axis=1, keepdims=True) for n in named]
    peak = jnp.maximum(picked[0], picked[1])
    powers = [jnp.exp(p - peak) for p in picked]
    total = powers[0] + powers[1]
    table = jnp.zeros((EXPERTS, 128), F32)
    for c in range(TOP):
        gate = powers[c] / total
        gates_ref[:, c : c + 1] = gate
        spot = (iota((TOK, 128), 1) == place_ref[:, c : c + 1]) & (place_ref[:, c : c + 1] < CAP)
        expert = named[c].astype(F32).astype(BF16)
        high, low = split_low(gate)
        for term in (high, low):
            table = table + dot(expert, jnp.where(spot, term.astype(F32), 0.0).astype(BF16), TN)
    rows_ref[:, :128] = (rows_ref[:, :128].astype(F32) + embed(table)).astype(BF16)


def slots_kernel(routes_ref, place_ref, picks_ref):
    cells = iota((TOK, EXPERTS * SLOTS), 1)
    for c in range(TOP):
        place = place_ref[:, c : c + 1]
        slot = jnp.where(place < CAP, routes_ref[:, c : c + 1] * SLOTS + place, -1)
        picks_ref[c] = (cells == slot).astype(F32).astype(BF16)


def middle_grad_kernel(
    rows_ref, gates_ref, middle_ref, cot_ref, routes_ref, place_ref, picks_ref, gain_ref, router_ref, wout_ref,
    middle_grad_ref, low_ref, heads_ref, gain_grad_ref, logit_ref,
):
    spots = iota((EXPERTS, EXPERTS * SLOTS), 1)
    first = iota((EXPERTS, EXPERTS * SLOTS), 0) * SLOTS + CAP
    packed = rows_ref[:, :128]
    table = [dot((spots == first + step).astype(BF16), packed).astype(BF16) for step in range(2)]
    across = iota((TOK, EXPERTS), 1)
    named = [routes_ref[:, c : c + 1] == across for c in range(TOP)]
    gates = [gates_ref[:, c : c + 1] for c in range(TOP)]
    gate_grads = []
    for c in range(TOP):
        expert = named[c].astype(F32).astype(BF16)
        lines = dot(expert, table[0]) + dot(expert, table[1])
        place = place_ref[:, c : c + 1]
        spot = (iota((TOK, 128), 1) == place) & (place < CAP)
        gate_grads.append(jnp.sum(jnp.where(spot, lines, 0.0), axis=1, keepdims=True))
    mean = gates[0] * gate_grads[0] + gates[1] * gate_grads[1]
    logit_grads = sum(
        jnp.where(n, g * (d - mean), 0.0) for n, g, d in zip(named, gates, gate_grads)
    )
    logit_ref[...] = logit_grads
    normed_grad = dot(logit_grads, router_ref[...], precision=HIGHEST)
    for c, gate in enumerate(gates):
        normed_grad = normed_grad + gate * dot(picks_ref[c], rows_ref[...])
    middle = middle_ref[...]
    scale = lax.rsqrt(jnp.mean(middle * middle, axis=-1, keepdims=True) + EPSILON)
    unit = middle * scale
    gain_grad_ref[...] = jnp.sum(normed_grad * unit, axis=0, keepdims=True)
    weighted = normed_grad * gain_ref[...]
    middle_grad = cot_ref[...].astype(F32) + scale * (
        weighted - unit * jnp.mean(weighted * unit, axis=-1, keepdims=True)
    )
    middle_grad_ref[...] = middle_grad
    low = middle_grad.astype(BF16)
    low_ref[...] = low
    for n in range(8):
        heads_ref[n] = dot(low, wout_ref[n * 128 : (n + 1) * 128, :], NT).astype(BF16)


def combine_kernel(rows_ref, middle_ref, gates_ref, picks_ref, layer_ref):
    layer = middle_ref[...]
    mixed = jnp.zeros_like(layer)
    for c in range(TOP):
        mixed = mixed + gates_ref[:, c : c + 1] * dot(picks_ref[c], rows_ref[...])
    layer_ref[...] = (layer + mixed).astype(BF16)


CUBIC = 0.044715
ROOT = math.sqrt(2.0 / math.pi)


def unpack_kernel(gated, blocks_ref, rows_ref):
    at = iota((ROWS, EXPERTS * SLOTS), 0)
    pick = (at // CAP) * SLOTS + at % CAP == iota((ROWS, EXPERTS * SLOTS), 1)
    rows_ref[:ROWS, :] = dot(pick.astype(F32).astype(BF16), blocks_ref[...]).astype(BF16)
    if gated:
        spots = iota((EXPERTS, EXPERTS * SLOTS), 1)
        first = iota((EXPERTS, EXPERTS * SLOTS), 0) * SLOTS + CAP
        lane = iota((128, ROWS), 1) % CAP == iota((128, ROWS), 0)
        mine = iota((EXPERTS, ROWS), 1) // CAP == iota((EXPERTS, ROWS), 0)
        rows_ref[ROWS:, :] = jnp.zeros((TILED - ROWS, WIDTH), BF16)
        terms = []
        for step in range(2):
            table = dot((spots == first + step).astype(BF16), blocks_ref[:, :128]).astype(BF16)
            spread = dot(table, lane.astype(F32).astype(BF16))
            terms.append(jnp.sum(jnp.where(mine, spread, 0.0), axis=0, keepdims=True))
        rows_ref[ROWS:, :ROWS] = stack_terms(*terms)


def stack_terms(high, low):
    step = iota((TILED - ROWS, ROWS), 0)
    return jnp.where(step == 0, high, jnp.where(step == 1, low, 0.0)).astype(BF16)


def unpack(blocks, gated):
    return call(
        functools.partial(unpack_kernel, gated),
        "unpack",
        [shape((TILED if gated else ROWS, WIDTH), BF16)],
        [blocks.reshape(EXPERTS * SLOTS, WIDTH)],
    )[0]


def expert_kernel(counts, merge, *refs):
    groups = []
    for count in counts:
        groups.append(refs[: count + 1])
        refs = refs[count + 1 :]
    pair_ref, pair_new_ref, down_ref, down_new_ref = refs[:4]
    refs = refs[4:]
    if merge:
        left_end, right_top = refs[:2]
        refs = refs[2:]
    for *rows_refs, grads_ref in groups:
        mid_ref, inner_ref, out_top_ref, out_end_ref, back_top_ref, back_end_ref = refs[:6]
        refs = refs[6:]
        if merge:
            out_top_ref[HALF:, :] = left_end[...]
            out_end_ref[:HALF, :] = right_top[...]
            out_top_ref, out_end_ref = out_top_ref.at[:HALF], out_end_ref.at[HALF:]
        if len(rows_refs) == 1:
            rows = rows_refs[0][:ROWS, :]
        else:
            rows = jnp.concatenate([rows_refs[0][...], rows_refs[1][:HALF, :]], axis=0)
        one = dot(rows, pair_ref[...], NT)
        two = dot(rows, pair_new_ref[...], NT)
        gate = jnp.concatenate([one[:, :PADDED], two[:, :PADDED]], axis=1)
        up = jnp.concatenate([one[:, PADDED:], two[:, PADDED:]], axis=1)
        down = jnp.concatenate([down_ref[...], down_new_ref[...]], axis=0)
        mid_grad = dot(grads_ref[...], down, NT)
        square = gate * gate
        turned = jnp.tanh(ROOT * gate * (1.0 + CUBIC * square))
        half = 0.5 * (1.0 + turned)
        curved = gate * half
        slope = half + 0.5 * gate * (1.0 - turned * turned) * (ROOT * (1.0 + 3.0 * CUBIC * square))
        mid = (curved * up).astype(BF16)
        mid_ref[...] = mid
        gate_grad = (mid_grad * (up * slope)).astype(BF16)
        up_grad = (mid_grad * curved).astype(BF16)
        for part in range(2):
            cut = slice(part * PADDED, (part + 1) * PADDED)
            inner_ref[:, 2 * part * PADDED : (2 * part + 1) * PADDED] = gate_grad[:, cut]
            inner_ref[:, (2 * part + 1) * PADDED : (2 * part + 2) * PADDED] = up_grad[:, cut]
        product = (mid.astype(F32) * mid_grad).astype(BF16)
        line = dot(jnp.ones((8, FULL), BF16), product, NT)[0:1]
        high, low = split_low(line)
        back_end_ref[HALF:, :] = jnp.zeros((TILED - ROWS, WIDTH), BF16)
        back_end_ref[HALF:, :ROWS] = stack_terms(high.astype(F32), low.astype(F32))
        pair = jnp.concatenate([pair_ref[...], pair_new_ref[...]], axis=0)
        back = dot(inner_ref[...], pair).astype(BF16)
        back_top_ref[...] = back[:HALF]
        back_end_ref[:HALF, :] = back[HALF:]
        out = dot(mid_ref[...], down).astype(BF16)
        out_top_ref[...] = out[:HALF]
        out_end_ref[...] = out[HALF:]


def run_expert(chunks, weights, merged=()):
    sent = ROWS if merged else HALF
    results = call(
        functools.partial(expert_kernel, [len(rows) for rows, _ in chunks], bool(merged)),
        "expert",
        [
            shape((ROWS, FULL), BF16),
            shape((ROWS, 2 * FULL), BF16),
            shape((sent, WIDTH), BF16),
            shape((sent, WIDTH), BF16),
            shape((HALF, WIDTH), BF16),
            shape((TILED - HALF, WIDTH), BF16),
        ]
        * len(chunks),
        [a for rows, grads in chunks for a in (*rows, grads)] + weights + list(merged),
    )
    return [list(results[6 * i : 6 * i + 6]) for i in range(len(chunks))]


def join_kernel(
    own_top, own_end, near_top, near_end, left_top, far_top, right_end, far_end,
    left_out, right_out, part_top, part_end,
):
    left_out[...] = (left_top[...].astype(F32) + far_top[...].astype(F32)).astype(BF16)
    right_out[...] = (right_end[...].astype(F32) + far_end[...].astype(F32)).astype(BF16)
    part_top[...] = own_top[...].astype(F32) + near_top[...].astype(F32)
    part_end[...] = own_end[...].astype(F32) + near_end[...].astype(F32)


def join(*pieces):
    return call(
        join_kernel,
        "join",
        [shape(p.shape, t) for t, p in ((BF16, pieces[0]), (BF16, pieces[1]), (F32, pieces[0]), (F32, pieces[1]))],
        pieces,
    )


def spread_slots(rows, out_ref):
    at = iota((EXPERTS * SLOTS, ROWS), 1)
    pick = iota((EXPERTS * SLOTS, ROWS), 0) == (at // CAP) * SLOTS + at % CAP
    out_ref[...] = dot(pick.astype(F32).astype(BF16), rows.astype(BF16)).astype(BF16)


def collect_kernel(part_top, part_end, got_top, got_end, out_ref):
    end = part_end[...] + got_end[...].astype(F32)
    rows = jnp.concatenate([part_top[...] + got_top[...].astype(F32), end[:HALF]], axis=0)
    spread_slots(rows, out_ref)
    line = jnp.sum(end[HALF:, :ROWS], axis=0, keepdims=True)
    mine = iota((EXPERTS, ROWS), 1) // CAP == iota((EXPERTS, ROWS), 0)
    spot = (iota((ROWS, 128), 0) % CAP == iota((ROWS, 128), 1)).astype(F32).astype(BF16)
    table = jnp.zeros((EXPERTS, 128), F32)
    for term in split_low(line):
        table = table + dot(jnp.where(mine, term.astype(F32), 0.0).astype(BF16), spot)
    out_ref[:, :128] = (out_ref[:, :128].astype(F32) + embed(table)).astype(BF16)


def collect_out_kernel(part_top, part_end, got_top, got_end, out_ref):
    top = part_top[...] + got_top[...].astype(F32)
    end = part_end[...] + got_end[...].astype(F32)
    spread_slots(jnp.concatenate([top, end], axis=0), out_ref)


def put_weight_grads(lefts, scaled, targets):
    width = 256
    for base in range(0, len(targets) * PADDED, width):
        total = jnp.zeros((width, WIDTH), F32)
        for chunk in range(4):
            at = slice(chunk * ROWS, (chunk + 1) * ROWS)
            total = total + dot(lefts[chunk][:, base : base + width], scaled[at, :], TN)
        for index, target in enumerate(targets):
            start = max(base, index * PADDED)
            stop = min(base + width, index * PADDED + HIDDEN)
            if start < stop:
                part = total[start - base : stop - base]
                to = slice(start - index * PADDED, stop - index * PADDED)
                target[to, :] = part.astype(target.dtype)


def scale_rows(part, gates, scaled, base):
    at = slice(base, base + part.shape[0])
    for cut in range(WIDTH // 128):
        lanes = slice(cut * 128, (cut + 1) * 128)
        scaled[at, lanes] = (part[:, lanes].astype(F32) * gates).astype(BF16)


def pair_grad_kernel(*refs):
    rights, lefts = refs[:5], refs[5:9]
    own_ref, low_ref, gates_ref, scaled = refs[9:]
    same = iota((ROWS, ROWS), 0) == iota((ROWS, ROWS), 1)
    ones = jnp.ones((ROWS, 128), BF16)
    for chunk in range(4):
        base = chunk * ROWS
        tile = rights[chunk][ROWS:, :ROWS] if chunk < 3 else rights[4][HALF:, :ROWS]
        gates = jnp.zeros((ROWS, 128), F32)
        for term in range(2):
            line = tile[term : term + 1, :].astype(F32)
            gates = gates + dot(jnp.where(same, line, 0.0).astype(BF16), ones)
        gates_ref[base : base + ROWS, :] = gates
        if chunk < 3:
            scale_rows(rights[chunk][:ROWS, :], gates, scaled, base)
        else:
            scale_rows(rights[3][...], gates[:HALF], scaled, base)
            scale_rows(rights[4][:HALF, :], gates[HALF:], scaled, base + HALF)
    put_weight_grads(lefts, scaled, [own_ref.at[0], own_ref.at[1], low_ref.at[0], low_ref.at[1]])


def down_grad_kernel(*refs):
    rights, lefts = refs[:4], refs[4:8]
    gates_ref, own_ref, low_ref, scaled = refs[8:]
    for chunk in range(4):
        at = slice(chunk * ROWS, (chunk + 1) * ROWS)
        scale_rows(rights[chunk][...], gates_ref[at, :], scaled, chunk * ROWS)
    put_weight_grads(lefts, scaled, [own_ref.at[0], low_ref.at[0]])


def assemble_kernel(core_ref, own_ref, got_ref, out_ref):
    core = core_ref[0]
    out_ref[core] = own_ref[...]
    out_ref[1 - core] = got_ref[...].astype(F32)


def halves_kernel(core_ref, pair_ref, down_ref, *outs):
    for which in range(2):
        expert = core_ref[which]
        pair_out, down_out = outs[2 * which : 2 * which + 2]
        zeros = jnp.zeros((PADDED - HIDDEN, WIDTH), BF16)
        for part in range(2):
            base = part * PADDED
            pair_out[base : base + HIDDEN, :] = pair_ref[expert, part].astype(BF16)
            pair_out[base + HIDDEN : base + PADDED, :] = zeros
        down_out[:HIDDEN, :] = down_ref[expert].astype(BF16)
        down_out[HIDDEN:, :] = zeros


def outer_sent_kernel(order_ref, heads_ref, low_ref, out_ref):
    for step in range(4):
        out_ref[step] = dot(heads_ref[order_ref[4 + step]], low_ref[...], TN).astype(BF16)


def outer_kept_kernel(order_ref, heads_ref, low_ref, got_ref, logit_ref, middle_ref, gain_ref, router_ref, *outs):
    for step, out in enumerate(outs):
        own = dot(heads_ref[order_ref[step]], low_ref[...], TN)
        out[...] = (own + got_ref[step].astype(F32)).astype(BF16)
    middle = middle_ref[...]
    scale = lax.rsqrt(jnp.mean(middle * middle, axis=-1, keepdims=True) + EPSILON)
    router_ref[...] = dot(logit_ref[...], middle * scale * gain_ref[...], TN, HIGHEST)


def fill_kernel(whole_hbm, *refs):
    parts, (out_hbm, total, sem) = refs[:4], refs[4:]
    total[...] = sum(p[...].astype(F32) for p in parts).astype(BF16)
    copy = pltpu.make_async_copy(total, out_hbm.at[384:512], sem)
    copy.start()
    copy.wait()


def fill(whole, parts):
    return pl.pallas_call(
        fill_kernel,
        out_shape=shape((512, WIDTH), BF16),
        in_specs=[HBM] + [VMEM] * 4,
        out_specs=HBM,
        scratch_shapes=[pltpu.VMEM((128, WIDTH), BF16), pltpu.SemaphoreType.DMA(())],
        input_output_aliases={0: 0},
        compiler_params=pltpu.CompilerParams(vmem_limit_bytes=24 << 20),
        cost_estimate=pl.CostEstimate(flops=100000000, bytes_accessed=0, transcendentals=0),
        name="fill",
    )(whole, *parts)


def kept_kernel(kept_ref, got_ref, *outs):
    for step, out in enumerate(outs):
        out[...] = (kept_ref[step].astype(F32) + got_ref[step].astype(F32)).astype(BF16)


def input_grad_kernel(own_ref, left_ref, right_ref, over_ref, tok_ref, gain_ref, middle_ref, out_ref):
    total = (own_ref[...].astype(F32) + left_ref[...].astype(F32)) + (
        right_ref[...].astype(F32) + over_ref[...].astype(F32)
    )
    inputs = tok_ref[...].astype(F32)
    scale = lax.rsqrt(jnp.mean(inputs * inputs, axis=-1, keepdims=True) + EPSILON)
    unit = inputs * scale
    weighted = total * gain_ref[...]
    out_ref[...] = middle_ref[...] + scale * (
        weighted - unit * jnp.mean(weighted * unit, axis=-1, keepdims=True)
    )


def share_kernel(parts_ref, out_ref):
    total = parts_ref[0].astype(F32)
    for index in range(1, 16):
        total = total + parts_ref[index].astype(F32)
    total = total.astype(BF16)
    for index in range(16):
        out_ref[index] = total


def finish_kernel(rows_ref, qkv_ref, out_ref):
    for c in range(3):
        for block in range(WIDTH // 128):
            cut = slice(block * 128, (block + 1) * 128)
            qkv_ref[c, cut, :] = rows_ref[c * 128 : (c + 1) * 128, cut].astype(F32).T
    out_ref[...] = rows_ref[384:512, :].astype(F32)


def on_device(
    tokens,
    layer_cotangent,
    attn_gain,
    qkv_weight,
    out_weight,
    rel_bias,
    moe_gain,
    router_weight,
    expert_in,
    expert_out,
    routes,
    buckets,
):
    narrow = lax.axis_index("narrow")
    core = lax.rem(narrow, 2)
    x = lax.div(narrow, 2)

    barrier = lax.optimization_barrier

    def shift(value, step):
        return lax.ppermute(value, "narrow", [(i, (i + 2 * step) % 8) for i in range(8)])

    def swap(value):
        return lax.ppermute(value, "narrow", [(i, i ^ 1) for i in range(8)])

    def flip(value, axis, mask):
        size = lax.axis_size(axis)
        return lax.ppermute(value, axis, [(i, i ^ mask) for i in range(size)])

    def sum_pairs(parts):
        parts = [p.astype(F32) for p in parts]
        return (parts[0] + parts[1]) + (parts[2] + parts[3])

    def sum_four(value, axis, unit):
        low = barrier(value.astype(BF16))
        parts = [low] + [flip(low, axis, mask * unit) for mask in (1, 2, 3)]
        return sum_pairs(parts)

    exchange_groups = [
        [w * 8 + chip * 2 + c for w in range(16) for c in range(2)] for chip in range(4)
    ]

    def exchange(value):
        return lax.all_to_all(
            value, ("wide", "narrow"), 0, 0, tiled=True, axis_index_groups=exchange_groups
        )

    def blocks(send):
        return exchange(send.reshape(EXPERTS, SLOTS, WIDTH)).reshape(EXPERTS * SLOTS, WIDTH)

    picks, place, cot_rows = call(
        spread_kernel,
        "spread",
        [
            shape((EXPERTS * SLOTS, TOK), BF16),
            shape((TOK, TOP), jnp.int32),
            shape((EXPERTS * SLOTS, WIDTH), BF16),
        ],
        [routes.T, routes, layer_cotangent],
    )
    cot_arrived = blocks(cot_rows)

    def everywhere(value):
        near = [value, shift(value, 1), shift(value, -1), shift(value, 2)]
        return near + [swap(v) for v in near]

    shards = everywhere(tokens)

    chips = [x, lax.rem(x + 3, 4), lax.rem(x + 1, 4), lax.rem(x + 2, 4)]
    order = jnp.stack([2 * c + core for c in chips] + [2 * c + (1 - core) for c in chips])
    order = order.astype(jnp.int32)
    bias = rel_bias.astype(BF16).astype(F32)
    offsets = jnp.pad(buckets, (0, 1), constant_values=-1)[None]
    backward_offsets = jnp.pad(buckets[::-1], (0, 1), constant_values=-1)[None]
    gain_one = attn_gain[None]
    gain_two = moe_gain[None]
    router_rows = router_weight.T
    wout_low, shards = barrier((out_weight.astype(BF16), shards))
    wouts = [wout_low, shift(wout_low, 1), shift(wout_low, -1), shift(wout_low, 2)]
    normed, qkv, attended, proj = attend_forward(
        order, bias, shards, gain_one, qkv_weight, offsets
    )
    attended, cot_arrived, wouts = barrier((attended, cot_arrived, wouts))
    wouts = wouts + [swap(w) for w in wouts]
    heads = lax.all_to_all(attended.reshape(8, TOK, 128), "narrow", 0, 0, tiled=True)
    cot_arrived, expert_in, expert_out = barrier((cot_arrived, expert_in, expert_out))

    pair, down, pair_other, down_other = call(
        halves_kernel,
        "halves",
        [shape((FULL, WIDTH), BF16), shape((PADDED, WIDTH), BF16)] * 2,
        [
            jnp.stack([core, 1 - core]).astype(jnp.int32),
            jnp.swapaxes(expert_in, 2, 3),
            expert_out,
        ],
        smem=1,
    )
    cot_arrived, pair = barrier((cot_arrived, pair))
    cot_own = unpack(cot_arrived, False)
    heads, pair, down, pair_other, down_other, cot_own = barrier(
        (heads, pair, down, pair_other, down_other, cot_own)
    )
    cot_parts = [cot_own, shift(cot_own, 1), shift(cot_own, -1), shift(cot_own, 2)]
    weights = [pair, swap(pair_other), down, swap(down_other)]
    middle, gates, send_rows, wout = call(
        dispatch_kernel,
        "dispatch",
        [
            shape((TOK, WIDTH), F32),
            shape((TOK, TOP), F32),
            shape((EXPERTS * SLOTS, WIDTH), BF16),
            shape((WIDTH, WIDTH), BF16),
        ],
        [order, heads, *wouts, tokens, gain_two, router_rows, routes, place, picks],
        smem=1,
    )

    arrived = blocks(send_rows)
    place, cot_parts = barrier((place, cot_parts))
    token_picks = call(
        slots_kernel,
        "slots",
        [shape((TOP, TOK, EXPERTS * SLOTS), BF16)],
        [routes, place],
    )[0]
    arrived, token_picks = barrier((arrived, token_picks))

    row_own = unpack(arrived, True)
    row_left, row_right = shift(row_own, 1), shift(row_own, -1)
    results = run_expert([([row_own], cot_parts[0])], weights)
    row_left, row_right, results = barrier((row_left, row_right, results))
    over = [shift(row_left[:HALF], 1), shift(row_right[HALF:], -1)]
    row_parts = [row_own, row_left, row_right]
    results += run_expert([([row_left], cot_parts[1]), ([row_right], cot_parts[2])], weights)
    over, results = barrier((over, results))
    row_parts = row_parts + over
    results += run_expert([(over, cot_parts[3])], weights, [results[1][3], results[2][2]])
    mids, inners = ([r[i] for r in results] for i in range(2))
    outs, backs = [r[2:4] for r in results], [r[4:6] for r in results]

    def leave_far(over):
        return [shift(over[0], -1), shift(over[1], 1)]

    def leave_near(left, right):
        return [shift(right[0], 1), shift(left[1], -1)]

    def land(own, left, right, near, far):
        left_top, right_end, part_top, part_end = join(*own, *near, left[0], far[0], right[1], far[1])
        return [part_top, part_end, left_top, right_end]

    def arrive(parts):
        return [parts[0], parts[1], shift(parts[2], -1), shift(parts[3], 1)]

    far, near = leave_far(backs[3]), leave_near(*backs[1:3])
    near, inners = barrier((near, inners))
    pair_part, pair_low, gate_columns = call(
        pair_grad_kernel,
        "pair_grad",
        [
            shape((2, HIDDEN, WIDTH), F32),
            shape((2, HIDDEN, WIDTH), BF16),
            shape((4 * ROWS, 128), F32),
        ],
        [*row_parts, *inners],
        [pltpu.VMEM((4 * ROWS, WIDTH), BF16)],
    )
    far, near, pair_part, pair_low = barrier((far, near, pair_part, pair_low))
    landed = land(*backs[:3], near, far)
    pair_part, landed = barrier((pair_part, landed))
    pair_grads = call(
        assemble_kernel,
        "assemble_pair",
        [shape((2, 2, HIDDEN, WIDTH), F32)],
        [core.astype(jnp.int32).reshape(1), pair_part, swap(pair_low)],
        smem=1,
    )[0]
    pieces, outs, mids, pair_grads = barrier((arrive(landed), outs, mids, pair_grads))
    from_right, from_left = leave_far(outs[3])
    back = call(collect_kernel, "collect", [shape((EXPERTS * SLOTS, WIDTH), BF16)], pieces)[0]
    row_grads = blocks(back)
    mids, _ = barrier((mids, back))
    down_part, down_low = call(
        down_grad_kernel,
        "down_grad",
        [shape((1, HIDDEN, WIDTH), F32), shape((1, HIDDEN, WIDTH), BF16)],
        [*cot_parts, *mids, gate_columns],
        [pltpu.VMEM((4 * ROWS, WIDTH), BF16)],
    )
    from_right, from_left, down_part = barrier((from_right, from_left, down_part))
    out_near, out_far = [from_left[:HALF], from_right[HALF:]], [from_right[:HALF], from_left[HALF:]]
    out_landed = land(*outs[:3], out_near, out_far)
    row_grads, down_part, out_landed = barrier((row_grads, down_part, out_landed))
    out_parts = arrive(out_landed)
    middle_grad, middle_low, send_heads, moe_gain_grad, logit_grads = call(
        middle_grad_kernel,
        "middle_grad",
        [
            shape((TOK, WIDTH), F32),
            shape((TOK, WIDTH), BF16),
            shape((8, TOK, 128), BF16),
            shape((1, WIDTH), F32),
            shape((TOK, EXPERTS), F32),
        ],
        [
            row_grads, gates, middle, layer_cotangent, routes, place, token_picks, gain_two,
            router_rows, wout,
        ],
    )
    head_grads = lax.all_to_all(send_heads, "narrow", 0, 0, tiled=True).reshape(LEN, 128)
    outer_sent = call(
        outer_sent_kernel,
        "outer_sent",
        [shape((4, 128, WIDTH), BF16)],
        [order, heads, middle_low],
        smem=1,
    )[0]
    back_out = call(collect_out_kernel, "collect_out", [shape((EXPERTS * SLOTS, WIDTH), BF16)], out_parts)[0]
    outer_got = swap(outer_sent)
    router_terms, *outer_parts = call(
        outer_kept_kernel,
        "outer_kept",
        [shape((EXPERTS, WIDTH), F32)] + [shape((128, WIDTH), BF16)] * 4,
        [order, heads, middle_low, outer_got, logit_grads, middle, gain_two],
        smem=1,
    )
    head_grads, back_out, outer_parts = barrier((head_grads, back_out, outer_parts))
    returned = blocks(back_out)

    def to_chips(parts):
        return [parts[0]] + [shift(p, step) for p, step in zip(parts[1:], (-1, 1, 2))]

    outer_parts = to_chips(outer_parts)
    bias_grad, weight_grads, gain_grad, sent, kept = attend_backward(
        order, bias, normed, qkv, attended, head_grads, backward_offsets, proj, gain_one
    )
    bias_grad, weight_grads, returned, outer_parts = barrier(
        (bias_grad, weight_grads, returned, outer_parts)
    )

    weight_grads = fill(weight_grads, outer_parts)
    arrived_grads = lax.all_to_all(weight_grads.reshape(16, 32, WIDTH), "wide", 0, 0, tiled=True)
    gain_grad, sent, _ = barrier((gain_grad, sent, weight_grads))

    low = barrier(jnp.concatenate([router_terms, gain_grad, moe_gain_grad]).astype(BF16))
    parts = [low] + [flip(low, "narrow", 2 * mask) for mask in (1, 2, 3)]
    kept = call(
        kept_kernel,
        "kept",
        [shape((TOK, WIDTH), BF16)] * 4,
        [kept, swap(sent)],
    )
    parts, kept = barrier((parts, kept))
    small = sum_pairs(parts)
    low = barrier(small.astype(BF16))
    small = low.astype(F32) + flip(low, "narrow", 1).astype(F32)
    small = jnp.concatenate(
        [small, jnp.pad(bias_grad.reshape(1, 64), ((0, 0), (0, WIDTH - 64)))]
    )
    arrived_grads, kept = barrier((arrived_grads, kept))
    copies = call(
        share_kernel, "share", [shape((16, 32, WIDTH), BF16)], [arrived_grads]
    )[0]
    returned, _ = barrier((returned, copies))
    layer_out = call(
        combine_kernel,
        "combine",
        [shape((TOK, WIDTH), BF16)],
        [returned, middle, gates, token_picks],
    )[0]
    gathered = lax.all_to_all(copies, "wide", 0, 0, tiled=True).reshape(512, WIDTH)
    small = sum_four(small, "wide", 1)
    chip_parts = to_chips(kept)
    down_part, small, chip_parts, _ = barrier((down_part, small, chip_parts, copies))
    down_grads = call(
        assemble_kernel,
        "assemble_down",
        [shape((2, 1, HIDDEN, WIDTH), F32)],
        [core.astype(jnp.int32).reshape(1), down_part, swap(down_low)],
        smem=1,
    )[0].reshape(2, HIDDEN, WIDTH)
    small = sum_four(small, "wide", 4)
    rel_bias_grad = small[EXPERTS + 2, : 2 * BUCKETS].reshape(2, BUCKETS)
    input_grad = call(
        input_grad_kernel,
        "input_grad",
        [shape((TOK, WIDTH), F32)],
        [*chip_parts, tokens, gain_one, middle_grad],
    )[0]
    qkv_weight_grad, out_weight_grad = call(
        finish_kernel,
        "finish",
        [shape((3, WIDTH, 128), F32), shape((128, WIDTH), F32)],
        [gathered],
    )
    return (
        layer_out,
        input_grad,
        small[EXPERTS],
        qkv_weight_grad,
        out_weight_grad,
        rel_bias_grad,
        small[EXPERTS + 1],
        small[:EXPERTS].T,
        jnp.swapaxes(pair_grads, 2, 3),
        down_grads,
    )


def solution(mesh):
    placed = (
        P(("wide", "narrow"), None),
        P(("wide", "narrow"), None),
        P(),
        P(None, None, "narrow"),
        P("narrow", None),
        P("narrow", None),
        P(),
        P(),
        P("wide", None, None, "narrow"),
        P("wide", "narrow", None),
        P(("wide", "narrow"), None),
        P(),
    )
    return jax.shard_map(
        on_device,
        mesh=mesh,
        in_specs=placed,
        out_specs=(
            P(("wide", "narrow"), None),
            P(("wide", "narrow"), None),
            P(),
            P(None, None, "narrow"),
            P("narrow", None),
            P("narrow", None),
            P(),
            P(),
            P("wide", None, None, "narrow"),
            P("wide", "narrow", None),
        ),
        check_vma=False,
    )
```
